128 devices in a mesh: group: 4 (over z_hi, core), dp: 2 (over z_lo), expert: 16 (over x, y).
Axes of the slice: x: 4, y: 4, z: 4 (z_hi: 2, z_lo: 2; z = z_hi * 2 + z_lo), core: 2. Of those that a mesh axis runs over, the one named last changes fastest.
Arguments:
- tokens: bfloat16 [2, 16384, 768], P(None, ('group', 'dp', 'expert')), may hold values from -24 to 24
- out_grad: bfloat16 [2, 16384, 768], P(None, ('group', 'dp', 'expert')), may hold values from -6 to 6
- expert_ids: int32 [2, 16384, 2], P(None, ('group', 'dp', 'expert')), may hold values from 0 to 16, all different within a row; in each aligned block of 128 rows (0 to 127, 128 to 255, ..., all dimensions but the last counted through in order) at most 22 rows name the same one
- replay: int32 [2, 16384], P(None, ('group', 'dp', 'expert')), may hold values 0 or 1
- frozen_in: bfloat16 [1, 768, 3072], replicated, may hold values from -0.21875 to 0.21875
- frozen_out: bfloat16 [1, 3072, 768], replicated, may hold values from -0.109375 to 0.109375
- gains: float32 [2, 768], P(None, ('dp', 'expert')), may hold values from 0.5 to 1.5
- w_qkv: float32 [768, 2304], P(('dp', 'expert')), may hold values from -0.21875 to 0.21875
- w_proj: float32 [768, 768], P(('dp', 'expert')), may hold values from -1.75 to 1.75
- router: float32 [768, 17], P(('dp', 'expert')), may hold values from -0.15625 to 0.15625
- exp_in: float32 [16, 768, 3072], P('expert', 'group', 'dp'), may hold values from -0.21875 to 0.21875
- exp_out: float32 [16, 3072, 768], P('expert', 'dp', 'group'), may hold values from -0.109375 to 0.109375
- mom_gains: float32 [2, 768], P(None, ('dp', 'expert')), may hold values from -1.5 to 1.5
- mom_qkv: float32 [768, 2304], P(('dp', 'expert')), may hold values from -0.046875 to 0.046875
- mom_proj: float32 [768, 768], P(('dp', 'expert')), may hold values from -0.3125 to 0.3125
- mom_router: float32 [768, 17], P(('dp', 'expert')), may hold values from -0.03125 to 0.03125
- mom_in: float32 [16, 768, 3072], P('expert', 'group', 'dp'), may hold values from -0.046875 to 0.046875
- mom_out: float32 [16, 3072, 768], P('expert', 'dp', 'group'), may hold values from -0.0234375 to 0.0234375
- state_gains: float32 [4, 2, 2, 768], P('group', None, None, ('dp', 'expert'))
- state_qkv: float32 [4, 2, 768, 2304], P('group', None, ('dp', 'expert'))
- state_proj: float32 [4, 2, 768, 768], P('group', None, ('dp', 'expert'))
- state_router: float32 [4, 2, 768, 17], P('group', None, ('dp', 'expert'))
- state_in: float32 [4, 2, 16, 768, 3072], P('group', None, 'expert', None, 'dp')
- state_out: float32 [4, 2, 16, 3072, 768], P('group', None, 'expert', 'dp')
Outputs:
- block_out: bfloat16 [2, 16384, 768], P(None, ('group', 'dp', 'expert'))
- input_grad: float32 [2, 16384, 768], P(None, ('group', 'dp', 'expert'))
- new_gains: float32 [2, 768], P(None, ('dp', 'expert'))
- new_qkv: float32 [768, 2304], P(('dp', 'expert'))
- new_proj: float32 [768, 768], P(('dp', 'expert'))
- new_router: float32 [768, 17], P(('dp', 'expert'))
- new_in: float32 [16, 768, 3072], P('expert', 'group', 'dp')
- new_out: float32 [16, 3072, 768], P('expert', 'dp', 'group')
- new_mom_gains: float32 [2, 768], P(None, ('dp', 'expert'))
- new_mom_qkv: float32 [768, 2304], P(('dp', 'expert'))
- new_mom_proj: float32 [768, 768], P(('dp', 'expert'))
- new_mom_router: float32 [768, 17], P(('dp', 'expert'))
- new_mom_in: float32 [16, 768, 3072], P('expert', 'group', 'dp')
- new_mom_out: float32 [16, 3072, 768], P('expert', 'dp', 'group')
The draws below stay inside these ranges and needn't reach their ends.
Inputs may be any that keep to these rules, and one draw needn't show every extreme that they name: `expert_ids`: A token's two experts differ. In every inner step the 128 consecutive rows of one device name each expert at most 22 times. Experts 0 to 0 are the frozen ones.
All inputs are finite; a program needn't handle non-finite values. No bound on the sum of `replay` on one device may be relied on, other than what follows from the above.
Results may differ from the reference program's by a relative error of at most 0.034.
Values may be sent and summed in bfloat16 or wider, within the bound.
A program may use at most 256 MiB of HBM per device.

```python
import math
import jax
import jax.numpy as jnp
import numpy as np
from jax import lax

D = 768
HEADS = 12
FF = 3072
FROZEN = 1
LEN = 128
STEPS = 2
STEP = 10
TOK_DEV = 128
GROUPS = 4
GROUP_TOK = 4096
TOKENS = 16384
NEW = 16
NEXP = 17
CAP = 22
N_DP = 2
N_EXPERT = 16


def moment_pair(key, shape, size):
    first_key, second_key = jax.random.split(key)
    first = 0.11 * size * jax.random.normal(first_key, shape, jnp.float32)
    spread = jax.random.uniform(second_key, shape, jnp.float32, -0.69, 0.69)
    second = 0.105 * size * size * jnp.exp(spread)
    return jnp.stack([first, second], axis=1)


def draw_state_gains(key, part):
    key = jax.random.fold_in(key, 11)
    return moment_pair(key, (GROUPS, 2, D), GROUP_TOK ** 0.5)


def draw_state_qkv(key, part):
    key = jax.random.fold_in(key, 12)
    return moment_pair(key, (GROUPS, D, 3 * D), GROUP_TOK ** 0.5)


def draw_state_proj(key, part):
    key = jax.random.fold_in(key, 13)
    return moment_pair(key, (GROUPS, D, D), 0.2 * GROUP_TOK ** 0.5)


def draw_state_router(key, part):
    key = jax.random.fold_in(key, 14)
    return moment_pair(key, (GROUPS, D, NEXP), 6.0 * (2.0 * GROUP_TOK / NEXP) ** 0.5)


def draw_state_in(key, part):
    key = jax.random.fold_in(key, 15)
    return moment_pair(key, (GROUPS, NEW, D, FF), 0.15 * (2.0 * GROUP_TOK / NEXP) ** 0.5)


def draw_state_out(key, part):
    key = jax.random.fold_in(key, 16)
    return moment_pair(key, (GROUPS, NEW, FF, D), 0.3 * (2.0 * GROUP_TOK / NEXP) ** 0.5)


def set_ends(array, own_key, smallest, high):
    dims = array.shape
    spot = [jax.random.randint(jax.random.fold_in(own_key, axis), (), 0, dims[axis]) for axis in range(len(dims))]
    array = array.at[tuple(spot)].set(smallest)
    longest = dims.index(max(dims))
    spot[longest] = (spot[longest] + 1) % dims[longest]
    return array.at[tuple(spot)].set(high)


def with_spikes(result, stream_key, source, target, blocks, factor):
    owner, partner = [(jnp.arange(result.shape[dim]) // (result.shape[dim] // blocks)).reshape([-1 if axis == dim else 1 for axis in range(result.ndim)]) for dim in (source, target)]
    chosen = jax.random.permutation(stream_key, blocks)[partner]
    strong = (owner == chosen) | (owner == (partner + blocks // 2) % blocks)
    return jnp.where(strong, factor * result, result)


def block_levels(key, dims, pieces, low, high):
    factor_of = 1.0
    for position, blocks in pieces:
        heights = jax.random.uniform(jax.random.fold_in(jax.random.fold_in(key, 6), position), (blocks,), jnp.float32, low / len(pieces), high / len(pieces))
        factor_of = factor_of * jnp.repeat(jnp.exp(heights), dims[position] // blocks).reshape((-1,) + (1,) * (len(dims) - 1 - position))
    return factor_of


def assign_block(key, own, number, rows, amount, top, reach, slope):
    ranking = jax.random.permutation(key, amount)
    crowded, usual = load_shares(amount, rows * top, reach, slope, True), load_shares(amount, rows * top, reach, slope, False)
    places = jnp.arange(amount)

    def named(lengths, turn):
        used = int((lengths > 0).sum())
        fixed = max(1, used // 4)
        passed = fixed + (places - fixed + turn * (used - fixed)) % max(1, amount - fixed)
        return jnp.zeros((amount,), jnp.int32).at[ranking[jnp.where(places < fixed, places, passed)]].set(jnp.asarray(lengths, jnp.int32))

    lengths = jnp.where(number % 4 == 0, named(crowded, number // 4), named(usual, number - number // 4 - 1))
    mixed = jax.random.permutation(jax.random.fold_in(own, 3), amount)
    donor, receiver = mixed[0:amount // 2 * 2:2], mixed[1:amount // 2 * 2:2]
    room = jnp.minimum(lengths[donor] - 1, reach - lengths[receiver]) // 2
    room = jnp.where((donor == ranking[0]) | (receiver == ranking[0]) | (lengths[receiver] == 0), 0, jnp.maximum(room, 0))
    passed = jax.random.randint(jax.random.fold_in(own, 4), (amount // 2,), 0, 1 << 20) % (room + 1)
    lengths = lengths.at[donor].add(-passed).at[receiver].add(passed)
    items = jnp.searchsorted(jnp.cumsum(lengths), jnp.arange(rows * top), side="right").astype(jnp.int32)
    table = items.reshape(top, rows).T
    table = table[jax.random.permutation(jax.random.fold_in(own, 1), rows)]
    turn = jax.random.randint(jax.random.fold_in(own, 2), (rows, 1), 0, top)
    return jnp.take_along_axis(table, (jnp.arange(top)[None, :] + turn) % top, axis=1)


def load_shares(amount, total, bound, skew, full):
    portions = [(1 << 20) // math.isqrt(rank ** skew) + 1 for rank in range(1, amount + 1)]
    largest = bound if full else min(bound, max(-(-total // amount), total * portions[0] // sum(portions)))
    least = 1 if total - largest >= amount - 1 else 0
    holding, spare = [largest] + [least] * (amount - 1), total - largest - least * (amount - 1)
    while spare > 0:
        movable = [i for i in range(1, amount) if holding[i] < largest] or [i for i in range(1, amount) if holding[i] < bound]
        pool, remaining = sum([portions[i] for i in movable]), spare
        for i in movable:
            more = min(bound - holding[i], max(1, remaining * portions[i] // pool), spare)
            holding[i] = holding[i] + more
            spare = spare - more
    return np.array(holding)


def normal_values(own_key, shape, scale, most, pieces=(), kind=jnp.bfloat16):
    entries = jax.random.normal(own_key, shape, jnp.float32) * scale
    if len(pieces) > 0:
        entries = block_levels(own_key, shape, pieces, -0.22, 0.18) * entries
    return jnp.clip(entries, min=-most, max=most).astype(kind)


def gaussian_with(key, extent, deviation, reach, cuts, heavy, kind=jnp.bfloat16):
    entries = deviation * jax.random.normal(key, extent, jnp.float32)
    if cuts:
        entries = entries * block_levels(key, extent, cuts, -0.22, 0.18)
    return jnp.clip(with_spikes(entries, jax.random.fold_in(key, 3), *heavy), -reach, reach).astype(kind)


def setup_inputs(seed: int = 0) -> dict:
    streams_of = jax.random.split(jax.random.key(seed), 25)
    tokens = gaussian_with(streams_of[0], (STEPS, TOKENS, D), 1.0, 24.0, ((1, 128),), (1, 2, 128, 5.5))
    out_grad = normal_values(streams_of[1], (STEPS, TOKENS, D), 1.0, 6.0, ((1, 128),))
    expert_ids_keys = jax.random.split(jax.random.fold_in(streams_of[2], 1), STEPS * TOKENS // TOK_DEV)
    expert_ids_turns = jax.random.permutation(jax.random.fold_in(streams_of[2], 3), STEPS * TOKENS // TOK_DEV)
    expert_ids = jax.vmap(lambda own, number: assign_block(jax.random.fold_in(streams_of[2], 2), own, number, TOK_DEV, NEXP, 2, CAP, 2))(expert_ids_keys, expert_ids_turns).reshape((STEPS, TOKENS, 2))
    replay = set_ends((jax.random.randint(streams_of[3], (STEPS, TOKENS), 0, 4) < 1).astype(jnp.int32), jax.random.fold_in(streams_of[3], 1), 0, 1)
    frozen_in = normal_values(streams_of[4], (FROZEN, D, FF), D ** -0.5, 0.21875)
    frozen_out = normal_values(streams_of[5], (FROZEN, FF, D), FF ** -0.5, 0.109375)
    gains = jnp.clip(1.0 + 0.1 * jax.random.normal(streams_of[6], (2, D), jnp.float32), 0.5, 1.5)
    w_qkv = normal_values(streams_of[7], (D, 3 * D), D ** -0.5, 0.21875, ((0, 32),), jnp.float32)
    w_proj = normal_values(streams_of[8], (D, D), (2 * D // LEN) ** -0.5, 1.75, ((0, 32),), jnp.float32)
    router = normal_values(streams_of[9], (D, NEXP), (2 * D) ** -0.5, 0.15625, ((0, 32),), jnp.float32)
    exp_in = normal_values(streams_of[10], (NEW, D, FF), D ** -0.5, 0.21875, ((0, 16), (1, 4), (2, 2)), jnp.float32)
    exp_out = normal_values(streams_of[11], (NEW, FF, D), FF ** -0.5, 0.109375, ((0, 16), (1, 2), (2, 4)), jnp.float32)
    mom_gains = normal_values(streams_of[12], (2, D), 0.1, 1.5, ((1, 32),), jnp.float32)
    mom_qkv = normal_values(streams_of[13], (D, 3 * D), 0.003, 0.046875, ((0, 32),), jnp.float32)
    mom_proj = normal_values(streams_of[14], (D, D), 0.02, 0.3125, ((0, 32),), jnp.float32)
    mom_router = normal_values(streams_of[15], (D, NEXP), 0.002, 0.03125, ((0, 32),), jnp.float32)
    mom_in = normal_values(streams_of[16], (NEW, D, FF), 0.003, 0.046875, ((0, 16), (1, 4), (2, 2)), jnp.float32)
    mom_out = normal_values(streams_of[17], (NEW, FF, D), 0.0015, 0.0234375, ((0, 16), (1, 2), (2, 4)), jnp.float32)
    state_gains = draw_state_gains(jax.random.fold_in(streams_of[24], 71), 0)
    state_qkv = draw_state_qkv(jax.random.fold_in(streams_of[24], 71), 0)
    state_proj = draw_state_proj(jax.random.fold_in(streams_of[24], 71), 0)
    state_router = draw_state_router(jax.random.fold_in(streams_of[24], 71), 0)
    state_in = draw_state_in(jax.random.fold_in(streams_of[24], 71), 0)
    state_out = draw_state_out(jax.random.fold_in(streams_of[24], 71), 0)
    return {"tokens": tokens, "out_grad": out_grad, "expert_ids": expert_ids, "replay": replay, "frozen_in": frozen_in, "frozen_out": frozen_out, "gains": gains, "w_qkv": w_qkv, "w_proj": w_proj, "router": router, "exp_in": exp_in, "exp_out": exp_out, "mom_gains": mom_gains, "mom_qkv": mom_qkv, "mom_proj": mom_proj, "mom_router": mom_router, "mom_in": mom_in, "mom_out": mom_out, "state_gains": state_gains, "state_qkv": state_qkv, "state_proj": state_proj, "state_router": state_router, "state_in": state_in, "state_out": state_out}


EPS_NORM = 1e-06
BETA_ONE = 0.9
BETA_TWO = 0.95
ADAM_EPS = 1e-08
DECAY = 0.1
OUTER_RATE = 0.7
OUTER_MOMENTUM = 0.9
REPLAY_WEIGHT = 0.25
RATES = (0.6, 0.04, 0.3, 0.03, 0.04, 0.02)
PRECISE = lax.Precision.HIGHEST

@jax.custom_vjp
def low(v):
    return lax.optimization_barrier(v.astype(jnp.bfloat16)).astype(jnp.float32)

@jax.custom_vjp
def low_back(v):
    return v

def low_keep(v):
    return (low(v), None)

def low_pass(kept, grad):
    return (grad,)

def back_keep(v):
    return (v, None)

def back_low(kept, grad):
    return (low(grad),)
low.defvjp(low_keep, low_pass)
low_back.defvjp(back_keep, back_low)

def normalize(values):
    return values * lax.rsqrt(lax.optimization_barrier(jnp.mean(values * values, axis=-1, keepdims=True)) + EPS_NORM)

def softmax_last(scores):
    top = lax.optimization_barrier(jnp.max(scores, axis=-1, keepdims=True))
    expo = jnp.exp(scores - top)
    return expo / lax.optimization_barrier(jnp.sum(expo, axis=-1, keepdims=True))

def gelu_exact(values):
    return jax.nn.gelu(values, approximate=False)

def route_table(choices, count, capacity):
    flat = choices.reshape(-1)
    onehot = (flat[:, None] == jnp.arange(count, dtype=jnp.int32)[None, :]).astype(jnp.int32)
    before = jnp.cumsum(onehot, axis=0) - onehot
    slot = lax.optimization_barrier(jnp.sum(before * onehot, axis=1))
    place = flat * capacity + slot
    marks = jnp.arange(flat.shape[0], dtype=jnp.int32) + 1
    table = jnp.zeros((count * capacity,), jnp.int32).at[place].set(marks)
    return (place, table)

def group_tables(choices):
    devices_group = N_DP * N_EXPERT
    blocks = choices.reshape(devices_group, TOK_DEV, 2)
    place, table = jax.vmap(lambda block: route_table(block, NEXP, CAP))(blocks)
    device = jnp.arange(devices_group, dtype=jnp.int32)
    expert = place // CAP
    slot = place % CAP
    global_place = expert * (devices_group * CAP) + device[:, None] * CAP + slot
    shifted = jnp.where(table > 0, table + device[:, None] * (2 * TOK_DEV), 0)
    shifted = shifted.reshape(devices_group, NEXP, CAP).transpose(1, 0, 2).reshape(-1)
    return (global_place.reshape(-1), shifted)

def expert_block(rows, first, second):
    pre = low_back(jnp.einsum('ecd,edf->ecf', rows, first, precision=PRECISE))
    act = low(gelu_exact(pre))
    return jnp.einsum('ecf,efd->ecd', act, second, precision=PRECISE)

def forward(params, inputs, choices, frozen_first, frozen_second, place, table):
    gains, w_qkv, w_proj, router, exp_in, exp_out = params
    gain_low = low(gains)
    acts = low(normalize(inputs) * gain_low[0])
    qkv = low(low_back(jnp.dot(acts, low(w_qkv), precision=PRECISE)))
    width = D // HEADS
    seqs = inputs.shape[0] // LEN
    parts = qkv.reshape(seqs, LEN, 3, HEADS, width)
    query, key, value = (parts[:, :, 0], parts[:, :, 1], parts[:, :, 2])
    scale = width ** (-0.5)
    scores = low_back(jnp.einsum('sqhd,skhd->shqk', query, key, precision=PRECISE) * scale)
    causal = jnp.arange(LEN)[:, None] >= jnp.arange(LEN)[None, :]
    scores = jnp.where(causal, scores, -1e+30)
    probs = low(softmax_last(scores))
    mixed = jnp.einsum('shqk,skhd->sqhd', probs, value, precision=PRECISE).reshape(-1, D)
    mixed = low(low_back(mixed))
    branch = low_back(jnp.dot(mixed, low(w_proj), precision=PRECISE))
    middle = inputs + branch
    routed = low(normalize(middle) * gain_low[1])
    logits = jnp.dot(routed, low(router), precision=PRECISE)
    select = (choices[:, :, None] == jnp.arange(NEXP, dtype=jnp.int32)[None, None, :]).astype(jnp.float32)
    picked = lax.optimization_barrier(jnp.sum(select * logits[:, None, :], axis=-1))
    weights = softmax_last(picked)
    doubled = jnp.repeat(routed, 2, axis=0)
    padded = jnp.concatenate([jnp.zeros((1, D), jnp.float32), doubled])
    rows = padded[table].reshape(NEXP, -1, D)
    frozen_res = low_back(expert_block(rows[:FROZEN], frozen_first, frozen_second))
    new_res = low(low_back(expert_block(low_back(rows[FROZEN:]), low(exp_in), low(exp_out))))
    results = jnp.concatenate([frozen_res, new_res]).reshape(-1, D)
    gathered = results[place].reshape(-1, 2, D)
    return middle + lax.optimization_barrier(jnp.sum(weights[:, :, None] * gathered, axis=1))

def adam_step(master, state, grad, rate, number):
    first = BETA_ONE * state[0] + (1.0 - BETA_ONE) * grad
    second = BETA_TWO * state[1] + (1.0 - BETA_TWO) * grad * grad
    fix_one = 1.0 - BETA_ONE ** number
    fix_two = 1.0 - BETA_TWO ** number
    update = first / fix_one / (jnp.sqrt(second / fix_two) + ADAM_EPS) + DECAY * master
    return (master - rate * update, jnp.stack([first, second]))

def reference(tokens, out_grad, expert_ids, replay, frozen_in, frozen_out, gains, w_qkv, w_proj, router, exp_in, exp_out, mom_gains, mom_qkv, mom_proj, mom_router, mom_in, mom_out, state_gains, state_qkv, state_proj, state_router, state_in, state_out):
    frozen_first = frozen_in.astype(jnp.float32)
    frozen_second = frozen_out.astype(jnp.float32)
    start = (gains, w_qkv, w_proj, router, exp_in, exp_out)
    states = (state_gains, state_qkv, state_proj, state_router, state_in, state_out)
    moms = (mom_gains, mom_qkv, mom_proj, mom_router, mom_in, mom_out)
    block_rows = [[None] * GROUPS for index in range(STEPS)]
    grad_rows = [[None] * GROUPS for index in range(STEPS)]
    totals = tuple((jnp.zeros_like(value) for value in start))
    for group in range(GROUPS):
        params = start
        moments = tuple((state[group] for state in states))
        first_row = group * GROUP_TOK
        last_row = first_row + GROUP_TOK
        for step in range(STEPS):
            inputs = tokens[step, first_row:last_row].astype(jnp.float32)
            choices = expert_ids[step, first_row:last_row]
            factor = jnp.where(replay[step, first_row:last_row] > 0, REPLAY_WEIGHT, 1.0).astype(jnp.float32)
            cotangent = out_grad[step, first_row:last_row].astype(jnp.float32) * factor[:, None]
            place, table = group_tables(choices)

            def run(values, inputs_now):
                return forward(values, inputs_now, choices, frozen_first, frozen_second, place, table)
            block, pullback = jax.vjp(run, params, inputs)
            grads, grad_inputs = pullback(cotangent)
            block_rows[step][group] = block.astype(jnp.bfloat16)
            grad_rows[step][group] = grad_inputs
            pairs = [adam_step(p, m, g, r, STEP + step) for p, m, g, r in zip(params, moments, grads, RATES)]
            params = tuple((pair[0] for pair in pairs))
            moments = tuple((pair[1] for pair in pairs))
        totals = tuple((total + (begin - final) for total, begin, final in zip(totals, start, params)))
    new_moms = []
    new_params = []
    for total, begin, moment in zip(totals, start, moms):
        delta = total / GROUPS
        renewed = OUTER_MOMENTUM * moment + delta
        new_moms.append(renewed)
        new_params.append(begin - OUTER_RATE * (delta + OUTER_MOMENTUM * renewed))
    block_out = jnp.stack([jnp.concatenate(row, axis=0) for row in block_rows])
    input_grad = jnp.stack([jnp.concatenate(row, axis=0) for row in grad_rows])
    return (block_out, input_grad, new_params[0], new_params[1], new_params[2], new_params[3], new_params[4], new_params[5], new_moms[0], new_moms[1], new_moms[2], new_moms[3], new_moms[4], new_moms[5])
```

```python
import functools

import jax
import jax.numpy as jnp
from jax import lax
from jax.experimental import pallas as pl
from jax.experimental.pallas import tpu as pltpu
from jax.sharding import PartitionSpec as P

MESH = pl.DeviceIdType.MESH
VMEM = pltpu.VMEM
F32 = jnp.float32
BF16 = jnp.bfloat16


class Links:
    def __init__(self, sends, recvs):
        self.sends, self.recvs, self.used, self.begun = sends, recvs, 0, []

    def make(self, src, dst, to):
        at = self.used
        self.used += 1
        copy = pltpu.make_async_remote_copy(
            src_ref=src, dst_ref=dst, send_sem=self.sends.at[at], recv_sem=self.recvs.at[at],
            device_id=to, device_id_type=MESH,
        )
        self.begun.append(copy)
        return copy

    def send(self, src, dst, to):
        copy = self.make(src, dst, to)
        copy.start()
        return copy

    def finish(self):
        for copy in self.begun:
            copy.wait_send()


class Place:
    def __init__(self):
        self.g, self.d = lax.axis_index("group"), lax.axis_index("dp")
        e = lax.axis_index("expert")
        self.x, self.y = lax.div(e, 4), lax.rem(e, 4)

    def along_x(self, step):
        return {"expert": lax.rem(self.x + step, 4) * 4 + self.y}

    def along_y(self, step):
        return {"expert": self.x * 4 + lax.rem(self.y + step, 4)}

    def other_dp(self):
        return {"dp": 1 - self.d}

    def in_group(self, step):
        return {"group": lax.rem(self.g + step, 4)}

    def other_core(self):
        return {"group": self.g + 1 - 2 * lax.rem(self.g, 2)}


def greet(partners):
    barrier = pltpu.get_barrier_semaphore()
    for partner in partners:
        pl.semaphore_signal(barrier, inc=1, device_id=partner, device_id_type=MESH)
    pl.semaphore_wait(barrier, len(partners))


class Gather:
    def __init__(self, links, place, whole, h, p1, p2, near1, near2, at):
        self.links, self.whole, self.h, self.at = links, whole, h, at
        self.d, self.place = place.d, place
        self.p1, self.p2, self.near1, self.near2 = p1, p2, near1, near2

    def slot(self, k1, k2, dp=None):
        c, x = self.at(lax.rem(k1, 4), lax.rem(k2, 4))
        return self.whole.at[c, slice(None) if dp is None else dp, x, self.h]

    def push(self, k1, k2, dp, to):
        ref = self.slot(k1, k2, dp)
        return self.links.send(ref, ref, to)

    def start(self):
        p1, p2, d = self.p1, self.p2, self.d
        self.over_dp = self.push(p1, p2, d, self.place.other_dp())
        self.own = [self.push(p1, p2, d, self.near1(1)), self.push(p1, p2, d, self.near1(3))]

    def ring_one(self):
        p1, p2, d = self.p1, self.p2, self.d
        self.over_dp.wait_recv()
        self.own += [self.push(p1, p2, 1 - d, self.near1(1)), self.push(p1, p2, 1 - d, self.near1(3))]
        self.pushed = [(p1, self.push(p1, p2, None, self.near2(1)), self.push(p1, p2, None, self.near2(3)))]
        for copy in self.own:
            copy.wait_recv()
        self.passed = [self.push(p1 + 3, p2, 0, self.near1(1)), self.push(p1 + 1, p2, 1, self.near1(3))]
        for k1 in (p1 + 3, p1 + 1):
            self.pushed.append((k1, self.push(k1, p2, None, self.near2(1)), self.push(k1, p2, None, self.near2(3))))

    def ring_two(self):
        p1, p2 = self.p1, self.p2
        for copy in self.passed:
            copy.wait_recv()
        k1 = p1 + 2
        self.pushed.append((k1, self.push(k1, p2, None, self.near2(1)), self.push(k1, p2, None, self.near2(3))))
        self.last = []
        for k1, right, left in self.pushed:
            right.wait_recv()
            self.last.append(self.push(k1, p2 + 3, 0, self.near2(1)))
            left.wait_recv()
            self.last.append(self.push(k1, p2 + 1, 1, self.near2(3)))

    def end(self):
        for copy in self.last:
            copy.wait_recv()


def gather_parts(links, place, whole):
    by_x = lambda kx, ky: (ky, kx)
    by_y = lambda ky, kx: (ky, kx)
    first = Gather(links, place, whole, 0, place.x, place.y, place.along_x, place.along_y, by_x)
    second = Gather(links, place, whole, 1, place.y, place.x, place.along_y, place.along_x, by_y)
    return first, second


def gather_all(links, place, whole):
    parts = gather_parts(links, place, whole)
    for stage in ("start", "ring_one", "ring_two", "end"):
        for part in parts:
            getattr(part, stage)()


class RingSum:
    def __init__(self, links, near, p, term, far, near_buf, add):
        self.links, self.near, self.p, self.term = links, near, p, term
        self.far, self.near_buf, self.add = far, near_buf, add

    def start(self):
        p, links = self.p, self.links
        right, left = self.near(1), self.near(3)
        self.far_copies = [
            links.send(self.term(p + 2, 1), self.far.at[0], right),
            links.send(self.term(p + 2, 0), self.far.at[1], left),
        ]
        self.direct = [
            links.send(self.term(p + 1, 0), self.near_buf.at[0, 0], right),
            links.send(self.term(p + 3, 1), self.near_buf.at[1, 1], left),
        ]

    def middle(self):
        p, links = self.p, self.links
        for side, to, dp, k in ((0, self.near(1), 1, p + 1), (1, self.near(3), 0, p + 3)):
            self.far_copies[side].wait_recv()
            self.far[side] = (self.far[side].astype(F32) + self.term(k, dp)[...].astype(F32)).astype(BF16)
            self.direct.append(links.send(self.far.at[side], self.near_buf.at[side, dp], to))

    def finish(self):
        for copy in self.direct:
            copy.wait_recv()
        return [
            self.term(self.p, dp)[...].astype(F32)
            + self.near_buf[0, dp].astype(F32)
            + self.near_buf[1, dp].astype(F32)
            for dp in range(2)
        ]


def add_over(links, own, box, position, size, reach):
    box[position] = own
    copies = [links.send(box.at[position], box.at[position], reach(step)) for step in range(1, size)]

    def finish():
        for copy in copies:
            copy.wait_recv()
        total = box[0]
        for k in range(1, size):
            total = total + box[k]
        return total

    return finish


def ring_scratch(blocks):
    return [VMEM((2, *blocks, 48, 768), BF16), VMEM((2, 2, *blocks, 48, 768), BF16)]


def reduce_all(links, place, grads, extra, scratch, result):
    (far_a, near_a, far_b, near_b, mid_a, mid_b, far_c, near_c, far_d, near_d, last, zbox, box_x, box_y, box_z) = scratch
    r4 = lambda k: lax.rem(k, 4)
    first = RingSum(links, place.along_y, place.y, lambda k, dp: grads.at[r4(k), dp, :, 0], far_a, near_a, None)
    second = RingSum(links, place.along_x, place.x, lambda k, dp: grads.at[:, dp, r4(k), 1], far_b, near_b, None)
    first.start()
    second.start()
    extra_x = add_over(links, extra[...], box_x, place.x, 4, place.along_x)
    first.middle()
    second.middle()
    extra_y = add_over(links, extra_x(), box_y, place.y, 4, place.along_y)
    for part, mid in ((first, mid_a), (second, mid_b)):
        for dp, value in enumerate(part.finish()):
            mid[dp] = value.astype(BF16)
    third = RingSum(links, place.along_x, place.x, lambda k, dp: mid_a.at[dp, r4(k)], far_c, near_c, None)
    fourth = RingSum(links, place.along_y, place.y, lambda k, dp: mid_b.at[dp, r4(k)], far_d, near_d, None)
    third.start()
    fourth.start()
    total_xy = extra_y()
    extra_z = add_over(links, total_xy, box_z, place.d, 2, lambda step: place.other_dp())
    third.middle()
    fourth.middle()
    over = []
    for h, part in enumerate((third, fourth)):
        for dp, value in enumerate(part.finish()):
            last[dp, h] = value.astype(BF16)
        over.append(links.send(last.at[1 - place.d, h], zbox.at[h], place.other_dp()))
    for h in range(2):
        over[h].wait_recv()
        result[h] = last[place.d, h].astype(F32) + zbox[h].astype(F32)
    return extra_z()


REDUCE_SCRATCH = (
    ring_scratch((4,)) + ring_scratch((4,))
    + [VMEM((2, 4, 48, 768), BF16)] * 2
    + ring_scratch(()) + ring_scratch(())
    + [VMEM((2, 2, 48, 768), BF16), VMEM((2, 48, 768), BF16)]
    + [VMEM((4, 24, 768), F32), VMEM((4, 24, 768), F32), VMEM((2, 24, 768), F32)]
)
REDUCE_COPIES = 4 * 6 + 2 + 7
GATHER_COPIES = 2 * 23


def ring_partners(place):
    return (
        [place.along_x(k) for k in (1, 2, 3)]
        + [place.along_y(k) for k in (1, 2, 3)]
        + [place.other_dp()]
    )


EPS_NORM = 1e-06
BETA_ONE = 0.9
BETA_TWO = 0.95
ADAM_EPS = 1e-08
DECAY = 0.1
OUTER_RATE = 0.7
OUTER_MOMENTUM = 0.9
REPLAY_WEIGHT = 0.25
RATES = (0.6, 0.04, 0.3, 0.03, 0.04, 0.02)
HEADS = 12
LEN = 128
STEPS = 2
STEP = 10


def entry_kernel(p_in, mv_in, e_in, whole, p_out, mv_out, e_out, sends, recvs):
    place = Place()
    greet(ring_partners(place) + [place.other_core()])
    links = Links(sends, recvs)
    x, y, d = place.x, place.y, place.d
    h = lax.rem(place.g, 2)
    masters = [links.send(p_in.at[lax.rem(y + k, 4)], p_out.at[y], place.along_y(k)) for k in (1, 2, 3)]
    e_out[d, x, y] = e_in[...]
    mine = e_out.at[d, x, y]
    extra_z = links.send(mine, mine, place.other_dp())
    p_out[y] = p_in[y]
    mv_out[:, y] = mv_in[:, y]
    for copy in masters:
        copy.wait_recv()
    low = p_out[...].astype(BF16).reshape(2, 48, 768)

    @pl.when(h == 0)
    def _():
        whole[y, d, x, 0] = low[0]

    @pl.when(h == 1)
    def _():
        whole[y, d, x, 1] = low[1]

    def mix(a, b):
        return a * (1 - h) + b * h

    def near1(step):
        return {"expert": mix(place.along_x(step)["expert"], place.along_y(step)["expert"])}

    def near2(step):
        return {"expert": mix(place.along_y(step)["expert"], place.along_x(step)["expert"])}

    def at(k1, k2):
        return mix(k2, k1), mix(k1, k2)

    part = Gather(links, place, whole, h, mix(x, y), mix(y, x), near1, near2, at)
    p1, p2 = part.p1, part.p2
    part.start()
    extra_z.wait_recv()
    mine = e_out.at[:, x, y]
    extra_x = [links.send(mine, mine, place.along_x(k)) for k in (1, 2, 3)]
    part.ring_one()
    share = place.other_core()
    shared = [part.push(k1, p2, None, share) for k1 in (p1, p1 + 3, p1 + 1)]
    for copy in extra_x:
        copy.wait_recv()
    mine = e_out.at[:, :, y]
    extra_y = [links.send(mine, mine, place.along_y(k)) for k in (1, 2, 3)]
    part.ring_two()
    moments = [links.send(mv_in.at[:, lax.rem(y + k, 4)], mv_out.at[:, y], place.along_y(k)) for k in (1, 2, 3)]
    shared.append(part.push(p1 + 2, p2, None, share))
    for k1 in (p1, p1 + 3, p1 + 1, p1 + 2):
        shared += [part.push(k1, p2 + 3, None, share), part.push(k1, p2 + 1, None, share)]
    part.end()
    shared += [part.push(k1, p2 + 2, None, share) for k1 in (p1, p1 + 3, p1 + 1, p1 + 2)]
    for copy in shared:
        copy.wait_recv()
    for copy in extra_y + moments:
        copy.wait_recv()
    links.finish()


def adam_values(master, first, second, grad, rate, number):
    first = BETA_ONE * first + (1.0 - BETA_ONE) * grad
    second = BETA_TWO * second + (1.0 - BETA_TWO) * grad * grad
    fix_one = 1.0 - BETA_ONE**number
    fix_two = 1.0 - BETA_TWO**number
    update = first / fix_one / (jnp.sqrt(second / fix_two) + ADAM_EPS) + DECAY * master
    return master - rate * update, first, second


def block_rate(place):
    return jnp.where(place.y == 3, RATES[2], RATES[1]).astype(F32)


def extra_rates():
    row = lax.broadcasted_iota(jnp.int32, (24, 768), 0)
    return jnp.where(row < 17, RATES[3], RATES[0]).astype(F32)


def renew_kernel(number, grads, extra, p_in, mv_in, pe_in, mve_in,
                 whole, p_out, mv_out, pe_out, mve_out, result, *scratch):
    *scratch, sends, recvs = scratch
    place = Place()
    greet(ring_partners(place))
    links = Links(sends, recvs)
    total = reduce_all(links, place, grads, extra, scratch, result)
    fresh, first, second = adam_values(p_in[...], mv_in[0], mv_in[1], result[...], block_rate(place), number)
    whole[place.y, place.d, place.x] = fresh.astype(BF16)
    gather = gather_parts(links, place, whole)
    for part in gather:
        part.start()
    p_out[...] = fresh
    mv_out[0] = first
    mv_out[1] = second
    pe_out[...], mve_out[0], mve_out[1] = adam_values(pe_in[...], mve_in[0], mve_in[1], total, extra_rates(), number)
    for stage in ("ring_one", "ring_two", "end"):
        for part in gather:
            getattr(part, stage)()
    links.finish()


def final_kernel(number, grads, extra, p_in, mv_in, pe_in, mve_in, p_start, pe_start, w_old, mom_old,
                 w_new, mom_new, delta_e, result, delta, quarters, whole, turned, boxes, *scratch):
    *scratch, sends, recvs = scratch
    place = Place()
    greet(ring_partners(place) + [place.in_group(k) for k in (1, 2, 3)])
    links = Links(sends, recvs)
    g, y = place.g, place.y
    total = reduce_all(links, place, grads, extra, scratch, result)
    fresh, _, _ = adam_values(p_in[...], mv_in[0], mv_in[1], result[...], block_rate(place), number)
    delta[...] = (p_start[...] - fresh).reshape(4, 24, 768)
    summed = [
        links.send(delta.at[lax.rem(g + k, 4)], quarters.at[g], place.in_group(k)) for k in (1, 2, 3)
    ]
    fresh_e, _, _ = adam_values(pe_in[...], mve_in[0], mve_in[1], total, extra_rates(), number)
    sum_e = add_over(links, pe_start[...] - fresh_e, boxes, g, 4, place.in_group)
    quarters[g] = delta[g]
    for copy in summed:
        copy.wait_recv()
    whole[g] = (quarters[0] + quarters[1] + quarters[2] + quarters[3]) * 0.25
    spread = [links.send(whole.at[g], whole.at[g], place.in_group(k)) for k in (1, 2, 3)]
    delta_e[...] = sum_e() * 0.25
    for copy in spread:
        copy.wait_recv()
    turned[y] = whole[y]
    across = [links.send(whole.at[lax.rem(y + k, 4)], turned.at[y], place.along_y(k)) for k in (1, 2, 3)]
    for copy in across:
        copy.wait_recv()
    mean = turned[...]
    renewed = OUTER_MOMENTUM * mom_old[...] + mean
    mom_new[...] = renewed
    w_new[...] = w_old[...] - OUTER_RATE * (mean + OUTER_MOMENTUM * renewed)
    links.finish()


def semaphores(count):
    return [pltpu.SemaphoreType.DMA((count,)), pltpu.SemaphoreType.DMA((count,))]


def vmem_call(kernel, outs, scratch, collective_id, *args, limit=56 << 20):
    return pl.pallas_call(
        kernel,
        out_shape=tuple(jax.ShapeDtypeStruct(shape, kind) for shape, kind in outs),
        in_specs=[pl.BlockSpec(memory_space=VMEM)] * len(args),
        out_specs=tuple(pl.BlockSpec(memory_space=VMEM) for _ in outs),
        scratch_shapes=scratch,
        compiler_params=pltpu.CompilerParams(
            collective_id=collective_id, has_side_effects=True, vmem_limit_bytes=limit
        ),
    )(*args)


WHOLE = (4, 2, 4, 2, 48, 768)


def entry_call(p_in, mv_in, e_in):
    return vmem_call(
        entry_kernel,
        [(WHOLE, BF16), ((4, 24, 768), F32), ((2, 4, 24, 768), F32), ((2, 4, 4, 24, 128), F32)],
        semaphores(3 + 7 + 23 + 3 + 16), 1, p_in, mv_in, e_in,
    )


def renew_call(number, *args):
    return vmem_call(
        functools.partial(renew_kernel, number),
        [(WHOLE, BF16), ((2, 48, 768), F32), ((2, 2, 48, 768), F32), ((24, 768), F32), ((2, 24, 768), F32)],
        [VMEM((2, 48, 768), F32)] + REDUCE_SCRATCH + semaphores(REDUCE_COPIES + GATHER_COPIES), 2, *args,
    )


def final_call(number, *args):
    box = VMEM((4, 24, 768), F32)
    return vmem_call(
        functools.partial(final_kernel, number),
        [((4, 24, 768), F32), ((4, 24, 768), F32), ((24, 768), F32)],
        [VMEM((2, 48, 768), F32), box, box, box, box, box] + REDUCE_SCRATCH + semaphores(REDUCE_COPIES + 12),
        3, *args,
    )


def turned_gather(arrays, axis, dims):
    turned = [jnp.moveaxis(a, dim, 0) for a, dim in zip(arrays, dims)]
    widths = [t[0].size for t in turned]
    both = jnp.concatenate([t.reshape(-1, w) for t, w in zip(turned, widths)], axis=1)
    whole = lax.all_gather(both, axis, axis=0, tiled=True)
    blocks = jnp.split(whole, [sum(widths[:k]) for k in range(1, len(widths))], axis=1)
    return tuple(
        (
            jnp.moveaxis(b.reshape(-1, *t.shape[1:]), 0, dim)
            for b, t, dim in zip(blocks, turned, dims)
        )
    )


def normalize(values):
    return values * lax.rsqrt(jnp.mean(values * values, axis=-1, keepdims=True) + EPS_NORM)


def norm_back(values, grad_norm):
    scale = lax.rsqrt(jnp.mean(values * values, axis=-1, keepdims=True) + EPS_NORM)
    normed = values * scale
    return scale * (grad_norm - normed * jnp.mean(grad_norm * normed, axis=-1, keepdims=True))


def gelu_exact(values):
    return jax.nn.gelu(values, approximate=False)


def route_table(choices, count, capacity):
    flat = choices.reshape(-1)
    onehot = (flat[:, None] == jnp.arange(count, dtype=jnp.int32)[None, :]).astype(jnp.int32)
    before = jnp.cumsum(onehot, axis=0) - onehot
    slot = jnp.sum(before * onehot, axis=1)
    place = flat * capacity + slot
    marks = jnp.arange(flat.shape[0], dtype=jnp.int32) + 1
    table = jnp.zeros((count * capacity,), jnp.int32).at[place].set(marks)
    return (place, table)


def split_heads(qkv, heads):
    tokens_here, triple = qkv.shape
    size = triple // (3 * heads)
    parts = qkv.reshape(tokens_here // LEN, LEN, 3, heads, size)
    return (parts[:, :, 0], parts[:, :, 1], parts[:, :, 2], size ** (-0.5))


def attend(qkv, heads):
    query, key, value, scale = split_heads(qkv, heads)
    scores = jnp.einsum("sqhd,skhd->shqk", query, key, preferred_element_type=jnp.float32) * scale
    causal = jnp.arange(LEN)[:, None] >= jnp.arange(LEN)[None, :]
    scores = jnp.where(causal, scores, -1e30)
    top = jnp.max(scores, axis=-1, keepdims=True)
    expo = jnp.exp(scores - top)
    probs = expo / jnp.sum(expo, axis=-1, keepdims=True)
    probs_low = probs.astype(jnp.bfloat16)
    mixed = jnp.einsum("shqk,skhd->sqhd", probs_low, value, preferred_element_type=jnp.float32)
    return (probs, probs_low, mixed.reshape(qkv.shape[0], -1).astype(jnp.bfloat16))


def attend_back(qkv, probs, probs_low, grad_mixed, heads):
    query, key, value, scale = split_heads(qkv, heads)
    grad_heads = grad_mixed.reshape(query.shape)
    grad_value = jnp.einsum(
        "shqk,sqhd->skhd", probs_low, grad_heads, preferred_element_type=jnp.float32
    )
    grad_probs = jnp.einsum(
        "sqhd,skhd->shqk", grad_heads, value, preferred_element_type=jnp.float32
    )
    grad_scores = probs * (grad_probs - jnp.sum(probs * grad_probs, axis=-1, keepdims=True))
    grad_low = grad_scores.astype(jnp.bfloat16)
    grad_query = (
        jnp.einsum("shqk,skhd->sqhd", grad_low, key, preferred_element_type=jnp.float32) * scale
    )
    grad_key = (
        jnp.einsum("shqk,sqhd->skhd", grad_low, query, preferred_element_type=jnp.float32) * scale
    )
    stacked = jnp.stack([grad_query, grad_key, grad_value], axis=2)
    return stacked.reshape(qkv.shape).astype(jnp.bfloat16)


def expert_forward(rows, first, second):
    pre = jnp.dot(rows, first, preferred_element_type=jnp.float32)
    act = gelu_exact(pre).astype(jnp.bfloat16)
    result = jnp.dot(act, second, preferred_element_type=jnp.float32)
    return (pre, act, result)


def expert_rows_back(first, second, pre, grad_result):
    grad_act = lax.dot_general(grad_result, second, (((1,), (1,)), ((), ())), preferred_element_type=F32)
    unused, gelu_pull = jax.vjp(gelu_exact, pre)
    grad_pre = gelu_pull(grad_act)[0].astype(jnp.bfloat16)
    grad_rows = lax.dot_general(grad_pre, first, (((1,), (1,)), ((), ())), preferred_element_type=F32)
    return grad_pre, grad_rows


def expert_weight_grads(rows, grad_pre, act, grad_result):
    over_rows = (((0,), (0,)), ((), ()))
    grad_second = lax.dot_general(act, grad_result, over_rows, preferred_element_type=F32)
    grad_first = lax.dot_general(rows, grad_pre, over_rows, preferred_element_type=F32)
    return grad_first, grad_second


def adam_step(master, state, grad, rate, number):
    fresh, first, second = adam_values(master, state[0], state[1], grad, rate, number)
    return fresh, (first, second)


def cols_and_square(wide, square):
    return jnp.stack([wide[:, :768], wide[:, 768:1536], wide[:, 1536:], square])


def extra_rows(all_extra, start):
    return jnp.pad(all_extra[:, start : start + 19].T, ((0, 5), (0, 0)))


def body(
    tokens,
    out_grad,
    expert_ids,
    replay,
    frozen_in,
    frozen_out,
    gains,
    w_qkv,
    w_proj,
    router,
    exp_in,
    exp_out,
    mom_gains,
    mom_qkv,
    mom_proj,
    mom_router,
    mom_in,
    mom_out,
    state_gains,
    state_qkv,
    state_proj,
    state_router,
    state_in,
    state_out,
):
    groups = lax.axis_size("group")
    frozen = frozen_in.shape[0]
    count = 17
    width = tokens.shape[2]
    tok = tokens.shape[1]
    capacity = 3 * tok // count
    start_in, start_out = tuple(
        (
            part[0].astype(jnp.float32)
            for part in turned_gather(
                (exp_in.astype(jnp.bfloat16), exp_out.astype(jnp.bfloat16)), "group", (1, 2)
            )
        )
    )
    w_start = cols_and_square(w_qkv, w_proj)
    moments = jnp.stack([cols_and_square(state_qkv[0, k], state_proj[0, k]) for k in range(2)])
    packed = jnp.concatenate(
        [router, gains.T, state_router[0, 0], state_gains[0, 0].T, state_router[0, 1], state_gains[0, 1].T], axis=1
    )
    packed = jnp.pad(packed, ((0, 0), (0, 128 - packed.shape[1])))
    whole, p_start, mv, all_extra = entry_call(w_start, moments, packed)
    p_start, mv = p_start.reshape(2, 48, 768), mv.reshape(2, 2, 48, 768)
    all_extra = all_extra.reshape(768, 128)
    pe_start = extra_rows(all_extra, 0)
    mve = jnp.stack([extra_rows(all_extra, 19), extra_rows(all_extra, 38)])
    p_now, pe_now = p_start, pe_start
    masters = [start_in, start_out]
    expert_moments = [state_in[0, :, 0], state_out[0, :, 0]]
    block_list = []
    grad_list = []
    for step in range(STEPS):
        blocks = whole.reshape(4, 768, 768)
        qkv_b = jnp.concatenate([blocks[0], blocks[1], blocks[2]], axis=1)
        proj_b = blocks[3]
        low_extra = pe_now.astype(BF16)
        router_b = low_extra[:17].T
        gain_f = low_extra[17:19].astype(F32)
        first_b = masters[0].astype(jnp.bfloat16)
        second_b = masters[1].astype(jnp.bfloat16)
        inputs = tokens[step].astype(jnp.float32)
        choices = expert_ids[step]
        factor = jnp.where(replay[step] > 0, REPLAY_WEIGHT, 1.0).astype(jnp.float32)
        cotangent = out_grad[step].astype(jnp.float32) * factor[:, None]
        normed = normalize(inputs)
        acts = (normed * gain_f[0]).astype(jnp.bfloat16)
        qkv = jnp.dot(acts, qkv_b, preferred_element_type=jnp.float32).astype(jnp.bfloat16)
        probs, probs_low, mixed = attend(qkv, HEADS)
        middle = inputs + jnp.dot(mixed, proj_b, preferred_element_type=jnp.float32)
        normed_mid = normalize(middle)
        routed = (normed_mid * gain_f[1]).astype(jnp.bfloat16)
        logits = jnp.dot(routed, router_b, preferred_element_type=jnp.float32)
        select = (choices[:, :, None] == jnp.arange(count, dtype=jnp.int32)[None, None, :]).astype(
            jnp.float32
        )
        picked = jnp.sum(select * logits[:, None, :], axis=-1)
        picked_top = jnp.max(picked, axis=-1, keepdims=True)
        picked_exp = jnp.exp(picked - picked_top)
        weights = picked_exp / jnp.sum(picked_exp, axis=-1, keepdims=True)
        place, table = route_table(choices, count, capacity)
        doubled = jnp.repeat(routed, 2, axis=0)
        grad_choice = (weights[:, :, None] * cotangent[:, None, :]).reshape(2 * tok, width).astype(BF16)
        both = jnp.concatenate([doubled, grad_choice], axis=1)
        padded = jnp.concatenate([jnp.zeros((1, 2 * width), jnp.bfloat16), both])
        rows = padded[table].reshape(count, capacity, 2 * width)
        sent = jnp.concatenate([rows[frozen:], rows[frozen:]])
        arrived = lax.all_to_all(sent, ("dp", "expert"), split_axis=0, concat_axis=0, tiled=True)
        frozen_rows, frozen_grad = rows[0, :, :width], rows[0, :, width:]
        frozen_pre, frozen_act, frozen_res = expert_forward(frozen_rows, frozen_in[0], frozen_out[0])
        unused_pre, frozen_back = expert_rows_back(frozen_in[0], frozen_out[0], frozen_pre, frozen_grad)
        expert_rows = arrived[:, :, :width].reshape(-1, width)
        expert_grad = arrived[:, :, width:].reshape(-1, width)
        pre, act, partial_value = expert_forward(expert_rows, first_b, second_b)
        grad_pre, partial_rows = expert_rows_back(first_b, second_b, pre, expert_grad)
        answer = jnp.concatenate([partial_value.astype(BF16), partial_rows.astype(BF16)], axis=1)
        answer = answer.reshape(32, capacity, 2 * width)
        returned = lax.all_to_all(answer, ("dp", "expert"), split_axis=0, concat_axis=0, tiled=True)
        returned = returned.astype(F32)
        returned = (returned[:16] + returned[16:]).astype(BF16).astype(F32).reshape(-1, 2 * width)
        grads = expert_weight_grads(expert_rows, grad_pre, act, expert_grad)
        outputs = jnp.concatenate([jnp.concatenate([frozen_res, frozen_back], axis=1), returned])
        gathered_both = outputs[place].reshape(tok, 2, 2 * width)
        gathered = gathered_both[:, :, :width]
        block = middle + jnp.sum(weights[:, :, None] * gathered, axis=1)
        block_list.append(block.astype(jnp.bfloat16))
        grad_pick = jnp.sum(cotangent[:, None, :] * gathered, axis=-1)
        grad_logit_pick = weights * (
            grad_pick - jnp.sum(weights * grad_pick, axis=-1, keepdims=True)
        )
        grad_logits = jnp.sum(select * grad_logit_pick[:, :, None], axis=1)
        grad_router = jnp.dot(
            grad_logits.T, routed.astype(jnp.float32), precision=lax.Precision.HIGHEST
        )
        grad_routed = jnp.dot(
            grad_logits, router_b.astype(jnp.float32).T, precision=lax.Precision.HIGHEST
        )
        grad_routed = grad_routed + jnp.sum(gathered_both[:, :, width:], axis=1)
        grad_gain_two = jnp.sum(normed_mid * grad_routed, axis=0)
        grad_middle = cotangent + norm_back(middle, grad_routed * gain_f[1])
        grad_branch = grad_middle.astype(jnp.bfloat16)
        over_rows = (((0,), (0,)), ((), ()))
        grad_proj = lax.dot_general(mixed, grad_branch, over_rows, preferred_element_type=F32)
        grad_mixed = jnp.einsum(
            "te,de->td", grad_branch, proj_b, preferred_element_type=jnp.float32
        ).astype(jnp.bfloat16)
        grad_qkv = attend_back(qkv, probs, probs_low, grad_mixed, HEADS)
        grad_acts = jnp.einsum("te,de->td", grad_qkv, qkv_b, preferred_element_type=jnp.float32)
        grad_gain_one = jnp.sum(normed * grad_acts, axis=0)
        grad_list.append(grad_middle + norm_back(inputs, grad_acts * gain_f[0]))
        dense_grads = jnp.stack(
            [
                lax.dot_general(acts, grad_qkv[:, k * 768 : (k + 1) * 768], over_rows, preferred_element_type=F32)
                for k in range(3)
            ]
            + [grad_proj]
        ).astype(BF16).reshape(WHOLE)
        extra = jnp.concatenate(
            [grad_router, grad_gain_one[None], grad_gain_two[None], jnp.zeros((5, 768), F32)]
        )
        if step == 0:
            whole, p_now, mv, pe_now, mve = renew_call(STEP, dense_grads, extra, p_now, mv, pe_now, mve)
        else:
            w_new, mom_new, delta_e = final_call(
                STEP + 1, dense_grads, extra, p_now, mv, pe_now, mve, p_start, pe_start,
                w_start, cols_and_square(mom_qkv, mom_proj),
            )
        for index in range(2):
            masters[index], expert_moments[index] = adam_step(
                masters[index], expert_moments[index], grads[index], RATES[4 + index], STEP + step
            )
    expert_deltas = (
        lax.psum_scatter(
            (start_in - masters[0]).astype(jnp.bfloat16), "group", scatter_dimension=0, tiled=True
        ).astype(jnp.float32),
        lax.psum_scatter(
            (start_out - masters[1]).astype(jnp.bfloat16), "group", scatter_dimension=1, tiled=True
        ).astype(jnp.float32),
    )
    at = 24 * (16 * lax.axis_index("dp") + lax.axis_index("expert"))
    mine = lax.dynamic_slice(delta_e, (0, at), (24, 24))
    new_params = []
    new_moms = []
    for delta, begin, moment in (
        (mine[17:19], gains, mom_gains),
        (mine[:17].T, router, mom_router),
        (expert_deltas[0][None] / groups, exp_in, mom_in),
        (expert_deltas[1][None] / groups, exp_out, mom_out),
    ):
        renewed = OUTER_MOMENTUM * moment + delta
        new_moms.append(renewed)
        new_params.append(begin - OUTER_RATE * (delta + OUTER_MOMENTUM * renewed))
    wide = lambda stack: jnp.concatenate([stack[0], stack[1], stack[2]], axis=1)
    return (
        jnp.stack(block_list),
        jnp.stack(grad_list),
        new_params[0],
        wide(w_new),
        w_new[3],
        new_params[1],
        new_params[2],
        new_params[3],
        new_moms[0],
        wide(mom_new),
        mom_new[3],
        new_moms[1],
        new_moms[2],
        new_moms[3],
    )


def solution(mesh):
    return jax.shard_map(
        body,
        mesh=mesh,
        in_specs=(
            P(None, ("group", "dp", "expert"), None),
            P(None, ("group", "dp", "expert"), None),
            P(None, ("group", "dp", "expert"), None),
            P(None, ("group", "dp", "expert")),
            P(),
            P(),
            P(None, ("dp", "expert")),
            P(("dp", "expert"), None),
            P(("dp", "expert"), None),
            P(("dp", "expert"), None),
            P("expert", "group", "dp"),
            P("expert", "dp", "group"),
            P(None, ("dp", "expert")),
            P(("dp", "expert"), None),
            P(("dp", "expert"), None),
            P(("dp", "expert"), None),
            P("expert", "group", "dp"),
            P("expert", "dp", "group"),
            P("group", None, None, ("dp", "expert")),
            P("group", None, ("dp", "expert"), None),
            P("group", None, ("dp", "expert"), None),
            P("group", None, ("dp", "expert"), None),
            P("group", None, "expert", None, "dp"),
            P("group", None, "expert", "dp", None),
        ),
        out_specs=(
            P(None, ("group", "dp", "expert"), None),
            P(None, ("group", "dp", "expert"), None),
            P(None, ("dp", "expert")),
            P(("dp", "expert"), None),
            P(("dp", "expert"), None),
            P(("dp", "expert"), None),
            P("expert", "group", "dp"),
            P("expert", "dp", "group"),
            P(None, ("dp", "expert")),
            P(("dp", "expert"), None),
            P(("dp", "expert"), None),
            P(("dp", "expert"), None),
            P("expert", "group", "dp"),
            P("expert", "dp", "group"),
        ),
        check_vma=False,
    )
```

```python
import functools

import jax
import jax.numpy as jnp
from jax import lax
from jax.experimental import pallas as pl
from jax.experimental.pallas import tpu as pltpu
from jax.sharding import PartitionSpec as P

MESH = pl.DeviceIdType.MESH
VMEM = pltpu.VMEM
F32 = jnp.float32
BF16 = jnp.bfloat16


class Links:
    def __init__(self, sends, recvs):
        self.sends, self.recvs, self.used, self.begun = sends, recvs, 0, []

    def make(self, src, dst, to):
        at = self.used
        self.used += 1
        copy = pltpu.make_async_remote_copy(
            src_ref=src, dst_ref=dst, send_sem=self.sends.at[at], recv_sem=self.recvs.at[at],
            device_id=to, device_id_type=MESH,
        )
        self.begun.append(copy)
        return copy

    def send(self, src, dst, to):
        copy = self.make(src, dst, to)
        copy.start()
        return copy

    def finish(self):
        for copy in self.begun:
            copy.wait_send()


class Place:
    def __init__(self):
        self.g, self.d = lax.axis_index("group"), lax.axis_index("dp")
        e = lax.axis_index("expert")
        self.x, self.y = lax.div(e, 4), lax.rem(e, 4)

    def along_x(self, step):
        return {"expert": lax.rem(self.x + step, 4) * 4 + self.y}

    def along_y(self, step):
        return {"expert": self.x * 4 + lax.rem(self.y + step, 4)}

    def other_dp(self):
        return {"dp": 1 - self.d}

    def in_group(self, step):
        return {"group": lax.rem(self.g + step, 4)}

    def other_core(self):
        return {"group": self.g + 1 - 2 * lax.rem(self.g, 2)}


def greet(partners):
    barrier = pltpu.get_barrier_semaphore()
    for partner in partners:
        pl.semaphore_signal(barrier, inc=1, device_id=partner, device_id_type=MESH)
    pl.semaphore_wait(barrier, len(partners))


class Gather:
    def __init__(self, links, place, whole, h, p1, p2, near1, near2, at):
        self.links, self.whole, self.h, self.at = links, whole, h, at
        self.d, self.place = place.d, place
        self.p1, self.p2, self.near1, self.near2 = p1, p2, near1, near2

    def slot(self, k1, k2, dp=None):
        c, x = self.at(lax.rem(k1, 4), lax.rem(k2, 4))
        return self.whole.at[c, slice(None) if dp is None else dp, x, self.h]

    def push(self, k1, k2, dp, to):
        ref = self.slot(k1, k2, dp)
        return self.links.send(ref, ref, to)

    def start(self):
        p1, p2, d = self.p1, self.p2, self.d
        self.over_dp = self.push(p1, p2, d, self.place.other_dp())
        self.own = [self.push(p1, p2, d, self.near1(1)), self.push(p1, p2, d, self.near1(3))]

    def ring_one(self):
        p1, p2, d = self.p1, self.p2, self.d
        self.over_dp.wait_recv()
        self.own += [self.push(p1, p2, 1 - d, self.near1(1)), self.push(p1, p2, 1 - d, self.near1(3))]
        self.pushed = [(p1, self.push(p1, p2, None, self.near2(1)), self.push(p1, p2, None, self.near2(3)))]
        for copy in self.own:
            copy.wait_recv()
        self.passed = [self.push(p1 + 3, p2, 0, self.near1(1)), self.push(p1 + 1, p2, 1, self.near1(3))]
        for k1 in (p1 + 3, p1 + 1):
            self.pushed.append((k1, self.push(k1, p2, None, self.near2(1)), self.push(k1, p2, None, self.near2(3))))

    def ring_two(self):
        p1, p2 = self.p1, self.p2
        for copy in self.passed:
            copy.wait_recv()
        k1 = p1 + 2
        self.pushed.append((k1, self.push(k1, p2, None, self.near2(1)), self.push(k1, p2, None, self.near2(3))))
        self.last = []
        for k1, right, left in self.pushed:
            right.wait_recv()
            self.last.append(self.push(k1, p2 + 3, 0, self.near2(1)))
            left.wait_recv()
            self.last.append(self.push(k1, p2 + 1, 1, self.near2(3)))

    def end(self):
        for copy in self.last:
            copy.wait_recv()


def gather_parts(links, place, whole):
    by_x = lambda kx, ky: (ky, kx)
    by_y = lambda ky, kx: (ky, kx)
    first = Gather(links, place, whole, 0, place.x, place.y, place.along_x, place.along_y, by_x)
    second = Gather(links, place, whole, 1, place.y, place.x, place.along_y, place.along_x, by_y)
    return first, second


def gather_all(links, place, whole):
    parts = gather_parts(links, place, whole)
    for stage in ("start", "ring_one", "ring_two", "end"):
        for part in parts:
            getattr(part, stage)()


class RingSum:
    def __init__(self, links, near, p, term, far, near_buf, add):
        self.links, self.near, self.p, self.term = links, near, p, term
        self.far, self.near_buf, self.add = far, near_buf, add

    def start(self):
        p, links = self.p, self.links
        right, left = self.near(1), self.near(3)
        self.far_copies = [
            links.send(self.term(p + 2, 1), self.far.at[0], right),
            links.send(self.term(p + 2, 0), self.far.at[1], left),
        ]
        self.direct = [
            links.send(self.term(p + 1, 0), self.near_buf.at[0, 0], right),
            links.send(self.term(p + 3, 1), self.near_buf.at[1, 1], left),
        ]

    def middle(self):
        p, links = self.p, self.links
        for side, to, dp, k in ((0, self.near(1), 1, p + 1), (1, self.near(3), 0, p + 3)):
            self.far_copies[side].wait_recv()
            self.far[side] = (self.far[side].astype(F32) + self.term(k, dp)[...].astype(F32)).astype(BF16)
            self.direct.append(links.send(self.far.at[side], self.near_buf.at[side, dp], to))

    def finish(self):
        for copy in self.direct:
            copy.wait_recv()
        return [
            self.term(self.p, dp)[...].astype(F32)
            + self.near_buf[0, dp].astype(F32)
            + self.near_buf[1, dp].astype(F32)
            for dp in range(2)
        ]


def add_over(links, own, box, position, size, reach):
    box[position] = own
    copies = [links.send(box.at[position], box.at[position], reach(step)) for step in range(1, size)]

    def finish():
        for copy in copies:
            copy.wait_recv()
        total = box[0]
        for k in range(1, size):
            total = total + box[k]
        return total

    return finish


def ring_scratch(blocks):
    return [VMEM((2, *blocks, 48, 768), BF16), VMEM((2, 2, *blocks, 48, 768), BF16)]


def reduce_all(links, place, grads, extra, scratch, result):
    (far_a, near_a, far_b, near_b, mid_a, mid_b, far_c, near_c, far_d, near_d, last, zbox, box_x, box_y, box_z) = scratch
    r4 = lambda k: lax.rem(k, 4)
    first = RingSum(links, place.along_y, place.y, lambda k, dp: grads.at[r4(k), dp, :, 0], far_a, near_a, None)
    second = RingSum(links, place.along_x, place.x, lambda k, dp: grads.at[:, dp, r4(k), 1], far_b, near_b, None)
    first.start()
    second.start()
    extra_x = add_over(links, extra[...], box_x, place.x, 4, place.along_x)
    first.middle()
    second.middle()
    extra_y = add_over(links, extra_x(), box_y, place.y, 4, place.along_y)
    for part, mid in ((first, mid_a), (second, mid_b)):
        for dp, value in enumerate(part.finish()):
            mid[dp] = value.astype(BF16)
    third = RingSum(links, place.along_x, place.x, lambda k, dp: mid_a.at[dp, r4(k)], far_c, near_c, None)
    fourth = RingSum(links, place.along_y, place.y, lambda k, dp: mid_b.at[dp, r4(k)], far_d, near_d, None)
    third.start()
    fourth.start()
    total_xy = extra_y()
    extra_z = add_over(links, total_xy, box_z, place.d, 2, lambda step: place.other_dp())
    third.middle()
    fourth.middle()
    over = []
    for h, part in enumerate((third, fourth)):
        for dp, value in enumerate(part.finish()):
            last[dp, h] = value.astype(BF16)
        over.append(links.send(last.at[1 - place.d, h], zbox.at[h], place.other_dp()))
    for h in range(2):
        over[h].wait_recv()
        result[h] = last[place.d, h].astype(F32) + zbox[h].astype(F32)
    return extra_z()


REDUCE_SCRATCH = (
    ring_scratch((4,)) + ring_scratch((4,))
    + [VMEM((2, 4, 48, 768), BF16)] * 2
    + ring_scratch(()) + ring_scratch(())
    + [VMEM((2, 2, 48, 768), BF16), VMEM((2, 48, 768), BF16)]
    + [VMEM((4, 24, 768), F32), VMEM((4, 24, 768), F32), VMEM((2, 24, 768), F32)]
)
REDUCE_COPIES = 4 * 6 + 2 + 7
GATHER_COPIES = 2 * 23


def ring_partners(place):
    return (
        [place.along_x(k) for k in (1, 2, 3)]
        + [place.along_y(k) for k in (1, 2, 3)]
        + [place.other_dp()]
    )


EPS_NORM = 1e-06
BETA_ONE = 0.9
BETA_TWO = 0.95
ADAM_EPS = 1e-08
DECAY = 0.1
OUTER_RATE = 0.7
OUTER_MOMENTUM = 0.9
REPLAY_WEIGHT = 0.25
RATES = (0.6, 0.04, 0.3, 0.03, 0.04, 0.02)
HEADS = 12
LEN = 128
STEPS = 2
STEP = 10


def entry_kernel(p_in, mv_in, e_in, whole, p_out, mv_out, e_out, sends, recvs):
    place = Place()
    greet(ring_partners(place) + [place.other_core()])
    links = Links(sends, recvs)
    x, y, d = place.x, place.y, place.d
    h = lax.rem(place.g, 2)
    masters = [links.send(p_in.at[lax.rem(y + k, 4)], p_out.at[y], place.along_y(k)) for k in (1, 2, 3)]
    e_out[d, x, y] = e_in[...]
    mine = e_out.at[d, x, y]
    extra_z = links.send(mine, mine, place.other_dp())
    p_out[y] = p_in[y]
    mv_out[:, y] = mv_in[:, y]
    for copy in masters:
        copy.wait_recv()
    low = p_out[...].astype(BF16).reshape(2, 48, 768)

    @pl.when(h == 0)
    def _():
        whole[y, d, x, 0] = low[0]

    @pl.when(h == 1)
    def _():
        whole[y, d, x, 1] = low[1]

    def mix(a, b):
        return a * (1 - h) + b * h

    def near1(step):
        return {"expert": mix(place.along_x(step)["expert"], place.along_y(step)["expert"])}

    def near2(step):
        return {"expert": mix(place.along_y(step)["expert"], place.along_x(step)["expert"])}

    def at(k1, k2):
        return mix(k2, k1), mix(k1, k2)

    part = Gather(links, place, whole, h, mix(x, y), mix(y, x), near1, near2, at)
    p1, p2 = part.p1, part.p2
    part.start()
    extra_z.wait_recv()
    mine = e_out.at[:, x, y]
    extra_x = [links.send(mine, mine, place.along_x(k)) for k in (1, 2, 3)]
    part.ring_one()
    share = place.other_core()
    shared = [part.push(k1, p2, None, share) for k1 in (p1, p1 + 3, p1 + 1)]
    for copy in extra_x:
        copy.wait_recv()
    mine = e_out.at[:, :, y]
    extra_y = [links.send(mine, mine, place.along_y(k)) for k in (1, 2, 3)]
    part.ring_two()
    moments = [links.send(mv_in.at[:, lax.rem(y + k, 4)], mv_out.at[:, y], place.along_y(k)) for k in (1, 2, 3)]
    shared.append(part.push(p1 + 2, p2, None, share))
    for k1 in (p1, p1 + 3, p1 + 1, p1 + 2):
        shared += [part.push(k1, p2 + 3, None, share), part.push(k1, p2 + 1, None, share)]
    part.end()
    shared += [part.push(k1, p2 + 2, None, share) for k1 in (p1, p1 + 3, p1 + 1, p1 + 2)]
    for copy in shared:
        copy.wait_recv()
    for copy in extra_y + moments:
        copy.wait_recv()
    links.finish()


def adam_values(master, first, second, grad, rate, number):
    first = BETA_ONE * first + (1.0 - BETA_ONE) * grad
    second = BETA_TWO * second + (1.0 - BETA_TWO) * grad * grad
    fix_one = 1.0 - BETA_ONE**number
    fix_two = 1.0 - BETA_TWO**number
    update = first / fix_one / (jnp.sqrt(second / fix_two) + ADAM_EPS) + DECAY * master
    return master - rate * update, first, second


def block_rate(place):
    return jnp.where(place.y == 3, RATES[2], RATES[1]).astype(F32)


def extra_rates():
    row = lax.broadcasted_iota(jnp.int32, (24, 768), 0)
    return jnp.where(row < 17, RATES[3], RATES[0]).astype(F32)


def renew_kernel(number, grads, extra, p_in, mv_in, pe_in, mve_in,
                 whole, p_out, mv_out, pe_out, mve_out, result, *scratch):
    *scratch, sends, recvs = scratch
    place = Place()
    greet(ring_partners(place))
    links = Links(sends, recvs)
    total = reduce_all(links, place, grads, extra, scratch, result)
    fresh, first, second = adam_values(p_in[...], mv_in[0], mv_in[1], result[...], block_rate(place), number)
    whole[place.y, place.d, place.x] = fresh.astype(BF16)
    gather = gather_parts(links, place, whole)
    for part in gather:
        part.start()
    p_out[...] = fresh
    mv_out[0] = first
    mv_out[1] = second
    pe_out[...], mve_out[0], mve_out[1] = adam_values(pe_in[...], mve_in[0], mve_in[1], total, extra_rates(), number)
    for stage in ("ring_one", "ring_two", "end"):
        for part in gather:
            getattr(part, stage)()
    links.finish()


def final_kernel(number, grads, extra, p_in, mv_in, pe_in, mve_in, p_start, pe_start, w_old, mom_old,
                 w_new, mom_new, delta_e, result, delta, quarters, whole, turned, boxes, *scratch):
    *scratch, sends, recvs = scratch
    place = Place()
    greet(ring_partners(place) + [place.in_group(k) for k in (1, 2, 3)])
    links = Links(sends, recvs)
    g, y = place.g, place.y
    total = reduce_all(links, place, grads, extra, scratch, result)
    fresh, _, _ = adam_values(p_in[...], mv_in[0], mv_in[1], result[...], block_rate(place), number)
    delta[...] = (p_start[...] - fresh).reshape(4, 24, 768)
    summed = [
        links.send(delta.at[lax.rem(g + k, 4)], quarters.at[g], place.in_group(k)) for k in (1, 2, 3)
    ]
    fresh_e, _, _ = adam_values(pe_in[...], mve_in[0], mve_in[1], total, extra_rates(), number)
    sum_e = add_over(links, pe_start[...] - fresh_e, boxes, g, 4, place.in_group)
    quarters[g] = delta[g]
    for copy in summed:
        copy.wait_recv()
    whole[g] = (quarters[0] + quarters[1] + quarters[2] + quarters[3]) * 0.25
    spread = [links.send(whole.at[g], whole.at[g], place.in_group(k)) for k in (1, 2, 3)]
    delta_e[...] = sum_e() * 0.25
    for copy in spread:
        copy.wait_recv()
    turned[y] = whole[y]
    across = [links.send(whole.at[lax.rem(y + k, 4)], turned.at[y], place.along_y(k)) for k in (1, 2, 3)]
    for copy in across:
        copy.wait_recv()
    mean = turned[...]
    renewed = OUTER_MOMENTUM * mom_old[...] + mean
    mom_new[...] = renewed
    w_new[...] = w_old[...] - OUTER_RATE * (mean + OUTER_MOMENTUM * renewed)
    links.finish()


def semaphores(count):
    return [pltpu.SemaphoreType.DMA((count,)), pltpu.SemaphoreType.DMA((count,))]


def vmem_call(kernel, outs, scratch, collective_id, *args, limit=56 << 20):
    return pl.pallas_call(
        kernel,
        out_shape=tuple(jax.ShapeDtypeStruct(shape, kind) for shape, kind in outs),
        in_specs=[pl.BlockSpec(memory_space=VMEM)] * len(args),
        out_specs=tuple(pl.BlockSpec(memory_space=VMEM) for _ in outs),
        scratch_shapes=scratch,
        compiler_params=pltpu.CompilerParams(
            collective_id=collective_id, has_side_effects=True, vmem_limit_bytes=limit
        ),
    )(*args)


WHOLE = (4, 2, 4, 2, 48, 768)


def entry_call(p_in, mv_in, e_in):
    return vmem_call(
        entry_kernel,
        [(WHOLE, BF16), ((4, 24, 768), F32), ((2, 4, 24, 768), F32), ((2, 4, 4, 24, 128), F32)],
        semaphores(3 + 7 + 23 + 3 + 16), 1, p_in, mv_in, e_in,
    )


def renew_call(number, *args):
    return vmem_call(
        functools.partial(renew_kernel, number),
        [(WHOLE, BF16), ((2, 48, 768), F32), ((2, 2, 48, 768), F32), ((24, 768), F32), ((2, 24, 768), F32)],
        [VMEM((2, 48, 768), F32)] + REDUCE_SCRATCH + semaphores(REDUCE_COPIES + GATHER_COPIES), 2, *args,
    )


def final_call(number, *args):
    box = VMEM((4, 24, 768), F32)
    return vmem_call(
        functools.partial(final_kernel, number),
        [((4, 24, 768), F32), ((4, 24, 768), F32), ((24, 768), F32)],
        [VMEM((2, 48, 768), F32), box, box, box, box, box] + REDUCE_SCRATCH + semaphores(REDUCE_COPIES + 12),
        3, *args,
    )

CAP = 24
TOK = 128
DIMS = {"nn": (((1,), (0,)), ((), ())), "nt": (((1,), (1,)), ((), ())), "tn": (((0,), (0,)), ((), ()))}


def mm(a, b, form="nn"):
    return lax.dot_general(a, b, DIMS[form], preferred_element_type=F32)


def split_low(values):
    high = values.astype(BF16)
    return high, (values - high.astype(F32)).astype(BF16)


def row_scale(values):
    return lax.rsqrt(jnp.mean(values * values, axis=-1, keepdims=True) + EPS_NORM)


def iota(shape, dim):
    return lax.broadcasted_iota(jnp.int32, shape, dim)


def routing(ids):
    names = [(iota((24, TOK), 0) == ids[k : k + 1]).astype(F32) for k in range(2)]
    either = names[0] + names[1]
    earlier = (iota((TOK, TOK), 0) < iota((TOK, TOK), 1)).astype(BF16)
    slot = mm(either.astype(BF16), earlier).astype(jnp.int32)
    taken = jnp.where(iota((17, CAP, TOK), 1) == slot[:17][:, None, :], 1.0, 0.0)
    return names, taken * either[:17][:, None, :]


def pair_stack(part):
    lane = iota(part.shape, 1)
    zero = jnp.zeros_like(part)
    return jnp.concatenate([jnp.where(lane < 64, part, zero), jnp.where(lane < 64, zero, part)], axis=0)


def side_by_side(stacked):
    return jnp.concatenate([stacked[:TOK], stacked[TOK:]], axis=1)


def front_kernel(x_ref, og_ref, factor_ref, ids_ref, whole, pe_ref,
                 send, frozen, qkv_out, probs_out, mixed_out, middle_out, a1_out, a2_out, weights_out):
    gain = pe_ref[16:24].astype(BF16).astype(F32)
    x = x_ref[...].astype(F32)
    a1 = (x * row_scale(x) * gain[1:2]).astype(BF16)
    a1_out[...] = a1
    for c in range(3):
        qkv_out[c] = mm(a1, whole[c]).astype(BF16)
    row, col = iota((2 * TOK, TOK), 0), iota((2 * TOK, TOK), 1)
    causal = lax.rem(row, TOK) >= col
    for pair in range(6):
        lanes = slice(128 * pair, 128 * pair + 128)
        scores = mm(pair_stack(qkv_out[0, :, lanes]), qkv_out[1, :, lanes], "nt") * 0.125
        scores = jnp.where(causal, scores, -1e30)
        expo = jnp.exp(scores - jnp.max(scores, axis=-1, keepdims=True))
        probs = expo / jnp.sum(expo, axis=-1, keepdims=True)
        probs_out[pair] = probs
        mixed_out[:, lanes] = mm(side_by_side(probs.astype(BF16)), pair_stack(qkv_out[2, :, lanes])).astype(BF16)
    middle = x + mm(mixed_out[...], whole[3])
    middle_out[...] = middle
    a2 = (middle * row_scale(middle) * gain[2:3]).astype(BF16)
    a2_out[...] = a2
    logits = mm(pe_ref[...].astype(BF16), a2, "nt")
    names, taken = routing(ids_ref[...])
    picked = [jnp.sum(name * logits, axis=0, keepdims=True) for name in names]
    top = jnp.maximum(picked[0], picked[1])
    expo = [jnp.exp(z - top) for z in picked]
    whole_sum = expo[0] + expo[1]
    weights = [e / whole_sum for e in expo]
    weights_out[...] = jnp.zeros((8, TOK), F32)
    for k in range(2):
        weights_out[k : k + 1] = weights[k]
    by_expert = names[0] * weights[0] + names[1] * weights[1]
    row_weight = jnp.sum(taken * by_expert[:17][:, None, :], axis=-1, keepdims=True)
    cot = (og_ref[...].astype(F32) * factor_ref[...]).astype(BF16)
    low = taken.astype(BF16).reshape(17 * CAP, TOK)
    rows = mm(low, a2).reshape(17, CAP, 768)
    grads = mm(low, cot).reshape(17, CAP, 768) * row_weight
    both = jnp.concatenate([rows, grads], axis=1).astype(BF16)
    frozen[...] = both[0]
    send[...] = both[1:]


def back_kernel(x_ref, og_ref, factor_ref, ids_ref, whole, pe_ref, qkv, probs_ref, mixed, middle_ref, a1, a2,
                weights_ref, ret, frozen, block_out, grad_out, grads, extra):
    gain = pe_ref[16:24].astype(BF16).astype(F32)
    low_rows = pe_ref[...].astype(BF16)
    cot = og_ref[...].astype(F32) * factor_ref[...]
    names, taken = routing(ids_ref[...])
    weights = [weights_ref[k : k + 1] for k in range(2)]
    by_expert = names[0] * weights[0] + names[1] * weights[1]
    row_weight = jnp.sum(taken * by_expert[:17][:, None, :], axis=-1, keepdims=True)
    low = taken.astype(BF16).reshape(17 * CAP, TOK)
    both = (ret[:16].astype(F32) + ret[16:].astype(F32)).astype(BF16).astype(F32)
    both = jnp.concatenate([frozen[...][None], both], axis=0)
    results, back = both[:, :CAP], both[:, CAP:].reshape(17 * CAP, 768)
    high, rest = split_low((results * row_weight).reshape(17 * CAP, 768))
    middle = middle_ref[...]
    block_out[...] = (middle + mm(low, high, "tn") + mm(low, rest, "tn")).astype(BF16)
    cot_rows = mm(low, cot.astype(BF16)).reshape(17, CAP, 768)
    grad_row = jnp.sum(cot_rows * results, axis=-1, keepdims=True)
    by_name = jnp.concatenate([jnp.sum(taken * grad_row, axis=1), jnp.zeros((7, TOK), F32)], axis=0)
    grad_w = [jnp.sum(name * by_name, axis=0, keepdims=True) for name in names]
    mean = weights[0] * grad_w[0] + weights[1] * grad_w[1]
    grad_logits = sum(names[k] * (weights[k] * (grad_w[k] - mean)) for k in range(2))
    high, rest = split_low(grad_logits)
    extra[0:16] = (mm(high, a2[...]) + mm(rest, a2[...]))[0:16]
    last_router = (mm(high, a2[...]) + mm(rest, a2[...]))[16:17]
    da2 = mm(high, low_rows, "tn") + mm(rest, low_rows, "tn")
    high, rest = split_low(back)
    da2 = da2 + mm(low, high, "tn") + mm(low, rest, "tn")
    scale = row_scale(middle)
    normed = middle * scale
    dg2 = jnp.sum(normed * da2, axis=0, keepdims=True)
    into = da2 * gain[2:3]
    dmiddle = cot + scale * (into - normed * jnp.mean(into * normed, axis=-1, keepdims=True))
    branch = dmiddle.astype(BF16)
    grads[3] = mm(mixed[...], branch, "tn").astype(BF16)
    dmixed = mm(branch, whole[3], "nt").astype(BF16)
    da1 = jnp.zeros((TOK, 768), F32)
    parts = [[], [], []]
    for pair in range(6):
        lanes = slice(128 * pair, 128 * pair + 128)
        probs = probs_ref[pair]
        dms = pair_stack(dmixed[:, lanes])
        parts[2].append(mm(probs.astype(BF16), dms, "tn").astype(BF16))
        dpb = mm(dms, qkv[2, :, lanes], "nt")
        ds = (probs * (dpb - jnp.sum(probs * dpb, axis=-1, keepdims=True))).astype(BF16)
        parts[0].append((mm(side_by_side(ds), pair_stack(qkv[1, :, lanes])) * 0.125).astype(BF16))
        parts[1].append((mm(ds, pair_stack(qkv[0, :, lanes]), "tn") * 0.125).astype(BF16))
    for c in range(3):
        dqkv = jnp.concatenate(parts[c], axis=1)
        grads[c] = mm(a1[...], dqkv, "tn").astype(BF16)
        da1 = da1 + mm(dqkv, whole[c], "nt")
    x = x_ref[...].astype(F32)
    scale = row_scale(x)
    normed = x * scale
    dg1 = jnp.sum(normed * da1, axis=0, keepdims=True)
    into = da1 * gain[1:2]
    grad_out[...] = dmiddle + scale * (into - normed * jnp.mean(into * normed, axis=-1, keepdims=True))
    extra[16:24] = jnp.concatenate([last_router, dg1, dg2, jnp.zeros((5, 768), F32)], axis=0)


SQRT_HALF = 0.7071067811865476
DENSITY = 0.3989422804014327


def expert_rows(rows, grad, first, second):
    u = mm(rows, first)
    chance = 0.5 + 0.5 * lax.erf(u * SQRT_HALF)
    h = (u * chance).astype(BF16)
    value = mm(h, second)
    slope = chance + u * (jnp.exp(u * u * -0.5) * DENSITY)
    du = (slope * mm(grad, second, "nt")).astype(BF16)
    return value, mm(du, first, "nt"), h, du


def trade_kernel(send, frozen_in, w1_hbm, w2_hbm, fin_hbm, fout_hbm,
                 ret, frozen_out, rows_out, grad_out, h_out, du_out,
                 recv, ans, w1, w2, fin, fout, loads, sends, recvs, sends2, recvs2):
    copies = [
        pltpu.make_async_copy(src, dst, loads.at[k])
        for k, (src, dst) in enumerate(((fin_hbm, fin), (fout_hbm, fout), (w1_hbm, w1), (w2_hbm, w2)))
    ]
    for copy in copies:
        copy.start()
    d, e = lax.axis_index("dp"), lax.axis_index("expert")
    me = d * 16 + e

    def device(k, sign):
        dd, ee = lax.rem(k, 2), lax.div(k, 2)
        return lax.rem(d + dd, 2), lax.rem(e + sign * ee + 16, 16)

    barrier = pltpu.get_barrier_semaphore()

    @pl.loop(1, 32)
    def _(k):
        dp, ex = device(k, 1)
        pl.semaphore_signal(barrier, inc=1, device_id={"dp": dp, "expert": ex}, device_id_type=MESH)

    pl.semaphore_wait(barrier, 31)

    def out_copy(k):
        dp, ex = device(k, 1)
        return pltpu.make_async_remote_copy(
            src_ref=send.at[ex], dst_ref=recv.at[me], send_sem=sends.at[k], recv_sem=recvs.at[k],
            device_id={"dp": dp, "expert": ex}, device_id_type=MESH,
        )

    def back_copy(k):
        dp, ex = device(k, -1)
        return pltpu.make_async_remote_copy(
            src_ref=ans.at[dp * 16 + ex], dst_ref=ret.at[me], send_sem=sends2.at[k], recv_sem=recvs2.at[k],
            device_id={"dp": dp, "expert": ex}, device_id_type=MESH,
        )

    @pl.loop(1, 32)
    def _(k):
        out_copy(k).start()

    recv[me] = send[e]
    copies[0].wait()
    copies[1].wait()
    both = frozen_in[...].astype(F32)
    value, back, _, _ = expert_rows(both[:CAP].astype(BF16), both[CAP:].astype(BF16), fin[...], fout[...])
    frozen_out[...] = jnp.concatenate([value, back], axis=0)
    copies[2].wait()
    copies[3].wait()

    @pl.loop(0, 4)
    def _(j):
        @pl.loop(0, 8)
        def _(i):
            k = j * 8 + i

            @pl.when(k > 0)
            def _():
                out_copy(k).wait_recv()

        blocks = []
        for i in range(8):
            dp, ex = device(j * 8 + i, -1)
            blocks.append(recv[dp * 16 + ex].astype(F32))
        rows = jnp.concatenate([b[:CAP] for b in blocks], axis=0).astype(BF16)
        grad = jnp.concatenate([b[CAP:] for b in blocks], axis=0).astype(BF16)
        value, back, h, du = expert_rows(rows, grad, w1[...], w2[...])
        at = pl.ds(pl.multiple_of(j * 192, 192), 192)
        rows_out[at] = rows
        grad_out[at] = grad
        h_out[at] = h
        du_out[at] = du
        for i in range(8):
            dp, ex = device(j * 8 + i, -1)
            part = slice(i * CAP, (i + 1) * CAP)
            ans[dp * 16 + ex] = jnp.concatenate([value[part], back[part]], axis=0).astype(BF16)

        @pl.loop(0, 8)
        def _(i):
            k = j * 8 + i

            @pl.when(k > 0)
            def _():
                back_copy(k).start()

    ret[me] = ans[me]

    @pl.loop(1, 32)
    def _(k):
        back_copy(k).wait_recv()
        back_copy(k).wait_send()
        out_copy(k).wait_send()


def plain_call(kernel, outs, *args, scratch=(), limit=48 << 20, spaces=None):
    spaces = spaces or [VMEM] * len(args)
    return pl.pallas_call(
        kernel,
        out_shape=tuple(jax.ShapeDtypeStruct(shape, kind) for shape, kind in outs),
        in_specs=[pl.BlockSpec(memory_space=space) for space in spaces],
        out_specs=tuple(pl.BlockSpec(memory_space=VMEM) for _ in outs),
        scratch_shapes=list(scratch),
        compiler_params=pltpu.CompilerParams(vmem_limit_bytes=limit),
    )(*args)


def front_call(*args):
    row = (TOK, 768)
    return plain_call(
        front_kernel,
        [((16, 48, 768), BF16), ((48, 768), BF16), ((3, *row), BF16), ((6, 256, 128), F32), (row, BF16), (row, F32),
         (row, BF16), (row, BF16), ((8, TOK), F32)],
        *args,
    )


def back_call(*args):
    row = (TOK, 768)
    return plain_call(
        back_kernel, [(row, BF16), (row, F32), ((4, 768, 768), BF16), ((24, 768), F32)], *args
    )


def trade_call(collective_id, *args):
    wide, tall = (768, 1536), (1536, 768)
    return pl.pallas_call(
        trade_kernel,
        out_shape=tuple(
            jax.ShapeDtypeStruct(shape, kind)
            for shape, kind in (
                ((32, 48, 768), BF16), ((48, 768), F32), ((768, 768), BF16), ((768, 768), BF16), (wide, BF16), (wide, BF16)
            )
        ),
        in_specs=[pl.BlockSpec(memory_space=VMEM)] * 2 + [pl.BlockSpec(memory_space=pl.ANY)] * 4,
        out_specs=tuple(pl.BlockSpec(memory_space=VMEM) for _ in range(6)),
        scratch_shapes=[
            VMEM((32, 48, 768), BF16), VMEM((32, 48, 768), BF16), VMEM(wide, BF16), VMEM(tall, BF16),
            VMEM((768, 3072), BF16), VMEM((3072, 768), BF16), pltpu.SemaphoreType.DMA((4,)),
        ] + semaphores(32) + semaphores(32),
        compiler_params=pltpu.CompilerParams(
            collective_id=collective_id, has_side_effects=True, vmem_limit_bytes=56 << 20
        ),
    )(*args)


def grow_kernel(number, rate, first_step, lhs, rhs, w_ref, mv_ref, *refs):
    grad = mm(lhs[...], rhs[...], "tn")
    if first_step:
        w_out, mv_out, delta_out = refs
        begin = w_ref[...].astype(F32)
        fresh, first, second = adam_values(begin, mv_ref[0], mv_ref[1], grad, rate, number)
        w_out[...] = fresh.astype(BF16)
        mv_out[0] = first.astype(BF16)
        mv_out[1] = second.astype(BF16)
        delta_out[...] = (begin - fresh).astype(BF16)
    else:
        delta_in, delta_out = refs
        begin = w_ref[...].astype(F32)
        fresh, _, _ = adam_values(begin, mv_ref[0].astype(F32), mv_ref[1].astype(F32), grad, rate, number)
        delta_out[...] = (delta_in[...].astype(F32) + (begin - fresh)).astype(BF16)


def grow_call(number, rate, first_step, lhs, rhs, w, mv, *more):
    deep, wide = w.shape
    tile = 256
    mat = pl.BlockSpec((tile, wide), lambda i: (i, 0))
    pair = pl.BlockSpec((2, tile, wide), lambda i: (0, i, 0))
    low = jax.ShapeDtypeStruct((deep, wide), BF16)
    if first_step:
        outs, specs = (low, jax.ShapeDtypeStruct((2, deep, wide), BF16), low), (mat, pair, mat)
    else:
        outs, specs = low, mat
    return pl.pallas_call(
        functools.partial(grow_kernel, number, rate, first_step),
        out_shape=outs,
        grid=(deep // tile,),
        in_specs=[pl.BlockSpec((768, tile), lambda i: (0, i)), pl.BlockSpec((768, wide), lambda i: (0, 0)), mat, pair]
        + [mat] * len(more),
        out_specs=specs,
        compiler_params=pltpu.CompilerParams(vmem_limit_bytes=48 << 20),
    )(lhs, rhs, w, mv, *more)


def turned_gather(arrays, axis, dims):
    turned = [jnp.moveaxis(a, dim, 0) for a, dim in zip(arrays, dims)]
    widths = [t[0].size for t in turned]
    both = jnp.concatenate([t.reshape(-1, w) for t, w in zip(turned, widths)], axis=1)
    whole = lax.all_gather(both, axis, axis=0, tiled=True)
    blocks = jnp.split(whole, [sum(widths[:k]) for k in range(1, len(widths))], axis=1)
    return tuple(
        (
            jnp.moveaxis(b.reshape(-1, *t.shape[1:]), 0, dim)
            for b, t, dim in zip(blocks, turned, dims)
        )
    )


def cols_and_square(wide, square):
    return jnp.stack([wide[:, :768], wide[:, 768:1536], wide[:, 1536:], square])


def extra_rows(all_extra, start):
    return jnp.pad(all_extra[:, start : start + 19].T, ((0, 5), (0, 0)))


def body(
    tokens,
    out_grad,
    expert_ids,
    replay,
    frozen_in,
    frozen_out,
    gains,
    w_qkv,
    w_proj,
    router,
    exp_in,
    exp_out,
    mom_gains,
    mom_qkv,
    mom_proj,
    mom_router,
    mom_in,
    mom_out,
    state_gains,
    state_qkv,
    state_proj,
    state_router,
    state_in,
    state_out,
):
    low_in, low_out = tuple(
        part[0]
        for part in turned_gather((exp_in.astype(BF16), exp_out.astype(BF16)), "group", (1, 2))
    )
    w_start = cols_and_square(w_qkv, w_proj)
    moments = jnp.stack([cols_and_square(state_qkv[0, k], state_proj[0, k]) for k in range(2)])
    packed = jnp.concatenate(
        [router, gains.T, state_router[0, 0], state_gains[0, 0].T, state_router[0, 1], state_gains[0, 1].T], axis=1
    )
    packed = jnp.pad(packed, ((0, 0), (0, 128 - packed.shape[1])))
    ids = jnp.pad(jnp.swapaxes(expert_ids, 1, 2), ((0, 0), (0, 6), (0, 0)))
    factor = jnp.where(replay > 0, REPLAY_WEIGHT, 1.0).astype(F32)[:, :, None]
    whole, p_start, mv, all_extra = entry_call(w_start, moments, packed)
    p_start, mv = p_start.reshape(2, 48, 768), mv.reshape(2, 2, 48, 768)
    all_extra = all_extra.reshape(768, 128)
    pe_start = extra_rows(all_extra, 0)
    mve = jnp.stack([extra_rows(all_extra, 19), extra_rows(all_extra, 38)])
    p_now, pe_now = p_start, pe_start
    states = [state_in[0, :, 0], state_out[0, :, 0]]
    weights = [low_in, low_out]
    deltas = [(), ()]
    block_list = []
    grad_list = []
    for step in range(STEPS):
        blocks = whole.reshape(4, 768, 768)
        given = (tokens[step], out_grad[step], factor[step], ids[step], blocks, pe_now)
        send, frozen, *kept = front_call(*given)
        ret, frozen_res, rows, grad_rows, hidden, grad_hidden = trade_call(
            4 + step, send, frozen, weights[0], weights[1], frozen_in[0], frozen_out[0]
        )
        for index, (lhs, rhs) in enumerate(((rows, grad_hidden), (hidden, grad_rows))):
            grown = grow_call(
                STEP + step, RATES[4 + index], step == 0, lhs, rhs, weights[index], states[index], *deltas[index]
            )
            if step == 0:
                weights[index], states[index], delta = grown
                deltas[index] = (delta,)
            else:
                deltas[index] = grown
        if step == 1:
            summed = [
                lax.psum_scatter(deltas[0], "group", scatter_dimension=0, tiled=True),
                lax.psum_scatter(deltas[1], "group", scatter_dimension=1, tiled=True),
            ]
        block, grad, dense_grads, extra = back_call(*given, *kept, ret, frozen_res)
        block_list.append(block)
        grad_list.append(grad)
        dense_grads = dense_grads.reshape(WHOLE)
        if step == 0:
            whole, p_now, mv, pe_now, mve = renew_call(STEP, dense_grads, extra, p_now, mv, pe_now, mve)
        else:
            w_new, mom_new, delta_e = final_call(
                STEP + 1, dense_grads, extra, p_now, mv, pe_now, mve, p_start, pe_start,
                w_start, cols_and_square(mom_qkv, mom_proj),
            )
    at = 24 * (16 * lax.axis_index("dp") + lax.axis_index("expert"))
    mine = lax.dynamic_slice(delta_e, (0, at), (24, 24))
    new_params = []
    new_moms = []
    for delta, begin, moment in (
        (mine[17:19], gains, mom_gains),
        (mine[:17].T, router, mom_router),
        (summed[0].astype(F32)[None] * 0.25, exp_in, mom_in),
        (summed[1].astype(F32)[None] * 0.25, exp_out, mom_out),
    ):
        renewed = OUTER_MOMENTUM * moment + delta
        new_moms.append(renewed)
        new_params.append(begin - OUTER_RATE * (delta + OUTER_MOMENTUM * renewed))
    wide = lambda stack: jnp.concatenate([stack[0], stack[1], stack[2]], axis=1)
    return (
        jnp.stack(block_list),
        jnp.stack(grad_list),
        new_params[0],
        wide(w_new),
        w_new[3],
        new_params[1],
        new_params[2],
        new_params[3],
        new_moms[0],
        wide(mom_new),
        mom_new[3],
        new_moms[1],
        new_moms[2],
        new_moms[3],
    )


def solution(mesh):
    return jax.shard_map(
        body,
        mesh=mesh,
        in_specs=(
            P(None, ("group", "dp", "expert"), None),
            P(None, ("group", "dp", "expert"), None),
            P(None, ("group", "dp", "expert"), None),
            P(None, ("group", "dp", "expert")),
            P(),
            P(),
            P(None, ("dp", "expert")),
            P(("dp", "expert"), None),
            P(("dp", "expert"), None),
            P(("dp", "expert"), None),
            P("expert", "group", "dp"),
            P("expert", "dp", "group"),
            P(None, ("dp", "expert")),
            P(("dp", "expert"), None),
            P(("dp", "expert"), None),
            P(("dp", "expert"), None),
            P("expert", "group", "dp"),
            P("expert", "dp", "group"),
            P("group", None, None, ("dp", "expert")),
            P("group", None, ("dp", "expert"), None),
            P("group", None, ("dp", "expert"), None),
            P("group", None, ("dp", "expert"), None),
            P("group", None, "expert", None, "dp"),
            P("group", None, "expert", "dp", None),
        ),
        out_specs=(
            P(None, ("group", "dp", "expert"), None),
            P(None, ("group", "dp", "expert"), None),
            P(None, ("dp", "expert")),
            P(("dp", "expert"), None),
            P(("dp", "expert"), None),
            P(("dp", "expert"), None),
            P("expert", "group", "dp"),
            P("expert", "dp", "group"),
            P(None, ("dp", "expert")),
            P(("dp", "expert"), None),
            P(("dp", "expert"), None),
            P(("dp", "expert"), None),
            P("expert", "group", "dp"),
            P("expert", "dp", "group"),
        ),
        check_vma=False,
    )
```

```python
import functools

import jax
import jax.numpy as jnp
from jax import lax
from jax.experimental import pallas as pl
from jax.experimental.pallas import tpu as pltpu
from jax.sharding import PartitionSpec as P

MESH = pl.DeviceIdType.MESH
VMEM = pltpu.VMEM
F32 = jnp.float32
BF16 = jnp.bfloat16


class Links:
    def __init__(self, sends, recvs):
        self.sends, self.recvs, self.used, self.begun = sends, recvs, 0, []

    def send(self, src, dst, to):
        at = self.used
        self.used += 1
        copy = pltpu.make_async_remote_copy(
            src_ref=src, dst_ref=dst, send_sem=self.sends.at[at], recv_sem=self.recvs.at[at],
            device_id=to, device_id_type=MESH,
        )
        self.begun.append(copy)
        copy.start()
        return copy

    def finish(self):
        for copy in self.begun:
            copy.wait_send()


class Place:
    def __init__(self):
        self.g, self.d = lax.axis_index("group"), lax.axis_index("dp")
        e = lax.axis_index("expert")
        self.x, self.y = lax.div(e, 4), lax.rem(e, 4)

    def along_x(self, step, over=0):
        return {"dp": lax.rem(self.d + over, 2), "expert": lax.rem(self.x + step, 4) * 4 + self.y}

    def along_y(self, step, over=0):
        return {"dp": lax.rem(self.d + over, 2), "expert": self.x * 4 + lax.rem(self.y + step, 4)}

    def other_dp(self):
        return {"dp": 1 - self.d}

    def in_group(self, step):
        return {"group": lax.rem(self.g + step, 4)}

    def other_core(self):
        return {"group": self.g + 1 - 2 * lax.rem(self.g, 2)}


def hail(partners):
    barrier = pltpu.get_barrier_semaphore()
    for partner in partners:
        pl.semaphore_signal(barrier, inc=1, device_id=partner, device_id_type=MESH)


def await_hails(partners):
    pl.semaphore_wait(pltpu.get_barrier_semaphore(), len(partners))


PEERS = ((0, 1), (1, 0), (3, 0), (1, 1), (3, 1), (2, 0), (2, 1))


def ring_partners(place):
    return (
        [place.along_x(*peer) for peer in PEERS]
        + [place.along_y(step) for step in (1, 2, 3)]
        + [place.along_y(step, 1) for step in (1, 2, 3)]
    )


class Gather:
    def __init__(self, links, place, whole, h, p1, p2, near1, near2, at, share=None):
        self.links, self.whole, self.h, self.at, self.d, self.place = links, whole, h, at, place.d, place
        self.p1, self.p2, self.near1, self.near2, self.share = p1, p2, near1, near2, share
        self.shared = []

    def push(self, k1, k2, dp, to):
        c, x = self.at(lax.rem(k1, 4), lax.rem(k2, 4))
        ref = self.whole.at[c, slice(None) if dp is None else dp, x, self.h]
        return self.links.send(ref, ref, to)

    def give(self, k1, k2):
        if self.share is not None:
            self.shared.append(self.push(k1, k2, None, self.share))

    def start(self):
        p1, p2, d = self.p1, self.p2, self.d
        self.over_dp = self.push(p1, p2, d, self.place.other_dp())
        self.own = [self.push(p1, p2, d, self.near1(1)), self.push(p1, p2, d, self.near1(3))]

    def ring_one(self):
        p1, p2, d = self.p1, self.p2, self.d
        self.over_dp.wait_recv()
        self.own += [self.push(p1, p2, 1 - d, self.near1(1)), self.push(p1, p2, 1 - d, self.near1(3))]
        self.pushed = [(p1, self.push(p1, p2, None, self.near2(1)), self.push(p1, p2, None, self.near2(3)))]
        self.give(p1, p2)
        for copy in self.own:
            copy.wait_recv()
        self.passed = [self.push(p1 + 3, p2, 0, self.near1(1)), self.push(p1 + 1, p2, 1, self.near1(3))]
        for k1 in (p1 + 3, p1 + 1):
            self.pushed.append((k1, self.push(k1, p2, None, self.near2(1)), self.push(k1, p2, None, self.near2(3))))
            self.give(k1, p2)

    def ring_two(self):
        p1, p2 = self.p1, self.p2
        for copy in self.passed:
            copy.wait_recv()
        k1 = p1 + 2
        self.pushed.append((k1, self.push(k1, p2, None, self.near2(1)), self.push(k1, p2, None, self.near2(3))))
        self.give(k1, p2)
        self.last = []
        for k1, right, left in self.pushed:
            right.wait_recv()
            self.last.append((k1, self.push(k1, p2 + 3, 0, self.near2(1))))
            self.give(k1, p2 + 3)
            left.wait_recv()
            self.last.append((k1, self.push(k1, p2 + 1, 1, self.near2(3))))
            self.give(k1, p2 + 1)

    def end(self):
        for n, (k1, copy) in enumerate(self.last):
            copy.wait_recv()
            if n % 2:
                self.give(k1, self.p2 + 2)
        for copy in self.shared:
            copy.wait_recv()


def run_gather(parts):
    for stage in ("ring_one", "ring_two", "end"):
        for part in parts:
            getattr(part, stage)()


def gather_parts(links, place, whole):
    by_x = lambda kx, ky: (ky, kx)
    by_y = lambda ky, kx: (ky, kx)
    first = Gather(links, place, whole, 0, place.x, place.y, place.along_x, place.along_y, by_x)
    second = Gather(links, place, whole, 1, place.y, place.x, place.along_y, place.along_x, by_y)
    return first, second


class RingSum:
    def __init__(self, links, near1, near2, p1, p2, d, term, far, near, mid, box):
        self.links, self.near1, self.near2, self.p1, self.p2, self.d = links, near1, near2, p1, p2, d
        self.term, self.far, self.near, self.mid, self.box = term, far, near, mid, box
        self.steps = (2, 1, 3, 0)
        self.far_copies, self.direct, self.summed, self.over = [], [], [], []

    def get(self, k, dp, i):
        return self.term(lax.rem(self.p1 + k, 4), dp, lax.rem(self.p2 + self.steps[i], 4))

    def send_far(self, i):
        self.far_copies.append([
            self.links.send(self.get(2, 1, i), self.far.at[0, i], self.near1(1)),
            self.links.send(self.get(2, 0, i), self.far.at[1, i], self.near1(3)),
        ])

    def send_direct(self, i):
        self.direct.append([
            self.links.send(self.get(1, 0, i), self.near.at[0, 0, i], self.near1(1)),
            self.links.send(self.get(3, 1, i), self.near.at[1, 1, i], self.near1(3)),
        ])

    def middle(self, i):
        out = []
        for side, step, dp in ((0, 1, 1), (1, 3, 0)):
            self.far_copies[i][side].wait_recv()
            self.far[side, i] = (self.far[side, i].astype(F32) + self.get(step, dp, i)[...].astype(F32)).astype(BF16)
            out.append(self.links.send(self.far.at[side, i], self.near.at[side, dp, i], self.near1(step)))
        self.summed.append(out)

    def finish(self, i):
        for copy in self.direct[i] + self.summed[i]:
            copy.wait_recv()
        mine = self.d * 4 + self.p2
        for dp in range(2):
            self.mid[i, dp] = (
                self.get(0, dp, i)[...].astype(F32)
                + self.near[0, dp, i].astype(F32)
                + self.near[1, dp, i].astype(F32)
            ).astype(BF16)
        step = self.steps[i]
        for over in (0, 1):
            src = self.mid.at[i, lax.rem(self.d + over, 2)]
            if step or over:
                self.over.append(self.links.send(src, self.box.at[mine], self.near2(step, over)))
            else:
                self.box[mine] = self.mid[i, self.d]

    def total(self):
        for copy in self.over:
            copy.wait_recv()
        value = self.box[0].astype(F32)
        for k in range(1, 8):
            value = value + self.box[k].astype(F32)
        return value


def add_over(links, own, box, position, size, reach):
    box[position] = own
    copies = [links.send(box.at[position], box.at[position], reach(step)) for step in range(1, size)]

    def finish():
        for copy in copies:
            copy.wait_recv()
        total = box[0]
        for k in range(1, size):
            total = total + box[k]
        return total

    return finish


HALF_SCRATCH = [
    VMEM((2, 4, 48, 768), BF16), VMEM((2, 2, 4, 48, 768), BF16), VMEM((4, 2, 48, 768), BF16), VMEM((8, 48, 768), BF16)
]
REDUCE_SCRATCH = HALF_SCRATCH * 2 + [VMEM((4, 24, 768), F32), VMEM((4, 24, 768), F32), VMEM((2, 24, 768), F32)]
REDUCE_COPIES = 2 * (24 + 7) + 7
GATHER_COPIES = 2 * (1 + 4 + 2 + 8 + 8)


def reduce_all(links, place, grads, extra, scratch, between=None):
    box_x, box_y, box_z = scratch[8:]
    first = RingSum(
        links, place.along_y, place.along_x, place.y, place.x, place.d,
        lambda k, dp, j: grads.at[k, dp, j, 0], *scratch[:4],
    )
    second = RingSum(
        links, place.along_x, place.along_y, place.x, place.y, place.d,
        lambda k, dp, j: grads.at[j, dp, k, 1], *scratch[4:8],
    )
    parts = (first, second)
    for i in range(4):
        for part in parts:
            part.send_far(i)
    extra_x = add_over(links, extra, box_x, place.x, 4, place.along_x)
    for i in range(4):
        for part in parts:
            part.send_direct(i)
        for part in parts:
            part.middle(i)
        if between is not None:
            between(i)
        if i == 1:
            extra_y = add_over(links, extra_x(), box_y, place.y, 4, place.along_y)
        if i == 3:
            extra_z = add_over(links, extra_y(), box_z, place.d, 2, lambda step: place.other_dp())
    for i in range(4):
        for part in parts:
            part.finish(i)
    return [part.total() for part in parts], extra_z()


EPS_NORM = 1e-06
BETA_ONE = 0.9
BETA_TWO = 0.95
ADAM_EPS = 1e-08
DECAY = 0.1
OUTER_RATE = 0.7
OUTER_MOMENTUM = 0.9
REPLAY_WEIGHT = 0.25
RATES = (0.6, 0.04, 0.3, 0.03, 0.04, 0.02)
HEADS = 12
LEN = 128
STEPS = 2
STEP = 10


def entry_kernel(p_in, mv_in, e_in, whole, p_out, mv_out, pe_out, mve_out, e_out, p_box, mv_box, sends, recvs):
    place = Place()
    partners = ring_partners(place) + [place.other_core()]
    hail(partners)
    await_hails(partners)
    links = Links(sends, recvs)
    x, y, d = place.x, place.y, place.d
    h = lax.rem(place.g, 2)
    masters = [links.send(p_in.at[lax.rem(y + k, 4)], p_box.at[y], place.along_y(k)) for k in (1, 2, 3)]
    e_out[d, x, y] = e_in[...]
    mine = e_out.at[d, x, y]
    extra_z = links.send(mine, mine, place.other_dp())
    p_box[y] = p_in[y]
    mv_box[y] = mv_in[y]
    for copy in masters:
        copy.wait_recv()
    folded = p_box[...].astype(F32)
    master = jnp.concatenate([folded[:, :24], folded[:, 24:]], axis=2).reshape(2, 48, 768)
    p_out[...] = master

    @pl.when(h == 0)
    def _():
        whole[y, d, x, 0] = master[0].astype(BF16)

    @pl.when(h == 1)
    def _():
        whole[y, d, x, 1] = master[1].astype(BF16)

    def mix(a, b):
        return a * (1 - h) + b * h

    def near1(step, over=0):
        one, two = place.along_x(step, over), place.along_y(step, over)
        return {"dp": one["dp"], "expert": mix(one["expert"], two["expert"])}

    def near2(step):
        one, two = place.along_y(step), place.along_x(step)
        return {"dp": one["dp"], "expert": mix(one["expert"], two["expert"])}

    def at(k1, k2):
        return mix(k2, k1), mix(k1, k2)

    part = Gather(links, place, whole, h, mix(x, y), mix(y, x), near1, near2, at, place.other_core())
    part.start()
    extra_z.wait_recv()
    mine = e_out.at[:, x, y]
    extra_x = [links.send(mine, mine, place.along_x(k)) for k in (1, 2, 3)]
    part.ring_one()
    for copy in extra_x:
        copy.wait_recv()
    mine = e_out.at[:, :, y]
    extra_y = [links.send(mine, mine, place.along_y(k)) for k in (1, 2, 3)]
    part.ring_two()
    moments = [links.send(mv_in.at[lax.rem(y + k, 4)], mv_box.at[y], place.along_y(k)) for k in (1, 2, 3)]
    for copy in extra_y:
        copy.wait_recv()
    turned = e_out[...].reshape(768, 128).T
    pe_out[...] = turned[:24]
    mve_out[0] = turned[24:48]
    mve_out[1] = turned[48:72]
    part.end()
    for copy in moments:
        copy.wait_recv()
    moment = mv_box[...].astype(F32)
    for k in range(2):
        mv_out[k] = moment[:, 24 * k : 24 * k + 24].reshape(2, 48, 768)
    links.finish()


def adam_values(master, first, second, grad, rate, number):
    first = BETA_ONE * first + (1.0 - BETA_ONE) * grad
    second = BETA_TWO * second + (1.0 - BETA_TWO) * grad * grad
    level = second * (1.0 / (1.0 - BETA_TWO**number))
    below = level * lax.rsqrt(jnp.maximum(level, 1e-30)) + ADAM_EPS
    guess = pl.reciprocal(below, approx=True)
    update = first * ((1.0 / (1.0 - BETA_ONE**number)) * rate) * (guess * (2.0 - below * guess))
    return master - (update + (rate * DECAY) * master), first, second


def block_rate(place):
    return jnp.where(place.y == 3, RATES[2], RATES[1]).astype(F32)


def extra_rates():
    row = lax.broadcasted_iota(jnp.int32, (24, 768), 0)
    return jnp.where(row < 17, RATES[3], RATES[0]).astype(F32)


def renew_part(number, place, links, grads, extra, scratch, p_in, mv_in, pe_in, mve_in,
               whole, p_out, mv_out, pe_out, mve_out):
    sums, total = reduce_all(links, place, grads, extra, scratch)
    parts = gather_parts(links, place, whole)
    for h, part in enumerate(parts):
        fresh, first, second = adam_values(p_in[h], mv_in[0, h], mv_in[1, h], sums[h], block_rate(place), number)
        whole[place.y, place.d, place.x, h] = fresh.astype(BF16)
        part.start()
        p_out[h] = fresh
        mv_out[0, h] = first
        mv_out[1, h] = second
    pe_out[...], mve_out[0], mve_out[1] = adam_values(pe_in[...], mve_in[0], mve_in[1], total, extra_rates(), number)
    run_gather(parts)


def outer(begin, moment, mean):
    renewed = OUTER_MOMENTUM * moment + mean
    return begin - OUTER_RATE * (mean + OUTER_MOMENTUM * renewed), renewed


def own_features(place, rows, turned):
    at = 24 * (16 * place.d + 4 * place.x + place.y)
    pick = (lax.broadcasted_iota(jnp.int32, (768, 24), 0) == at + lax.broadcasted_iota(jnp.int32, (768, 24), 1)).astype(BF16)
    total = 0.0
    for _ in range(3):
        part = rows.astype(BF16)
        total = total + (
            lax.dot_general(pick, part, (((0,), (1,)), ((), ())), preferred_element_type=F32) if turned
            else lax.dot_general(part, pick, (((1,), (0,)), ((), ())), preferred_element_type=F32)
        )
        rows = rows - part.astype(F32)
    return total


class ExpertMean:
    def __init__(self, links, place, copies, deltas, own, other, sent, far):
        self.links, self.place, self.deltas = links, place, deltas
        self.own, self.other, self.sent, self.far = own, other, sent, far
        self.core, self.high = lax.rem(place.g, 2), lax.div(place.g, 2)
        self.loads = [copies.start(delta.at[:, self.core], own.at[k]) for k, delta in enumerate(deltas)]

    def start(self):
        self.first = [
            self.links.send(delta.at[:, 1 - self.core], self.other.at[k], self.place.other_core())
            for k, delta in enumerate(self.deltas)
        ]

    def middle(self, k):
        self.loads[k].wait()
        self.first[k].wait_recv()
        self.sent[k] = (
            self.own[k, 1 - self.high].astype(F32) + self.other[k, 1 - self.high].astype(F32)
        ).astype(BF16)
        self.second = getattr(self, "second", [])
        self.second.append(self.links.send(self.sent.at[k], self.far.at[k], self.place.in_group(2)))

    def mean(self, k):
        self.second[k].wait_recv()
        mine = self.own[k, self.high].astype(F32) + self.other[k, self.high].astype(F32)
        return (mine + self.far[k].astype(F32)) * 0.25


def final_part(number, place, links, grads, extra, scratch, experts, p_in, mv_in, pe_in, mve_in, p_start, pe_start,
               turned, flat_out, turned_out, delta, quarters, whole, boxes):
    g, y = place.g, place.y

    def between(i):
        if i >= 2:
            experts.middle(i - 2)

    sums, total = reduce_all(links, place, grads, extra, scratch, between)
    for h in range(2):
        fresh, _, _ = adam_values(p_in[h], mv_in[0, h], mv_in[1, h], sums[h], block_rate(place), number)
        delta[2 * h : 2 * h + 2] = (p_start[h] - fresh).reshape(2, 24, 768)
    summed = [
        links.send(delta.at[lax.rem(g + k, 4)], quarters.at[g], place.in_group(k)) for k in (1, 2, 3)
    ]
    fresh_e, _, _ = adam_values(pe_in[...], mve_in[0], mve_in[1], total, extra_rates(), number)
    sum_e = add_over(links, pe_start[...] - fresh_e, boxes, g, 4, place.in_group)
    quarters[g] = delta[g]
    for copy in summed:
        copy.wait_recv()
    whole[g] = (quarters[0] + quarters[1] + quarters[2] + quarters[3]) * 0.25
    spread = [links.send(whole.at[g], whole.at[g], place.in_group(k)) for k in (1, 2, 3)]
    mean_e = sum_e() * 0.25
    flat_out[...] = own_features(place, mean_e, False)
    turned_out[...] = own_features(place, mean_e, True)
    for copy in spread:
        copy.wait_recv()
    turned[y] = whole[y]
    across = [links.send(whole.at[lax.rem(y + k, 4)], turned.at[y], place.along_y(k)) for k in (1, 2, 3)]
    for copy in across:
        copy.wait_recv()


def semaphores(count):
    return [pltpu.SemaphoreType.DMA((count,)), pltpu.SemaphoreType.DMA((count,))]


ANY = pl.ANY
WHOLE = (4, 2, 4, 2, 48, 768)
BLOCK = (2, 48, 768)
ROW = (128, 768)


def call(kernel, outs, scratch, collective_id, args, limit=60 << 20):
    return pl.pallas_call(
        kernel,
        out_shape=tuple(jax.ShapeDtypeStruct(shape, kind) for _, shape, kind in outs),
        in_specs=[pl.BlockSpec(memory_space=space) for space, _ in args],
        out_specs=tuple(pl.BlockSpec(memory_space=space) for space, _, _ in outs),
        scratch_shapes=scratch,
        compiler_params=pltpu.CompilerParams(
            collective_id=collective_id, has_side_effects=True, vmem_limit_bytes=limit
        ),
    )(*(array for _, array in args))


def entry_call(p_in, mv_in, e_in):
    return call(
        entry_kernel,
        [(VMEM, WHOLE, BF16), (VMEM, BLOCK, F32), (VMEM, (2, *BLOCK), F32), (VMEM, (24, 768), F32),
         (VMEM, (2, 24, 768), F32)],
        [VMEM((2, 4, 4, 24, 128), F32), VMEM((4, 48, 384), BF16), VMEM((4, 48, 768), BF16)]
        + semaphores(3 + 7 + 23 + 3 + 16), 1,
        [(VMEM, p_in), (VMEM, mv_in), (VMEM, e_in)],
    )

CAP = 24
TOK = 128
DIMS = {"nn": (((1,), (0,)), ((), ())), "nt": (((1,), (1,)), ((), ())), "tn": (((0,), (0,)), ((), ()))}


def mm(a, b, form="nn"):
    return lax.dot_general(a, b, DIMS[form], preferred_element_type=F32)


def split_low(values):
    high = values.astype(BF16)
    return high, (values - high.astype(F32)).astype(BF16)


def row_scale(values):
    return lax.rsqrt(jnp.mean(values * values, axis=-1, keepdims=True) + EPS_NORM)


def iota(shape, dim):
    return lax.broadcasted_iota(jnp.int32, shape, dim)


def routing(ids):
    names = [(iota((24, TOK), 0) == ids[k : k + 1]).astype(F32) for k in range(2)]
    either = names[0] + names[1]
    earlier = (iota((TOK, TOK), 0) < iota((TOK, TOK), 1)).astype(BF16)
    slot = mm(either.astype(BF16), earlier).astype(jnp.int32)
    taken = jnp.where(iota((17, CAP, TOK), 1) == slot[:17][:, None, :], 1.0, 0.0)
    return names, taken * either[:17][:, None, :]


def pair_stack(part):
    lane = iota(part.shape, 1)
    zero = jnp.zeros_like(part)
    return jnp.concatenate([jnp.where(lane < 64, part, zero), jnp.where(lane < 64, zero, part)], axis=0)


def side_by_side(stacked):
    return jnp.concatenate([stacked[:TOK], stacked[TOK:]], axis=1)


def flat(whole, c):
    return whole[c].reshape(768, 768)


def cotangent(og_ref, ids_ref):
    factor = jnp.where(ids_ref[2:3] > 0, REPLAY_WEIGHT, 1.0)
    spread = jnp.where(iota((TOK, TOK), 0) == iota((TOK, TOK), 1), factor, 0.0).astype(BF16)
    return mm(spread, og_ref[...])


def front_part(x_ref, og_ref, ids_ref, pe_ref, whole,
               send, frozen, qkv_out, probs_out, mixed_out, middle_out, a1_out, a2_out, weights_out):
    gain = pe_ref[16:24].astype(BF16).astype(F32)
    x = x_ref[...].astype(F32)
    a1 = (x * row_scale(x) * gain[1:2]).astype(BF16)
    a1_out[...] = a1
    for c in range(3):
        qkv_out[c] = mm(a1, flat(whole, c)).astype(BF16)
    row, col = iota((2 * TOK, TOK), 0), iota((2 * TOK, TOK), 1)
    causal = lax.rem(row, TOK) >= col
    for pair in range(6):
        lanes = slice(128 * pair, 128 * pair + 128)
        scores = mm(pair_stack(qkv_out[0, :, lanes]), qkv_out[1, :, lanes], "nt") * 0.125
        scores = jnp.where(causal, scores, -1e30)
        expo = jnp.exp(scores - jnp.max(scores, axis=-1, keepdims=True))
        probs = expo / jnp.sum(expo, axis=-1, keepdims=True)
        probs_out[pair] = probs
        mixed_out[:, lanes] = mm(side_by_side(probs.astype(BF16)), pair_stack(qkv_out[2, :, lanes])).astype(BF16)
    middle = x + mm(mixed_out[...], flat(whole, 3))
    middle_out[...] = middle
    a2 = (middle * row_scale(middle) * gain[2:3]).astype(BF16)
    a2_out[...] = a2
    logits = mm(pe_ref[...].astype(BF16), a2, "nt")
    names, taken = routing(ids_ref[...])
    picked = [jnp.sum(name * logits, axis=0, keepdims=True) for name in names]
    top = jnp.maximum(picked[0], picked[1])
    expo = [jnp.exp(z - top) for z in picked]
    whole_sum = expo[0] + expo[1]
    weights = [e / whole_sum for e in expo]
    weights_out[...] = jnp.concatenate(weights + [jnp.zeros((6, TOK), F32)], axis=0)
    by_expert = names[0] * weights[0] + names[1] * weights[1]
    row_weight = jnp.sum(taken * by_expert[:17][:, None, :], axis=-1, keepdims=True)
    cot = cotangent(og_ref, ids_ref).astype(BF16)
    low = taken.astype(BF16).reshape(17 * CAP, TOK)
    rows = mm(low, a2).reshape(17, CAP, 768)
    grads = mm(low, cot).reshape(17, CAP, 768) * row_weight
    both = jnp.concatenate([rows, grads], axis=1).astype(BF16)
    frozen[...] = both[0]
    send[...] = both[1:]


def back_part(x_ref, og_ref, ids_ref, pe_ref, whole, qkv, probs_ref, mixed, middle_ref, a1, a2,
              weights_ref, ret, frozen, block_out, grad_out, grads, arrived):
    gain = pe_ref[16:24].astype(BF16).astype(F32)
    low_rows = pe_ref[...].astype(BF16)
    cot = cotangent(og_ref, ids_ref)
    names, taken = routing(ids_ref[...])
    weights = [weights_ref[k : k + 1] for k in range(2)]
    by_expert = names[0] * weights[0] + names[1] * weights[1]
    row_weight = jnp.sum(taken * by_expert[:17][:, None, :], axis=-1, keepdims=True)
    low = taken.astype(BF16).reshape(17 * CAP, TOK)
    both = ret[...].astype(F32)
    both = jnp.concatenate([frozen[...][None], both], axis=0)
    results, back = both[:, :CAP], both[:, CAP:].reshape(17 * CAP, 768)
    high, rest = split_low((results * row_weight).reshape(17 * CAP, 768))
    middle = middle_ref[...]
    block_out[...] = (middle + mm(low, high, "tn") + mm(low, rest, "tn")).astype(BF16)
    cot_rows = mm(low, cot.astype(BF16)).reshape(17, CAP, 768)
    grad_row = jnp.sum(cot_rows * results, axis=-1, keepdims=True)
    by_name = jnp.concatenate([jnp.sum(taken * grad_row, axis=1), jnp.zeros((7, TOK), F32)], axis=0)
    grad_w = [jnp.sum(name * by_name, axis=0, keepdims=True) for name in names]
    mean = weights[0] * grad_w[0] + weights[1] * grad_w[1]
    grad_logits = sum(names[k] * (weights[k] * (grad_w[k] - mean)) for k in range(2))
    high, rest = split_low(grad_logits)
    grad_router = mm(high, a2[...]) + mm(rest, a2[...])
    da2 = mm(high, low_rows, "tn") + mm(rest, low_rows, "tn")
    high, rest = split_low(back)
    da2 = da2 + mm(low, high, "tn") + mm(low, rest, "tn")
    scale = row_scale(middle)
    normed = middle * scale
    dg2 = jnp.sum(normed * da2, axis=0, keepdims=True)
    into = da2 * gain[2:3]
    dmiddle = cot + scale * (into - normed * jnp.mean(into * normed, axis=-1, keepdims=True))
    branch = dmiddle.astype(BF16)
    arrived()
    grads[3] = mm(mixed[...], branch, "tn").astype(BF16).reshape(2, 4, 2, 48, 768)
    dmixed = mm(branch, flat(whole, 3), "nt").astype(BF16)
    da1 = jnp.zeros((TOK, 768), F32)
    parts = [[], [], []]
    for pair in range(6):
        lanes = slice(128 * pair, 128 * pair + 128)
        probs = probs_ref[pair]
        dms = pair_stack(dmixed[:, lanes])
        parts[2].append(mm(probs.astype(BF16), dms, "tn").astype(BF16))
        dpb = mm(dms, qkv[2, :, lanes], "nt")
        ds = (probs * (dpb - jnp.sum(probs * dpb, axis=-1, keepdims=True))).astype(BF16)
        parts[0].append((mm(side_by_side(ds), pair_stack(qkv[1, :, lanes])) * 0.125).astype(BF16))
        parts[1].append((mm(ds, pair_stack(qkv[0, :, lanes]), "tn") * 0.125).astype(BF16))
    for c in range(3):
        dqkv = jnp.concatenate(parts[c], axis=1)
        grads[c] = mm(a1[...], dqkv, "tn").astype(BF16).reshape(2, 4, 2, 48, 768)
        da1 = da1 + mm(dqkv, flat(whole, c), "nt")
    x = x_ref[...].astype(F32)
    scale = row_scale(x)
    normed = x * scale
    dg1 = jnp.sum(normed * da1, axis=0, keepdims=True)
    into = da1 * gain[1:2]
    grad_out[...] = dmiddle + scale * (into - normed * jnp.mean(into * normed, axis=-1, keepdims=True))
    return jnp.concatenate([grad_router[:17], dg1, dg2, jnp.zeros((5, 768), F32)], axis=0)


SQRT_HALF = 0.7071067811865476
DENSITY = 0.3989422804014327


def expert_rows(rows, grad, first, second, turned):
    u = mm(rows, first)
    chance = 0.5 + 0.5 * lax.erf(u * SQRT_HALF)
    h = (u * chance).astype(BF16)
    value = mm(h, second, "nt" if turned else "nn")
    slope = chance + u * (jnp.exp(u * u * -0.5) * DENSITY)
    du = (slope * mm(grad, second, "nn" if turned else "nt")).astype(BF16)
    return value, mm(du, first, "nt"), h, du


class Copies:
    def __init__(self, sems):
        self.sems, self.used = sems, 0

    def start(self, src, dst):
        copy = pltpu.make_async_copy(src, dst, self.sems.at[self.used])
        self.used += 1
        copy.start()
        return copy


def grow_experts(first_step, number, copies, rows, grad, h, du, w1, w2, mv1, mv2, starts, news, bufs, between):
    (mv1_buf, mv2_buf, d1_buf, d2_buf, w1_out, w2_out, mv1_out, mv2_out, d1_out, d2_out) = bufs
    tiles = [(0, t) for t in range(6)] + [(1, t) for t in range(6)]

    def cut(which, t):
        return (pl.ds(128 * t, 128), slice(None)) if which == 0 else (slice(None), pl.ds(256 * t, 256))

    def load(n):
        which, t = tiles[n]
        slot = n % 2
        mv, buf = ((mv1, mv1_buf), (mv2, mv2_buf))[which]
        size = (128, 256)[which]
        begun = [copies.start(mv.at[:, pl.ds(size * t, size)], buf.at[slot])]
        if not first_step:
            begun.append(copies.start(starts[which].at[cut(which, t)], (d1_buf, d2_buf)[which].at[slot]))
        return begun

    loads = {0: load(0)}
    stores = {}
    for n, (which, t) in enumerate(tiles):
        slot = n % 2
        if n + 1 < len(tiles):
            loads[n + 1] = load(n + 1)
        for copy in loads[n]:
            copy.wait()
        for copy in stores.get(n - 2, []):
            copy.wait()
        if which == 0:
            value = mm(rows[:, 128 * t : 128 * t + 128], du[...], "tn")
            begin = w1[128 * t : 128 * t + 128].astype(F32)
            moments = mv1_buf
        else:
            value = mm(h[:, 256 * t : 256 * t + 256], grad[...], "tn")
            begin = w2[:, 256 * t : 256 * t + 256].T.astype(F32)
            moments = mv2_buf
        fresh, first, second = adam_values(
            begin, moments[slot, 0].astype(F32), moments[slot, 1].astype(F32), value, RATES[4 + which], number
        )
        here = cut(which, t)
        if first_step:
            low, mv_low = (w1_out, w2_out)[which], (mv1_out, mv2_out)[which]
            low[slot] = fresh.astype(BF16) if which == 0 else fresh.astype(BF16).T
            mv_low[slot, 0] = first.astype(BF16)
            mv_low[slot, 1] = second.astype(BF16)
            size = (128, 256)[which]
            stores[n] = [
                copies.start(low.at[slot], news[which].at[here]),
                copies.start(mv_low.at[slot], news[2 + which].at[:, pl.ds(size * t, size)]),
            ]
        else:
            change = (begin - fresh).astype(BF16)
            since = (d1_buf, d2_buf)[which][slot].astype(F32) - (w1, w2)[which][here].astype(F32)
            out = (d1_out, d2_out)[which]
            out[slot] = (since + (change if which == 0 else change.T).astype(F32)).astype(BF16)
            stores[n] = [copies.start(out.at[slot], news[which].at[here])]
        between(n)
    return stores[len(tiles) - 2] + stores[len(tiles) - 1]


KEPT = [((3, *ROW), BF16), ((6, 256, 128), F32), (ROW, BF16), (ROW, F32), (ROW, BF16), (ROW, BF16), ((8, 128), F32)]


def trade_kernel(first_step, number, *refs):
    (x, og, ids, pe, whole_hbm, both_hbm), refs = refs[:6], refs[6:]
    step = 0 if first_step else 1
    x, og, ids = x.at[step], og.at[step], ids.at[step]
    starts = [both_hbm.at[:, :1536], both_hbm.at[:, 1536:]]
    if first_step:
        w1_hbm, w2_hbm = starts
    else:
        (w1_hbm, w2_hbm), refs = refs[:2], refs[2:]
    (fin_hbm, fout_hbm, mv1, mv2), refs = refs[:4], refs[4:]
    kept_out, refs = refs[:7], refs[7:]
    ret, frozen_out, refs = refs[0], refs[1], refs[2:]
    count = 4 if first_step else 2
    news, refs = refs[:count], refs[count:]
    kept, refs = refs[:7], refs[7:]
    (whole, w1, w2, fin, fout, send, frozen_in, recv, ans, zret, home, rows_all, grad_all, h_all, du_all, local_sems,
     in_send, in_recv, z_send, z_recv, zb_send, zb_recv, home_send, home_recv), bufs = refs[:24], refs[24:]
    copies = Copies(local_sems)
    loads = [
        copies.start(src, dst)
        for src, dst in ((whole_hbm, whole), (w1_hbm, w1), (w2_hbm, w2), (fin_hbm, fin), (fout_hbm, fout))
    ]
    d, e = lax.axis_index("dp"), lax.axis_index("expert")
    partner = {"dp": 1 - d}

    def ahead(k):
        return lax.rem(e + k, 16)

    def behind(k):
        return lax.rem(e + 16 - k, 16)

    barrier = pltpu.get_barrier_semaphore()

    @pl.loop(1, 16)
    def _(k):
        pl.semaphore_signal(barrier, inc=1, device_id={"expert": ahead(k)}, device_id_type=MESH)

    pl.semaphore_signal(barrier, inc=1, device_id=partner, device_id_type=MESH)
    loads[0].wait()
    front_part(x, og, ids, pe, whole, send, frozen_in, *kept)
    pl.semaphore_wait(barrier, 16)

    def remote(src, dst, sends, recvs, k, to):
        return pltpu.make_async_remote_copy(
            src_ref=src, dst_ref=dst, send_sem=sends.at[k], recv_sem=recvs.at[k], device_id=to, device_id_type=MESH
        )

    def to_expert(k):
        return remote(send.at[ahead(k)], recv.at[0, e], in_send, in_recv, k, {"expert": ahead(k)})

    def to_partner(k):
        return remote(recv.at[0, behind(k)], recv.at[1, behind(k)], z_send, z_recv, k, partner)

    def from_partner(k):
        return remote(ans.at[1, behind(k)], zret.at[behind(k)], zb_send, zb_recv, k, partner)

    def to_home(k):
        return remote(home.at[behind(k)], ret.at[e], home_send, home_recv, k, {"expert": behind(k)})

    @pl.loop(1, 16)
    def _(k):
        to_expert(k).start()

    recv[0, e] = send[e]
    to_partner(0).start()
    keeps = [copies.start(src, dst) for src, dst in zip(kept, kept_out)]

    @pl.loop(1, 16)
    def _(k):
        to_expert(k).wait_recv()
        to_partner(k).start()

    for copy in loads[1:3]:
        copy.wait()

    @pl.loop(0, 4)
    def _(j):
        other = lax.rem(lax.div(j + 1, 2) + 1, 2)
        half = lax.div(j, 2)

        @pl.when(other == 1)
        def _():
            @pl.loop(0, 8)
            def _(i):
                to_partner(half * 8 + i).wait_recv()

        blocks = [recv[other, behind(half * 8 + i)].astype(F32) for i in range(8)]
        rows = jnp.concatenate([b[:CAP] for b in blocks], axis=0).astype(BF16)
        grad = jnp.concatenate([b[CAP:] for b in blocks], axis=0).astype(BF16)
        value, back, h, du = expert_rows(rows, grad, w1[...], w2[...], True)
        at = pl.ds(pl.multiple_of(j * 192, 192), 192)
        rows_all[at] = rows
        grad_all[at] = grad
        h_all[at] = h
        du_all[at] = du
        for i in range(8):
            part = slice(i * CAP, (i + 1) * CAP)
            ans[other, behind(half * 8 + i)] = jnp.concatenate([value[part], back[part]], axis=0).astype(BF16)

        @pl.when(other == 1)
        def _():
            @pl.loop(0, 8)
            def _(i):
                from_partner(half * 8 + i).start()

    for copy in loads[3:]:
        copy.wait()
    both = frozen_in[...].astype(F32)
    value, back, _, _ = expert_rows(both[:CAP].astype(BF16), both[CAP:].astype(BF16), fin[...], fout[...], False)
    frozen_out[...] = jnp.concatenate([value, back], axis=0)

    def serve(k):
        from_partner(k).wait_recv()
        slot = behind(k)
        total = (ans[0, slot].astype(F32) + zret[slot].astype(F32)).astype(BF16)
        if k == 0:
            ret[e] = total
        else:
            home[slot] = total
            to_home(k).start()

    def between(n):
        for k in range(SERVED[n], SERVED[n + 1]):
            serve(k)

    for k in range(SERVED[0]):
        serve(k)
    left = grow_experts(
        first_step, number, copies, rows_all, grad_all, h_all, du_all, w1, w2, mv1, mv2, starts, news, bufs, between
    )

    @pl.loop(1, 16)
    def _(k):
        to_home(k).wait_recv()
        to_home(k).wait_send()
        to_expert(k).wait_send()

    @pl.loop(0, 16)
    def _(k):
        to_partner(k).wait_send()
        from_partner(k).wait_send()

    for copy in left + keeps:
        copy.wait()


SERVED = (5, 6, 7, 9, 10, 11, 12, 13, 15, 16, 16, 16, 16)


def trade_call(first_step, number, collective_id, small, *large):
    wide = (768, 1536)
    moment_kind = F32 if first_step else BF16
    news = [(ANY, wide, BF16)] * 2 + ([(ANY, (2, 768, 1536), BF16), (ANY, (2, 1536, 768), BF16)] if first_step else [])
    outs = [(ANY, *k) for k in KEPT] + [(VMEM, (16, 48, 768), BF16), (VMEM, (48, 768), F32)] + news
    t1, t2, c1, c2 = (2, 2, 128, 1536), (2, 2, 256, 768), (2, 128, 1536), (2, 768, 256)
    none = (8, 128)
    first = first_step
    bufs = [
        VMEM(t1, moment_kind), VMEM(t2, moment_kind),
        VMEM(none if first else c1, BF16), VMEM(none if first else c2, BF16),
        VMEM(c1 if first else none, BF16), VMEM(c2 if first else none, BF16),
        VMEM(t1 if first else none, BF16), VMEM(t2 if first else none, BF16),
        VMEM(none if first else c1, BF16), VMEM(none if first else c2, BF16),
    ]
    plane = (16, 48, 768)
    scratch = [VMEM(*k) for k in KEPT] + [
        VMEM(WHOLE, BF16), VMEM(wide, BF16), VMEM(wide, BF16), VMEM((768, 3072), BF16), VMEM((3072, 768), BF16),
        VMEM(plane, BF16), VMEM((48, 768), BF16), VMEM((2, *plane), BF16), VMEM((2, *plane), BF16),
        VMEM(plane, BF16), VMEM(plane, BF16),
        VMEM((768, 768), BF16), VMEM((768, 768), BF16), VMEM(wide, BF16), VMEM(wide, BF16),
        pltpu.SemaphoreType.DMA((72,)),
    ] + semaphores(16) * 4 + bufs
    args = [(VMEM, a) for a in small] + [(ANY, a) for a in large]
    return call(functools.partial(trade_kernel, first_step, number), outs, scratch, collective_id, args)


FETCHED = (0, 1, 2, 4)


def back_body(step, refs, scratch, copies, block_out, grad_out, grads, begin):
    (x, og, ids, pe), whole_hbm, kept, ret, frozen = refs[:4], refs[4], list(refs[5:12]), refs[12], refs[13]
    whole, buffers = scratch[0], scratch[1:5]
    loads = [copies.start(whole_hbm, whole)]
    for at, buffer in zip(FETCHED, buffers):
        loads.append(copies.start(kept[at], buffer))
        kept[at] = buffer

    def arrived():
        begin()
        for copy in loads:
            copy.wait()

    return back_part(
        x.at[step], og.at[step], ids.at[step], pe, whole, *kept, ret, frozen, block_out, grad_out, grads, arrived
    )


BACK_SCRATCH = [VMEM(WHOLE, BF16)] + [VMEM(*KEPT[at]) for at in FETCHED] + [VMEM(WHOLE, BF16), pltpu.SemaphoreType.DMA((16,))]


def renew_kernel(number, *refs):
    shared, (p_in, mv_in, pe_in, mve_in), refs = refs[:14], refs[14:18], refs[18:]
    (block_out, grad_out, whole, p_out, mv_out, pe_out, mve_out), refs = refs[:7], refs[7:]
    back_scratch, (grads, sems), refs = refs[:5], refs[5:7], refs[7:]
    scratch, (sends, recvs) = refs[:11], refs[11:]
    place = Place()
    partners = ring_partners(place)
    hail(partners)
    extra = back_body(
        0, shared, back_scratch, Copies(sems), block_out, grad_out, grads, lambda: await_hails(partners)
    )
    links = Links(sends, recvs)
    renew_part(number, place, links, grads, extra, scratch, p_in, mv_in, pe_in, mve_in,
               whole, p_out, mv_out, pe_out, mve_out)
    links.finish()


def final_kernel(number, *refs):
    shared, dense, refs = refs[:14], refs[14:20], refs[20:]
    deltas, refs = refs[:2], refs[2:]
    (block_out, grad_out, mean_out, flat_out, turned_out, expert_out), refs = refs[:6], refs[6:]
    back_scratch, (grads, sems), refs = refs[:5], refs[5:7], refs[7:]
    scratch, boxes, refs = refs[:11], refs[11:15], refs[15:]
    expert_scratch, (sends, recvs) = refs[:4], refs[4:]
    place = Place()
    partners = ring_partners(place) + [place.in_group(k) for k in (1, 2, 3)]
    hail(partners)
    copies, links = Copies(sems), Links(sends, recvs)
    experts = ExpertMean(links, place, copies, deltas, *expert_scratch)

    def begin():
        await_hails(partners)
        experts.start()

    extra = back_body(1, shared, back_scratch, copies, block_out, grad_out, grads, begin)
    final_part(
        number, place, links, grads, extra, scratch, experts, *dense, mean_out, flat_out, turned_out, *boxes
    )
    for k in range(2):
        expert_out[k] = experts.mean(k)
    links.finish()


def finish_kernel(*refs):
    given, refs = refs[:16], refs[16:]
    olds, refs = refs[:4], refs[4:]
    (block, grad, new_qkv, new_proj, new_mom_qkv, new_mom_proj, new_gains, new_router, new_mom_gains, new_mom_router,
     *news), (old_buf, new_buf, sems, *held) = refs[:14], refs[14:]
    copies = Copies(sems)
    rows = [copies.start(src, dst) for src, dst in zip(given, held)]
    loads = [copies.start(src, old_buf.at[n]) for n, src in enumerate(olds)]
    for copy in rows:
        copy.wait()
    (block0, block1, grad0, grad1, mean, flat_e, turned_e, experts,
     w_qkv, w_proj, mom_qkv, mom_proj, gains, router, mom_gains, mom_router) = held
    stores = []
    for k in range(2):
        for copy in loads[2 * k : 2 * k + 2]:
            copy.wait()
        new_buf[2 * k], new_buf[2 * k + 1] = outer(old_buf[2 * k], old_buf[2 * k + 1], experts[k])
        stores += [copies.start(new_buf.at[n], news[n]) for n in (2 * k, 2 * k + 1)]
    for n, (one, all_rows) in enumerate(((block0, block), (block1, block), (grad0, grad), (grad1, grad))):
        all_rows[n % 2] = one[...]
    new_gains[...], new_mom_gains[...] = outer(gains[...], mom_gains[...], flat_e[17:19])
    new_router[...], new_mom_router[...] = outer(router[...], mom_router[...], turned_e[:, :17])
    for c in range(3):
        lanes = slice(768 * c, 768 * c + 768)
        new_qkv[:, lanes], new_mom_qkv[:, lanes] = outer(w_qkv[:, lanes], mom_qkv[:, lanes], mean[c])
    new_proj[...], new_mom_proj[...] = outer(w_proj[...], mom_proj[...], mean[3])
    for copy in stores:
        copy.wait()


def finish_call(small, olds):
    part = (192, 1536)
    outs = [((2, *ROW), BF16), ((2, *ROW), F32), ((24, 2304), F32), ((24, 768), F32), ((24, 2304), F32), ((24, 768), F32),
            ((2, 24), F32), ((24, 17), F32), ((2, 24), F32), ((24, 17), F32)]
    return pl.pallas_call(
        finish_kernel,
        out_shape=tuple(jax.ShapeDtypeStruct(*out) for out in outs + [(part, F32)] * 4),
        in_specs=[pl.BlockSpec(memory_space=ANY)] * (len(small) + 4),
        out_specs=tuple([pl.BlockSpec(memory_space=VMEM)] * 10 + [pl.BlockSpec(memory_space=ANY)] * 4),
        scratch_shapes=[VMEM((4, *part), F32), VMEM((4, *part), F32), pltpu.SemaphoreType.DMA((24,))]
        + [VMEM(array.shape, array.dtype) for array in small],
        compiler_params=pltpu.CompilerParams(vmem_limit_bytes=60 << 20),
    )(*small, *olds)


def back_args(small, whole, kept, ret, frozen):
    args = [(VMEM, a) for a in small] + [(ANY, whole)]
    args += [(ANY if at in FETCHED else VMEM, a) for at, a in enumerate(kept)]
    return args + [(VMEM, ret), (VMEM, frozen)]


def renew_call(number, shared, *args):
    return call(
        functools.partial(renew_kernel, number),
        [(VMEM, ROW, BF16), (VMEM, ROW, F32), (VMEM, WHOLE, BF16), (VMEM, BLOCK, F32), (VMEM, (2, *BLOCK), F32),
         (VMEM, (24, 768), F32), (VMEM, (2, 24, 768), F32)],
        BACK_SCRATCH + REDUCE_SCRATCH + semaphores(REDUCE_COPIES + GATHER_COPIES), 2,
        back_args(*shared) + [(VMEM, a) for a in args],
    )


def final_call(number, shared, dense, deltas):
    box = VMEM((4, 24, 768), F32)
    part = (192, 1536)
    return call(
        functools.partial(final_kernel, number),
        [(VMEM, ROW, BF16), (VMEM, ROW, F32), (VMEM, (4, 24, 768), F32), (VMEM, (24, 24), F32), (VMEM, (24, 24), F32),
         (VMEM, (2, *part), F32)],
        BACK_SCRATCH + REDUCE_SCRATCH + [box] * 4
        + [VMEM((2, 2, *part), BF16), VMEM((2, 2, *part), BF16), VMEM((2, *part), BF16), VMEM((2, *part), BF16)]
        + semaphores(REDUCE_COPIES + 12 + 4),
        3,
        back_args(*shared) + [(VMEM, a) for a in dense] + [(ANY, a) for a in deltas],
    )


def cols_and_square(wide, square):
    return jnp.stack([wide[:, :768], wide[:, 768:1536], wide[:, 1536:], square])


def body(
    tokens,
    out_grad,
    expert_ids,
    replay,
    frozen_in,
    frozen_out,
    gains,
    w_qkv,
    w_proj,
    router,
    exp_in,
    exp_out,
    mom_gains,
    mom_qkv,
    mom_proj,
    mom_router,
    mom_in,
    mom_out,
    state_gains,
    state_qkv,
    state_proj,
    state_router,
    state_in,
    state_out,
):
    both_low = jnp.concatenate([exp_in[0], jnp.swapaxes(exp_out[0], 0, 1)], axis=1).astype(BF16)
    both_low = lax.all_gather(both_low, "group", axis=0, tiled=True)
    low_start = cols_and_square(w_qkv, w_proj).astype(BF16)
    low_start = jnp.concatenate([low_start[:, :, :384], low_start[:, :, 384:]], axis=1)
    moments = jnp.concatenate([cols_and_square(state_qkv[0, k], state_proj[0, k]) for k in range(2)], axis=1).astype(BF16)
    gap = jnp.zeros((24, 5), F32)
    packed = jnp.concatenate(
        [router, gains.T, gap, state_router[0, 0], state_gains[0, 0].T, gap, state_router[0, 1], state_gains[0, 1].T,
         jnp.zeros((24, 61), F32)], axis=1,
    )
    ids = jnp.concatenate([jnp.swapaxes(expert_ids, 1, 2), replay[:, None], jnp.zeros((2, 5, 128), jnp.int32)], axis=1)
    whole, p_start, mv, pe_start, mve = entry_call(low_start, moments, packed)
    frozen_both = (frozen_in[0], frozen_out[0])
    small = (tokens, out_grad, ids, pe_start)
    made = trade_call(
        True, STEP, 4, small, whole, both_low, *frozen_both, state_in[0, :, 0], state_out[0, :, 0]
    )
    shared = (small, whole, made[:7], made[7], made[8])
    block0, grad0, whole, p_now, mv, pe_now, mve = renew_call(STEP, shared, p_start, mv, pe_start, mve)
    small = (tokens, out_grad, ids, pe_now)
    made = trade_call(False, STEP + 1, 5, small, whole, both_low, *made[9:11], *frozen_both, *made[11:13])
    shared = (small, whole, made[:7], made[7], made[8])
    dense = (p_now, mv, pe_now, mve, p_start, pe_start)
    deltas = tuple(delta.reshape(2, 2, 192, 1536) for delta in made[9:11])
    block1, grad1, *means = final_call(STEP + 1, shared, dense, deltas)
    turn = lambda array: jnp.swapaxes(array[0], 0, 1)
    back = lambda array: jnp.swapaxes(array, 0, 1)[None]
    (block, grad, new_qkv, new_proj, new_mom_qkv, new_mom_proj, new_gains, new_router, new_mom_gains, new_mom_router,
     new_in, new_mom_in, new_out, new_mom_out) = finish_call(
        (block0, block1, grad0, grad1, *means, w_qkv, w_proj, mom_qkv, mom_proj, gains, router, mom_gains, mom_router),
        (exp_in[0], mom_in[0], turn(exp_out), turn(mom_out)),
    )
    return (
        block, grad, new_gains, new_qkv, new_proj, new_router, new_in[None], back(new_out),
        new_mom_gains, new_mom_qkv, new_mom_proj, new_mom_router, new_mom_in[None], back(new_mom_out),
    )


def solution(mesh):
    return jax.shard_map(
        body,
        mesh=mesh,
        in_specs=(
            P(None, ("group", "dp", "expert"), None),
            P(None, ("group", "dp", "expert"), None),
            P(None, ("group", "dp", "expert"), None),
            P(None, ("group", "dp", "expert")),
            P(),
            P(),
            P(None, ("dp", "expert")),
            P(("dp", "expert"), None),
            P(("dp", "expert"), None),
            P(("dp", "expert"), None),
            P("expert", "group", "dp"),
            P("expert", "dp", "group"),
            P(None, ("dp", "expert")),
            P(("dp", "expert"), None),
            P(("dp", "expert"), None),
            P(("dp", "expert"), None),
            P("expert", "group", "dp"),
            P("expert", "dp", "group"),
            P("group", None, None, ("dp", "expert")),
            P("group", None, ("dp", "expert"), None),
            P("group", None, ("dp", "expert"), None),
            P("group", None, ("dp", "expert"), None),
            P("group", None, "expert", None, "dp"),
            P("group", None, "expert", "dp", None),
        ),
        out_specs=(
            P(None, ("group", "dp", "expert"), None),
            P(None, ("group", "dp", "expert"), None),
            P(None, ("dp", "expert")),
            P(("dp", "expert"), None),
            P(("dp", "expert"), None),
            P(("dp", "expert"), None),
            P("expert", "group", "dp"),
            P("expert", "dp", "group"),
            P(None, ("dp", "expert")),
            P(("dp", "expert"), None),
            P(("dp", "expert"), None),
            P(("dp", "expert"), None),
            P("expert", "group", "dp"),
            P("expert", "dp", "group"),
        ),
        check_vma=False,
    )
```

```python
import functools

import jax
import jax.numpy as jnp
from jax import lax
from jax.experimental import pallas as pl
from jax.experimental.pallas import tpu as pltpu
from jax.sharding import PartitionSpec as P

MESH = pl.DeviceIdType.MESH
VMEM = pltpu.VMEM
F32 = jnp.float32
BF16 = jnp.bfloat16


class Links:
    def __init__(self, sends, recvs):
        self.sends, self.recvs, self.used, self.begun = sends, recvs, 0, []

    def send(self, src, dst, to):
        at = self.used
        self.used += 1
        copy = pltpu.make_async_remote_copy(
            src_ref=src, dst_ref=dst, send_sem=self.sends.at[at], recv_sem=self.recvs.at[at],
            device_id=to, device_id_type=MESH,
        )
        self.begun.append(copy)
        copy.start()
        return copy

    def finish(self):
        for copy in self.begun:
            copy.wait_send()


class Place:
    def __init__(self):
        self.g, self.d = lax.axis_index("group"), lax.axis_index("dp")
        e = lax.axis_index("expert")
        self.x, self.y = lax.div(e, 4), lax.rem(e, 4)

    def along_x(self, step, over=0):
        return {"dp": lax.rem(self.d + over, 2), "expert": lax.rem(self.x + step, 4) * 4 + self.y}

    def along_y(self, step, over=0):
        return {"dp": lax.rem(self.d + over, 2), "expert": self.x * 4 + lax.rem(self.y + step, 4)}

    def other_dp(self):
        return {"dp": 1 - self.d}

    def in_group(self, step, over=0):
        return {"group": lax.rem(self.g + step, 4), "expert": self.x * 4 + lax.rem(self.y + over, 4)}

    def other_core(self):
        return {"group": self.g + 1 - 2 * lax.rem(self.g, 2)}


def hail(partners):
    barrier = pltpu.get_barrier_semaphore()
    for partner in partners:
        pl.semaphore_signal(barrier, inc=1, device_id=partner, device_id_type=MESH)


def await_hails(partners):
    pl.semaphore_wait(pltpu.get_barrier_semaphore(), len(partners))


PEERS = ((0, 1), (1, 0), (3, 0), (1, 1), (3, 1), (2, 0), (2, 1))


def ring_partners(place):
    return (
        [place.along_x(*peer) for peer in PEERS]
        + [place.along_y(step) for step in (1, 2, 3)]
        + [place.along_y(step, 1) for step in (1, 2, 3)]
    )


class Gather:
    def __init__(self, links, place, whole, h, p1, p2, near1, near2, at, share=None):
        self.links, self.whole, self.h, self.at, self.d, self.place = links, whole, h, at, place.d, place
        self.p1, self.p2, self.near1, self.near2, self.share = p1, p2, near1, near2, share
        self.shared = []

    def push(self, k1, k2, dp, to):
        c, x = self.at(lax.rem(k1, 4), lax.rem(k2, 4))
        ref = self.whole.at[c, slice(None) if dp is None else dp, x, self.h]
        return self.links.send(ref, ref, to)

    def give(self, k1, k2):
        if self.share is not None:
            self.shared.append(self.push(k1, k2, None, self.share))

    def start(self):
        p1, p2, d = self.p1, self.p2, self.d
        self.over_dp = self.push(p1, p2, d, self.place.other_dp())
        self.own = [self.push(p1, p2, d, self.near1(1)), self.push(p1, p2, d, self.near1(3))]

    def ring_one(self):
        p1, p2, d = self.p1, self.p2, self.d
        self.over_dp.wait_recv()
        self.own += [self.push(p1, p2, 1 - d, self.near1(1)), self.push(p1, p2, 1 - d, self.near1(3))]
        self.pushed = [(p1, self.push(p1, p2, None, self.near2(1)), self.push(p1, p2, None, self.near2(3)))]
        self.give(p1, p2)
        for copy in self.own:
            copy.wait_recv()
        self.passed = [self.push(p1 + 3, p2, 0, self.near1(1)), self.push(p1 + 1, p2, 1, self.near1(3))]
        for k1 in (p1 + 3, p1 + 1):
            self.pushed.append((k1, self.push(k1, p2, None, self.near2(1)), self.push(k1, p2, None, self.near2(3))))
            self.give(k1, p2)

    def ring_two(self):
        p1, p2 = self.p1, self.p2
        for copy in self.passed:
            copy.wait_recv()
        k1 = p1 + 2
        self.pushed.append((k1, self.push(k1, p2, None, self.near2(1)), self.push(k1, p2, None, self.near2(3))))
        self.give(k1, p2)
        self.last = []
        for k1, right, left in self.pushed:
            right.wait_recv()
            self.last.append((k1, self.push(k1, p2 + 3, 0, self.near2(1))))
            self.give(k1, p2 + 3)
            left.wait_recv()
            self.last.append((k1, self.push(k1, p2 + 1, 1, self.near2(3))))
            self.give(k1, p2 + 1)

    def end(self):
        for n, (k1, copy) in enumerate(self.last):
            copy.wait_recv()
            if n % 2:
                self.give(k1, self.p2 + 2)
        for copy in self.shared:
            copy.wait_recv()


def run_gather(parts):
    for stage in ("ring_one", "ring_two", "end"):
        for part in parts:
            getattr(part, stage)()


def gather_parts(links, place, whole):
    by_x = lambda kx, ky: (ky, kx)
    by_y = lambda ky, kx: (ky, kx)
    first = Gather(links, place, whole, 0, place.x, place.y, place.along_x, place.along_y, by_x)
    second = Gather(links, place, whole, 1, place.y, place.x, place.along_y, place.along_x, by_y)
    return first, second


class RingSum:
    def __init__(self, links, near1, near2, p1, p2, d, term, far, near, mid, box):
        self.links, self.near1, self.near2, self.p1, self.p2, self.d = links, near1, near2, p1, p2, d
        self.term, self.far, self.near, self.mid, self.box = term, far, near, mid, box
        self.steps = (2, 1, 3, 0)
        self.far_copies, self.direct, self.summed, self.over = [], [], [], []

    def get(self, k, dp, i):
        return self.term(lax.rem(self.p1 + k, 4), dp, lax.rem(self.p2 + self.steps[i], 4))

    def send_far(self, i):
        self.far_copies.append([
            self.links.send(self.get(2, 1, i), self.far.at[0, i], self.near1(1)),
            self.links.send(self.get(2, 0, i), self.far.at[1, i], self.near1(3)),
        ])

    def send_direct(self, i):
        self.direct.append([
            self.links.send(self.get(1, 0, i), self.near.at[0, 0, i], self.near1(1)),
            self.links.send(self.get(3, 1, i), self.near.at[1, 1, i], self.near1(3)),
        ])

    def middle(self, i):
        out = []
        for side, step, dp in ((0, 1, 1), (1, 3, 0)):
            self.far_copies[i][side].wait_recv()
            self.far[side, i] = (self.far[side, i].astype(F32) + self.get(step, dp, i)[...].astype(F32)).astype(BF16)
            out.append(self.links.send(self.far.at[side, i], self.near.at[side, dp, i], self.near1(step)))
        self.summed.append(out)

    def finish(self, i):
        for copy in self.direct[i] + self.summed[i]:
            copy.wait_recv()
        mine = self.d * 4 + self.p2
        for dp in range(2):
            self.mid[i, dp] = (
                self.get(0, dp, i)[...].astype(F32)
                + self.near[0, dp, i].astype(F32)
                + self.near[1, dp, i].astype(F32)
            ).astype(BF16)
        step = self.steps[i]
        for over in (0, 1):
            src = self.mid.at[i, lax.rem(self.d + over, 2)]
            if step or over:
                self.over.append(self.links.send(src, self.box.at[mine], self.near2(step, over)))
            else:
                self.box[mine] = self.mid[i, self.d]

    def total(self):
        for copy in self.over:
            copy.wait_recv()
        value = self.box[0].astype(F32)
        for k in range(1, 8):
            value = value + self.box[k].astype(F32)
        return value


def folded(rows):
    return jnp.concatenate([rows[:, :384], rows[:, 384:]], axis=0).astype(BF16)


def unfolded(rows):
    return jnp.concatenate([rows[:24], rows[24:]], axis=1)


def add_over(links, own, box, position, size, reach):
    box[position] = folded(own)
    copies = [links.send(box.at[position], box.at[position], reach(step)) for step in range(1, size)]

    def finish():
        for copy in copies:
            copy.wait_recv()
        total = box[0].astype(F32)
        for k in range(1, size):
            total = total + box[k].astype(F32)
        return unfolded(total)

    return finish


HALF_SCRATCH = [
    VMEM((2, 4, 48, 768), BF16), VMEM((2, 2, 4, 48, 768), BF16), VMEM((4, 2, 48, 768), BF16), VMEM((8, 48, 768), BF16)
]
REDUCE_SCRATCH = HALF_SCRATCH * 2 + [VMEM((4, 48, 384), BF16), VMEM((4, 48, 384), BF16), VMEM((2, 48, 384), BF16)]
REDUCE_COPIES = 2 * (24 + 7) + 7
GATHER_COPIES = 2 * (1 + 4 + 2 + 8 + 8)


class Reduction:
    def __init__(self, links, place, grads, scratch):
        self.links, self.place, self.boxes = links, place, scratch[8:]
        self.parts = (
            RingSum(
                links, place.along_y, place.along_x, place.y, place.x, place.d,
                lambda k, dp, j: grads.at[k, dp, j, 0], *scratch[:4],
            ),
            RingSum(
                links, place.along_x, place.along_y, place.x, place.y, place.d,
                lambda k, dp, j: grads.at[j, dp, k, 1], *scratch[4:8],
            ),
        )

    def start(self):
        for i in range(4):
            for part in self.parts:
                part.send_far(i)
        for part in self.parts:
            part.send_direct(0)

    def finish(self, extra):
        links, place, parts = self.links, self.place, self.parts
        box_x, box_y, box_z = self.boxes
        extra_x = add_over(links, extra, box_x, place.x, 4, place.along_x)
        for i in range(4):
            for part in parts:
                if i:
                    part.send_direct(i)
                part.middle(i)
            if i == 1:
                extra_y = add_over(links, extra_x(), box_y, place.y, 4, place.along_y)
            if i == 3:
                extra_z = add_over(links, extra_y(), box_z, place.d, 2, lambda step: place.other_dp())
        for i in range(4):
            for part in parts:
                part.finish(i)
        return [part.total() for part in parts], extra_z()


EPS_NORM = 1e-06
BETA_ONE = 0.9
BETA_TWO = 0.95
ADAM_EPS = 1e-08
DECAY = 0.1
OUTER_RATE = 0.7
OUTER_MOMENTUM = 0.9
REPLAY_WEIGHT = 0.25
RATES = (0.6, 0.04, 0.3, 0.03, 0.04, 0.02)
HEADS = 12
LEN = 128
STEPS = 2
STEP = 10


PIECE = 32


class ExpertGather:
    def __init__(self, links, place, own, both):
        self.links, self.place, self.own, self.both = links, place, own, both
        self.far, self.near = [], []

    def rows(self, group, n=None):
        if n is None:
            return self.both.at[pl.ds(pl.multiple_of(group * 192, 192), 192)]
        return self.both.at[pl.ds(pl.multiple_of(group * 192 + n * PIECE, PIECE), PIECE)]

    def send(self, n):
        part = self.own.at[pl.ds(n * PIECE, PIECE)]
        self.far.append(self.links.send(part, self.rows(self.place.g, n), self.place.in_group(2)))

    def share(self):
        self.near.append(self.links.send(self.own, self.rows(self.place.g), self.place.other_core()))

    def pass_on(self, n):
        self.far[n].wait_recv()
        ref = self.rows(lax.rem(self.place.g + 2, 4), n)
        self.near.append(self.links.send(ref, ref, self.place.other_core()))

    def end(self):
        for copy in self.near:
            copy.wait_recv()


def entry_kernel(w_qkv, w_proj, s_qkv, s_proj, e_in, in_hbm, out_hbm, whole, p_out, mv_out, pe_out, mve_out, both,
                 p_in, mv_in, own, loaded, e_out, p_box, mv_box, local_sems, sends, recvs):
    place = Place()
    partners = ring_partners(place) + [place.other_core(), place.in_group(2)]
    hail(partners)
    loads = [
        pltpu.make_async_copy(src, loaded.at[k], local_sems.at[k]) for k, src in enumerate((in_hbm, out_hbm))
    ]
    for copy in loads:
        copy.start()
    for c in range(4):
        lanes = slice(768 * c, 768 * c + 768) if c < 3 else slice(None)
        master, state = (w_qkv, s_qkv) if c < 3 else (w_proj, s_proj)
        p_in[c] = folded(master[:, lanes])
        mv_in[c] = jnp.concatenate([state[0, :, lanes], state[1, :, lanes]], axis=0).astype(BF16)
    await_hails(partners)
    links = Links(sends, recvs)
    x, y, d = place.x, place.y, place.d
    h = lax.rem(place.g, 2)
    masters = [links.send(p_in.at[lax.rem(y + k, 4)], p_box.at[y], place.along_y(k)) for k in (1, 2, 3)]
    e_out[d, x, y] = e_in[...]
    mine = e_out.at[d, x, y]
    extra_z = links.send(mine, mine, place.other_dp())
    p_box[y] = p_in[y]
    mv_box[y] = mv_in[y]
    for k in range(2):
        loads[k].wait()
        own[:, 1536 * k : 1536 * k + 1536] = loaded[k].astype(BF16)
    experts = ExpertGather(links, place, own, both)
    experts.send(0)
    mine_there = pltpu.make_async_copy(own, experts.rows(place.g), local_sems.at[2])
    mine_there.start()
    for copy in masters:
        copy.wait_recv()
    halves = p_box[...].astype(F32)
    master = jnp.concatenate([halves[:, :24], halves[:, 24:]], axis=2).reshape(2, 48, 768)
    p_out[...] = master

    @pl.when(h == 0)
    def _():
        whole[y, d, x, 0] = master[0].astype(BF16)

    @pl.when(h == 1)
    def _():
        whole[y, d, x, 1] = master[1].astype(BF16)

    def mix(a, b):
        return a * (1 - h) + b * h

    def near1(step, over=0):
        one, two = place.along_x(step, over), place.along_y(step, over)
        return {"dp": one["dp"], "expert": mix(one["expert"], two["expert"])}

    def near2(step):
        one, two = place.along_y(step), place.along_x(step)
        return {"dp": one["dp"], "expert": mix(one["expert"], two["expert"])}

    def at(k1, k2):
        return mix(k2, k1), mix(k1, k2)

    part = Gather(links, place, whole, h, mix(x, y), mix(y, x), near1, near2, at, place.other_core())
    part.start()
    for n in range(1, 192 // PIECE):
        experts.send(n)
    extra_z.wait_recv()
    mine = e_out.at[:, x, y]
    extra_x = [links.send(mine, mine, place.along_x(k)) for k in (1, 2, 3)]
    part.ring_one()
    experts.share()
    for copy in extra_x:
        copy.wait_recv()
    mine = e_out.at[:, :, y]
    extra_y = [links.send(mine, mine, place.along_y(k)) for k in (1, 2, 3)]
    part.ring_two()
    moments = [links.send(mv_in.at[lax.rem(y + k, 4)], mv_box.at[y], place.along_y(k)) for k in (1, 2, 3)]
    for n in range(192 // PIECE - 1):
        experts.pass_on(n)
    for copy in extra_y:
        copy.wait_recv()
    turned = e_out[...].reshape(768, 128).T
    pe_out[...] = turned[:24]
    mve_out[0] = turned[24:48]
    mve_out[1] = turned[48:72]
    part.end()
    experts.pass_on(192 // PIECE - 1)
    for copy in moments:
        copy.wait_recv()
    moment = mv_box[...].astype(F32)
    for k in range(2):
        mv_out[k] = moment[:, 24 * k : 24 * k + 24].reshape(2, 48, 768)
    experts.end()
    mine_there.wait()
    links.finish()


def adam_values(master, first, second, grad, rate, number):
    first = BETA_ONE * first + (1.0 - BETA_ONE) * grad
    second = BETA_TWO * second + (1.0 - BETA_TWO) * grad * grad
    level = second * (1.0 / (1.0 - BETA_TWO**number))
    below = level * lax.rsqrt(jnp.maximum(level, 1e-30)) + ADAM_EPS
    guess = pl.reciprocal(below, approx=True)
    update = first * ((1.0 / (1.0 - BETA_ONE**number)) * rate) * (guess * (2.0 - below * guess))
    return master - (update + (rate * DECAY) * master), first, second


def block_rate(place):
    return jnp.where(place.y == 3, RATES[2], RATES[1]).astype(F32)


def extra_rates():
    row = lax.broadcasted_iota(jnp.int32, (24, 768), 0)
    return jnp.where(row < 17, RATES[3], RATES[0]).astype(F32)


def renew_part(number, place, links, reduction, extra, p_in, mv_in, pe_in, mve_in,
               whole, p_out, mv_out, pe_out, mve_out):
    sums, total = reduction.finish(extra)
    parts = gather_parts(links, place, whole)
    for h, part in enumerate(parts):
        fresh, first, second = adam_values(p_in[h], mv_in[0, h], mv_in[1, h], sums[h], block_rate(place), number)
        whole[place.y, place.d, place.x, h] = fresh.astype(BF16)
        part.start()
        p_out[h] = fresh
        mv_out[0, h] = first
        mv_out[1, h] = second
    pe_out[...], mve_out[0], mve_out[1] = adam_values(pe_in[...], mve_in[0], mve_in[1], total, extra_rates(), number)
    run_gather(parts)


def outer(begin, moment, mean):
    renewed = OUTER_MOMENTUM * moment + mean
    return begin - OUTER_RATE * (mean + OUTER_MOMENTUM * renewed), renewed


def own_features(place, rows, turned):
    at = 24 * (16 * place.d + 4 * place.x + place.y)
    pick = (lax.broadcasted_iota(jnp.int32, (768, 24), 0) == at + lax.broadcasted_iota(jnp.int32, (768, 24), 1)).astype(BF16)
    total = 0.0
    for _ in range(3):
        part = rows.astype(BF16)
        total = total + (
            lax.dot_general(pick, part, (((0,), (1,)), ((), ())), preferred_element_type=F32) if turned
            else lax.dot_general(part, pick, (((1,), (0,)), ((), ())), preferred_element_type=F32)
        )
        rows = rows - part.astype(F32)
    return total


class ExpertMean:
    def __init__(self, links, place, copies, deltas, others, own, other, sent, far):
        self.links, self.place, self.own, self.other, self.sent, self.far = links, place, own, other, sent, far
        self.high = lax.div(place.g, 2)
        self.loads = [copies.start(delta.at[:, lax.rem(place.g, 2)], own.at[k]) for k, delta in enumerate(deltas)]
        self.loads += [copies.start(array, other.at[k]) for k, array in enumerate(others)]

    def start(self):
        for copy in self.loads:
            copy.wait()
        self.copies = []
        for k in range(2):
            self.sent[k] = (
                self.own[k, 1 - self.high].astype(F32) + self.other[k, 1 - self.high].astype(F32)
            ).astype(BF16)
            self.copies.append(self.links.send(self.sent.at[k], self.far.at[k], self.place.in_group(2)))

    def mean(self, k):
        self.copies[k].wait_recv()
        mine = self.own[k, self.high].astype(F32) + self.other[k, self.high].astype(F32)
        return (mine + self.far[k].astype(F32)) * 0.25


def final_part(number, place, links, reduction, extra, p_in, mv_in, pe_in, mve_in, p_start, pe_start,
               turned, flat_out, turned_out, delta, quarters, mean, boxes):
    g, y = place.g, place.y
    sums, total = reduction.finish(extra)
    for h in range(2):
        fresh, _, _ = adam_values(p_in[h], mv_in[0, h], mv_in[1, h], sums[h], block_rate(place), number)
        delta[2 * h : 2 * h + 2] = (p_start[h] - fresh).reshape(2, 24, 768)
    summed = [
        links.send(delta.at[lax.rem(g + k, 4)], quarters.at[g], place.in_group(k)) for k in (1, 2, 3)
    ]
    fresh_e, _, _ = adam_values(pe_in[...], mve_in[0], mve_in[1], total, extra_rates(), number)
    sum_e = add_over(links, pe_start[...] - fresh_e, boxes, g, 4, place.in_group)
    quarters[g] = delta[g]
    for copy in summed:
        copy.wait_recv()
    mean[...] = (quarters[0] + quarters[1] + quarters[2] + quarters[3]) * 0.25
    at = links.used
    links.used += 4

    def spread(k):
        return pltpu.make_async_remote_copy(
            src_ref=mean, dst_ref=turned.at[y], send_sem=links.sends.at[at + k], recv_sem=links.recvs.at[at + y],
            device_id={"group": lax.rem(g + k, 4), "expert": place.x * 4 + g}, device_id_type=MESH,
        )

    def arrival(c):
        return pltpu.make_async_remote_copy(
            src_ref=mean, dst_ref=turned.at[c], send_sem=links.sends.at[at], recv_sem=links.recvs.at[at + c],
            device_id=place.other_core(), device_id_type=MESH,
        )

    for k in (1, 2, 3):
        spread(k).start()

    @pl.when(y != g)
    def _():
        spread(0).start()

    @pl.when(y == g)
    def _():
        turned[y] = mean[...]

    mean_e = sum_e() * 0.25
    flat_out[...] = own_features(place, mean_e, False)
    turned_out[...] = own_features(place, mean_e, True)
    for c in range(4):
        @pl.when(jnp.logical_or(y != g, c != y))
        def _(c=c):
            arrival(c).wait_recv()

    for k in (1, 2, 3):
        spread(k).wait_send()

    @pl.when(y != g)
    def _():
        spread(0).wait_send()


def semaphores(count):
    return [pltpu.SemaphoreType.DMA((count,)), pltpu.SemaphoreType.DMA((count,))]


ANY = pl.ANY
WHOLE = (4, 2, 4, 2, 48, 768)
BLOCK = (2, 48, 768)
ROW = (128, 768)


def call(kernel, outs, scratch, collective_id, args, limit=60 << 20):
    return pl.pallas_call(
        kernel,
        out_shape=tuple(jax.ShapeDtypeStruct(shape, kind) for _, shape, kind in outs),
        in_specs=[pl.BlockSpec(memory_space=space) for space, _ in args],
        out_specs=tuple(pl.BlockSpec(memory_space=space) for space, _, _ in outs),
        scratch_shapes=scratch,
        compiler_params=pltpu.CompilerParams(
            collective_id=collective_id, has_side_effects=True, vmem_limit_bytes=limit
        ),
    )(*(array for _, array in args))


def entry_call(w_qkv, w_proj, s_qkv, s_proj, e_in, exp_in, exp_out):
    return call(
        entry_kernel,
        [(VMEM, WHOLE, BF16), (VMEM, BLOCK, F32), (VMEM, (2, *BLOCK), F32), (VMEM, (24, 768), F32),
         (VMEM, (2, 24, 768), F32), (ANY, (768, 3072), BF16)],
        [VMEM((4, 48, 384), BF16), VMEM((4, 48, 768), BF16), VMEM((192, 3072), BF16), VMEM((2, 192, 1536), F32),
         VMEM((2, 4, 4, 24, 128), F32), VMEM((4, 48, 384), BF16), VMEM((4, 48, 768), BF16),
         pltpu.SemaphoreType.DMA((3,))]
        + semaphores(3 + 7 + 23 + 3 + 16 + 2 * (192 // PIECE) + 1), 1,
        [(VMEM, a) for a in (w_qkv, w_proj, s_qkv, s_proj, e_in)] + [(ANY, exp_in), (ANY, exp_out)],
    )

CAP = 24
TOK = 128
DIMS = {"nn": (((1,), (0,)), ((), ())), "nt": (((1,), (1,)), ((), ())), "tn": (((0,), (0,)), ((), ()))}


def mm(a, b, form="nn"):
    return lax.dot_general(a, b, DIMS[form], preferred_element_type=F32)


def split_low(values):
    high = values.astype(BF16)
    return high, (values - high.astype(F32)).astype(BF16)


def row_scale(values):
    return lax.rsqrt(jnp.mean(values * values, axis=-1, keepdims=True) + EPS_NORM)


def iota(shape, dim):
    return lax.broadcasted_iota(jnp.int32, shape, dim)


def routing(ids):
    names = [(iota((24, TOK), 0) == ids[k : k + 1]).astype(F32) for k in range(2)]
    either = names[0] + names[1]
    earlier = (iota((TOK, TOK), 0) < iota((TOK, TOK), 1)).astype(BF16)
    slot = mm(either.astype(BF16), earlier).astype(jnp.int32)
    taken = jnp.where(iota((17, CAP, TOK), 1) == slot[:17][:, None, :], 1.0, 0.0)
    return names, taken * either[:17][:, None, :]


def pair_stack(part):
    lane = iota(part.shape, 1)
    zero = jnp.zeros_like(part)
    return jnp.concatenate([jnp.where(lane < 64, part, zero), jnp.where(lane < 64, zero, part)], axis=0)


def side_by_side(stacked):
    return jnp.concatenate([stacked[:TOK], stacked[TOK:]], axis=1)


def flat(whole, c):
    return whole[c].reshape(768, 768)


def cotangent(og_ref, ids_ref):
    factor = jnp.where(ids_ref[2:3] > 0, REPLAY_WEIGHT, 1.0)
    spread = jnp.where(iota((TOK, TOK), 0) == iota((TOK, TOK), 1), factor, 0.0).astype(BF16)
    return mm(spread, og_ref[...])


def front_part(x_ref, og_ref, ids_ref, pe_ref, whole,
               send, frozen, qkv_out, probs_out, mixed_out, middle_out, a1_out, a2_out, weights_out):
    gain = pe_ref[16:24].astype(BF16).astype(F32)
    x = x_ref[...].astype(F32)
    a1 = (x * row_scale(x) * gain[1:2]).astype(BF16)
    a1_out[...] = a1
    for c in range(3):
        qkv_out[c] = mm(a1, flat(whole, c)).astype(BF16)
    row, col = iota((2 * TOK, TOK), 0), iota((2 * TOK, TOK), 1)
    causal = lax.rem(row, TOK) >= col
    for pair in range(6):
        lanes = slice(128 * pair, 128 * pair + 128)
        scores = mm(pair_stack(qkv_out[0, :, lanes]), qkv_out[1, :, lanes], "nt") * 0.125
        scores = jnp.where(causal, scores, -1e30)
        expo = jnp.exp(scores - jnp.max(scores, axis=-1, keepdims=True))
        probs = expo / jnp.sum(expo, axis=-1, keepdims=True)
        probs_out[pair] = probs
        mixed_out[:, lanes] = mm(side_by_side(probs.astype(BF16)), pair_stack(qkv_out[2, :, lanes])).astype(BF16)
    middle = x + mm(mixed_out[...], flat(whole, 3))
    middle_out[...] = middle
    a2 = (middle * row_scale(middle) * gain[2:3]).astype(BF16)
    a2_out[...] = a2
    logits = mm(pe_ref[...].astype(BF16), a2, "nt")
    names, taken = routing(ids_ref[...])
    picked = [jnp.sum(name * logits, axis=0, keepdims=True) for name in names]
    top = jnp.maximum(picked[0], picked[1])
    expo = [jnp.exp(z - top) for z in picked]
    whole_sum = expo[0] + expo[1]
    weights = [e / whole_sum for e in expo]
    weights_out[...] = jnp.concatenate(weights + [jnp.zeros((6, TOK), F32)], axis=0)
    by_expert = names[0] * weights[0] + names[1] * weights[1]
    row_weight = jnp.sum(taken * by_expert[:17][:, None, :], axis=-1, keepdims=True)
    cot = cotangent(og_ref, ids_ref).astype(BF16)
    low = taken.astype(BF16).reshape(17 * CAP, TOK)
    rows = mm(low, a2).reshape(17, CAP, 768)
    grads = mm(low, cot).reshape(17, CAP, 768) * row_weight
    both = jnp.concatenate([rows, grads], axis=1).astype(BF16)
    frozen[...] = both[0]
    send[...] = both[1:]


def back_part(x_ref, og_ref, ids_ref, pe_ref, whole, qkv, probs_ref, mixed, middle_ref, a1, a2,
              weights_ref, ret, frozen, block_out, grad_out, grads, arrived, ready):
    gain = pe_ref[16:24].astype(BF16).astype(F32)
    low_rows = pe_ref[...].astype(BF16)
    cot = cotangent(og_ref, ids_ref)
    names, taken = routing(ids_ref[...])
    weights = [weights_ref[k : k + 1] for k in range(2)]
    by_expert = names[0] * weights[0] + names[1] * weights[1]
    row_weight = jnp.sum(taken * by_expert[:17][:, None, :], axis=-1, keepdims=True)
    low = taken.astype(BF16).reshape(17 * CAP, TOK)
    both = ret[...].astype(F32)
    both = jnp.concatenate([frozen[...][None], both], axis=0)
    results, back = both[:, :CAP], both[:, CAP:].reshape(17 * CAP, 768)
    middle = middle_ref[...]
    cot_rows = mm(low, cot.astype(BF16)).reshape(17, CAP, 768)
    grad_row = jnp.sum(cot_rows * results, axis=-1, keepdims=True)
    by_name = jnp.concatenate([jnp.sum(taken * grad_row, axis=1), jnp.zeros((7, TOK), F32)], axis=0)
    grad_w = [jnp.sum(name * by_name, axis=0, keepdims=True) for name in names]
    mean = weights[0] * grad_w[0] + weights[1] * grad_w[1]
    grad_logits = sum(names[k] * (weights[k] * (grad_w[k] - mean)) for k in range(2))
    logit_parts = split_low(grad_logits)
    da2 = sum(mm(part, low_rows, "tn") for part in logit_parts)
    da2 = da2 + sum(mm(low, part, "tn") for part in split_low(back))
    scale = row_scale(middle)
    normed = middle * scale
    dg2 = jnp.sum(normed * da2, axis=0, keepdims=True)
    into = da2 * gain[2:3]
    dmiddle = cot + scale * (into - normed * jnp.mean(into * normed, axis=-1, keepdims=True))
    branch = dmiddle.astype(BF16)
    arrived()
    grads[3] = mm(mixed[...], branch, "tn").astype(BF16).reshape(2, 4, 2, 48, 768)
    dmixed = mm(branch, flat(whole, 3), "nt").astype(BF16)
    da1 = jnp.zeros((TOK, 768), F32)
    parts = [[], [], []]
    for pair in range(6):
        lanes = slice(128 * pair, 128 * pair + 128)
        probs = probs_ref[pair]
        dms = pair_stack(dmixed[:, lanes])
        parts[2].append(mm(probs.astype(BF16), dms, "tn").astype(BF16))
        dpb = mm(dms, qkv[2, :, lanes], "nt")
        ds = (probs * (dpb - jnp.sum(probs * dpb, axis=-1, keepdims=True))).astype(BF16)
        parts[0].append((mm(side_by_side(ds), pair_stack(qkv[1, :, lanes])) * 0.125).astype(BF16))
        parts[1].append((mm(ds, pair_stack(qkv[0, :, lanes]), "tn") * 0.125).astype(BF16))
    dqkv = [jnp.concatenate(part, axis=1) for part in parts]
    for c in range(3):
        grads[c] = mm(a1[...], dqkv[c], "tn").astype(BF16).reshape(2, 4, 2, 48, 768)
    ready()
    for c in range(3):
        da1 = da1 + mm(dqkv[c], flat(whole, c), "nt")
    x = x_ref[...].astype(F32)
    scale = row_scale(x)
    normed = x * scale
    dg1 = jnp.sum(normed * da1, axis=0, keepdims=True)
    into = da1 * gain[1:2]
    grad_out[...] = dmiddle + scale * (into - normed * jnp.mean(into * normed, axis=-1, keepdims=True))
    grad_router = sum(mm(part, a2[...]) for part in logit_parts)
    block_out[...] = (
        middle + sum(mm(low, part, "tn") for part in split_low((results * row_weight).reshape(17 * CAP, 768)))
    ).astype(BF16)
    return jnp.concatenate([grad_router[:17], dg1, dg2, jnp.zeros((5, 768), F32)], axis=0)


SQRT_HALF = 0.7071067811865476
DENSITY = 0.3989422804014327


def expert_rows(rows, grad, first, second):
    u = mm(rows, first)
    chance = 0.5 + 0.5 * lax.erf(u * SQRT_HALF)
    h = (u * chance).astype(BF16)
    value = mm(h, second)
    slope = chance + u * (jnp.exp(u * u * -0.5) * DENSITY)
    du = (slope * mm(grad, second, "nt")).astype(BF16)
    return value, mm(du, first, "nt"), h, du


class Copies:
    def __init__(self, sems):
        self.sems, self.used = sems, 0

    def start(self, src, dst):
        copy = pltpu.make_async_copy(src, dst, self.sems.at[self.used])
        self.used += 1
        copy.start()
        return copy


def grow_experts(first_step, number, copies, rows, grad, h, du, w1, w2, mv1, mv2, starts, news, bufs, between):
    (mv1_buf, mv2_buf, d1_buf, d2_buf, w1_out, w2_out, mv1_out, mv2_out, d1_out, d2_out) = bufs
    tiles = [(0, t) for t in range(6)] + [(1, t) for t in range(6)]

    def cut(which, t):
        size = (128, 256)[which]
        return pl.ds(size * t, size), slice(None)

    def parts_of(t):
        begin, end = 128 * t, 128 * t + 128
        cuts = sorted({begin, end} | {192 * q for q in range(5) if begin < 192 * q < end})
        return [(low // 192, low % 192, high - low, low - begin) for low, high in zip(cuts, cuts[1:])]

    def load(n):
        which, t = tiles[n]
        slot = n % 2
        mv, buf = ((mv1, mv1_buf), (mv2, mv2_buf))[which]
        size = (128, 256)[which]
        begun = [copies.start(mv.at[:, pl.ds(size * t, size)], buf.at[slot])]
        if not first_step:
            begun.append(copies.start(starts[which].at[cut(which, t)], (d1_buf, d2_buf)[which].at[slot]))
        return begun

    loads = {0: load(0)}
    stores = {}
    for n, (which, t) in enumerate(tiles):
        slot = n % 2
        if n + 1 < len(tiles):
            loads[n + 1] = load(n + 1)
        for copy in loads[n]:
            copy.wait()
        for copy in stores.pop(n - 2, ()):
            copy.wait()
        if which == 0:
            value = mm(rows[:, 128 * t : 128 * t + 128], du[...], "tn")
            begin = w1[128 * t : 128 * t + 128].astype(F32)
            moments = mv1_buf
        else:
            value = mm(h[:, 256 * t : 256 * t + 256], grad[...], "tn")
            begin = w2[256 * t : 256 * t + 256].astype(F32)
            moments = mv2_buf
        fresh, first, second = adam_values(
            begin, moments[slot, 0].astype(F32), moments[slot, 1].astype(F32), value, RATES[4 + which], number
        )
        here = cut(which, t)
        if first_step:
            low, mv_low = (w1_out, w2_out)[which], (mv1_out, mv2_out)[which]
            low[slot] = fresh.astype(BF16)
            mv_low[slot, 0] = first.astype(BF16)
            mv_low[slot, 1] = second.astype(BF16)
            size = (128, 256)[which]
            stores[n] = [
                copies.start(low.at[slot], news[which].at[here]),
                copies.start(mv_low.at[slot], news[2 + which].at[:, pl.ds(size * t, size)]),
            ]
        else:
            change = (d1_buf, d2_buf)[which][slot].astype(F32) - fresh
            if which == 0:
                d1_out[slot] = change.astype(BF16)
                stores[n] = [
                    copies.start(d1_out.at[slot, pl.ds(inside, size)], news[0].at[q // 2, q % 2, pl.ds(low, size)])
                    for q, low, size, inside in parts_of(t)
                ]
            else:
                d2_out[slot] = change.astype(BF16).T.reshape(2, 2, 192, 256)
                stores[n] = [copies.start(d2_out.at[slot], news[1].at[:, :, :, pl.ds(256 * t, 256)])]
        between(n, stores)
    return [copy for group in (len(tiles) - 2, len(tiles) - 1) for copy in stores.get(group, ())]


KEPT = [((3, *ROW), BF16), ((6, 256, 128), F32), (ROW, BF16), (ROW, F32), (ROW, BF16), (ROW, BF16), ((8, 128), F32)]


def trade_kernel(first_step, number, *refs):
    (x, og, ids, pe, whole_hbm, both_hbm), refs = refs[:6], refs[6:]
    step = 0 if first_step else 1
    x, og, ids = x.at[step], og.at[step], ids.at[step]
    if first_step:
        starts, w1_hbm = (), both_hbm.at[:, :1536]
    else:
        (w2_start, w1_hbm, w2_hbm), refs = refs[:3], refs[3:]
        starts = (both_hbm.at[:, :1536], w2_start)
    (fin_hbm, fout_hbm, mv1, mv2), refs = refs[:4], refs[4:]
    kept_out, refs = refs[:7], refs[7:]
    ret, frozen_out, refs = refs[0], refs[1], refs[2:]
    news, others, refs = refs[:4], refs[2:4], refs[4:]
    if first_step:
        w2_start, refs = refs[0], refs[1:]
    kept, refs = refs[:7], refs[7:]
    (whole, w1, w2, fin, fout, send, frozen_in, recv, ans, zret, home, rows_all, grad_all, h_all, du_all, local_sems,
     in_send, in_recv, z_send, z_recv, zb_send, zb_recv, home_send, home_recv,
     core_send, core_recv, w2_turned), bufs = refs[:27], refs[27:]
    copies = Copies(local_sems)
    w2_load = (both_hbm.at[:, 1536:], w2_turned) if first_step else (w2_hbm, w2)
    loads = [
        copies.start(src, dst)
        for src, dst in ((whole_hbm, whole), (fin_hbm, fin), (fout_hbm, fout), (w1_hbm, w1), w2_load)
    ]
    d, e = lax.axis_index("dp"), lax.axis_index("expert")
    partner = {"dp": 1 - d}
    g = lax.axis_index("group")
    core = lax.rem(g, 2)
    other_core = {"group": g + 1 - 2 * core}

    def ahead(k):
        return lax.rem(e + k, 16)

    def behind(k):
        return lax.rem(e + 16 - k, 16)

    barrier = pltpu.get_barrier_semaphore()

    @pl.loop(1, 16)
    def _(k):
        pl.semaphore_signal(barrier, inc=1, device_id={"expert": ahead(k)}, device_id_type=MESH)

    pl.semaphore_signal(barrier, inc=1, device_id=partner, device_id_type=MESH)
    if not first_step:
        pl.semaphore_signal(barrier, inc=1, device_id=other_core, device_id_type=MESH)
    loads[0].wait()
    front_part(x, og, ids, pe, whole, send, frozen_in, *kept)
    pl.semaphore_wait(barrier, 16 if first_step else 17)

    def remote(src, dst, sends, recvs, k, to):
        return pltpu.make_async_remote_copy(
            src_ref=src, dst_ref=dst, send_sem=sends.at[k], recv_sem=recvs.at[k], device_id=to, device_id_type=MESH
        )

    def to_expert(k):
        return remote(send.at[ahead(k)], recv.at[0, e], in_send, in_recv, k, {"expert": ahead(k)})

    def to_partner(k):
        return remote(recv.at[0, behind(k)], recv.at[1, behind(k)], z_send, z_recv, k, partner)

    def from_partner(k):
        return remote(ans.at[1, behind(k)], zret.at[behind(k)], zb_send, zb_recv, k, partner)

    def to_home(k):
        return remote(home.at[behind(k)], ret.at[e], home_send, home_recv, k, {"expert": behind(k)})

    @pl.loop(1, 16)
    def _(k):
        to_expert(k).start()

    recv[0, e] = send[e]
    to_partner(0).start()
    keeps = [copies.start(src, dst) for src, dst in zip(kept, kept_out)]

    def pass_on(k):
        to_expert(k).wait_recv()
        to_partner(k).start()

    pl.loop(1, 6)(pass_on)
    for copy in loads[1:3]:
        copy.wait()
    both = frozen_in[...].astype(F32)
    value, back, _, _ = expert_rows(both[:CAP].astype(BF16), both[CAP:].astype(BF16), fin[...], fout[...])
    frozen_out[...] = jnp.concatenate([value, back], axis=0)
    pl.loop(6, 16)(pass_on)
    for copy in loads[3:]:
        copy.wait()
    if first_step:
        for t in range(6):
            w2[256 * t : 256 * t + 256] = w2_turned[:, 256 * t : 256 * t + 256].T
        keeps.append(copies.start(w2, w2_start))

    @pl.loop(0, 4)
    def _(j):
        other = lax.rem(lax.div(j + 1, 2) + 1, 2)
        half = lax.div(j, 2)

        @pl.when(other == 1)
        def _():
            @pl.loop(0, 8)
            def _(i):
                to_partner(half * 8 + i).wait_recv()

        blocks = [recv[other, behind(half * 8 + i)].astype(F32) for i in range(8)]
        rows = jnp.concatenate([b[:CAP] for b in blocks], axis=0).astype(BF16)
        grad = jnp.concatenate([b[CAP:] for b in blocks], axis=0).astype(BF16)
        value, back, h, du = expert_rows(rows, grad, w1[...], w2[...])
        at = pl.ds(pl.multiple_of(j * 192, 192), 192)
        rows_all[at] = rows
        grad_all[at] = grad
        h_all[at] = h
        du_all[at] = du
        for i in range(8):
            part = slice(i * CAP, (i + 1) * CAP)
            ans[other, behind(half * 8 + i)] = jnp.concatenate([value[part], back[part]], axis=0).astype(BF16)

        @pl.when(other == 1)
        def _():
            @pl.loop(0, 8)
            def _(i):
                from_partner(half * 8 + i).start()

    def serve(k):
        from_partner(k).wait_recv()
        slot = behind(k)
        total = (ans[0, slot].astype(F32) + zret[slot].astype(F32)).astype(BF16)
        if k == 0:
            ret[e] = total
        else:
            home[slot] = total
            to_home(k).start()

    def to_core(which):
        return remote(news[which].at[:, 1 - core], others[which], core_send, core_recv, which, other_core)

    def between(n, stores):
        for k in range(SERVED[n], SERVED[n + 1]):
            serve(k)
        if not first_step and n in (7, 11):
            for tile in ((4, 5) if n == 7 else (10, 11)):
                for copy in stores.pop(tile, ()):
                    copy.wait()
            to_core(0 if n == 7 else 1).start()

    for k in range(SERVED[0]):
        serve(k)
    left = grow_experts(
        first_step, number, copies, rows_all, grad_all, h_all, du_all, w1, w2, mv1, mv2, starts, news, bufs, between
    )

    @pl.loop(1, 16)
    def _(k):
        to_home(k).wait_recv()
        to_home(k).wait_send()
        to_expert(k).wait_send()

    @pl.loop(0, 16)
    def _(k):
        to_partner(k).wait_send()
        from_partner(k).wait_send()

    if not first_step:
        for which in range(2):
            to_core(which).wait_recv()
            to_core(which).wait_send()
    for copy in left + keeps:
        copy.wait()


SERVED = (3, 4, 6, 7, 9, 10, 12, 13, 15, 16, 16, 16, 16)


def trade_call(first_step, number, collective_id, small, *large):
    wide = (768, 1536)
    moment_kind = F32 if first_step else BF16
    tall, quarters = (1536, 768), (2, 2, 192, 1536)
    news = (
        [(ANY, wide, BF16), (ANY, tall, BF16), (ANY, (2, 768, 1536), BF16), (ANY, (2, 1536, 768), BF16), (ANY, tall, BF16)]
        if first_step else [(ANY, quarters, BF16)] * 2 + [(ANY, (2, 192, 1536), BF16)] * 2
    )
    outs = [(ANY, *k) for k in KEPT] + [(VMEM, (16, 48, 768), BF16), (VMEM, (48, 768), F32)] + news
    t1, t2, c1, c2 = (2, 2, 128, 1536), (2, 2, 256, 768), (2, 128, 1536), (2, 256, 768)
    none = (8, 128)
    first = first_step
    bufs = [
        VMEM(t1, moment_kind), VMEM(t2, moment_kind),
        VMEM(none if first else c1, BF16), VMEM(none if first else c2, BF16),
        VMEM(c1 if first else none, BF16), VMEM(c2 if first else none, BF16),
        VMEM(t1 if first else none, BF16), VMEM(t2 if first else none, BF16),
        VMEM(none if first else c1, BF16), VMEM(none if first else (2, 2, 2, 192, 256), BF16),
    ]
    plane = (16, 48, 768)
    scratch = [VMEM(*k) for k in KEPT] + [
        VMEM(WHOLE, BF16), VMEM(wide, BF16), VMEM(tall, BF16), VMEM((768, 3072), BF16), VMEM((3072, 768), BF16),
        VMEM(plane, BF16), VMEM((48, 768), BF16), VMEM((2, *plane), BF16), VMEM((2, *plane), BF16),
        VMEM(plane, BF16), VMEM(plane, BF16),
        VMEM((768, 768), BF16), VMEM((768, 768), BF16), VMEM(wide, BF16), VMEM(wide, BF16),
        pltpu.SemaphoreType.DMA((72,)),
    ] + semaphores(16) * 4 + semaphores(2) + [VMEM(wide if first else none, BF16)] + bufs
    args = [(VMEM, a) for a in small] + [(ANY, a) for a in large]
    return call(functools.partial(trade_kernel, first_step, number), outs, scratch, collective_id, args)


FETCHED = (0, 1, 2, 4)


def back_body(step, refs, scratch, copies, block_out, grad_out, grads, begin, ready):
    (x, og, ids, pe), whole_hbm, kept, ret, frozen = refs[:4], refs[4], list(refs[5:12]), refs[12], refs[13]
    whole, buffers = scratch[0], scratch[1:5]
    loads = [copies.start(whole_hbm, whole)]
    for at, buffer in zip(FETCHED, buffers):
        loads.append(copies.start(kept[at], buffer))
        kept[at] = buffer

    def arrived():
        begin()
        for copy in loads:
            copy.wait()

    return back_part(
        x.at[step], og.at[step], ids.at[step], pe, whole, *kept, ret, frozen, block_out, grad_out, grads, arrived, ready
    )


BACK_SCRATCH = [VMEM(WHOLE, BF16)] + [VMEM(*KEPT[at]) for at in FETCHED] + [VMEM(WHOLE, BF16), pltpu.SemaphoreType.DMA((16,))]


def renew_kernel(number, *refs):
    shared, (p_in, mv_in, pe_in, mve_in), refs = refs[:14], refs[14:18], refs[18:]
    (block_out, grad_out, whole, p_out, mv_out, pe_out, mve_out), refs = refs[:7], refs[7:]
    back_scratch, (grads, sems), refs = refs[:5], refs[5:7], refs[7:]
    scratch, (sends, recvs) = refs[:11], refs[11:]
    place = Place()
    partners = ring_partners(place)
    hail(partners)
    links = Links(sends, recvs)
    reduction = Reduction(links, place, grads, scratch)
    extra = back_body(
        0, shared, back_scratch, Copies(sems), block_out, grad_out, grads, lambda: await_hails(partners), reduction.start
    )
    renew_part(number, place, links, reduction, extra, p_in, mv_in, pe_in, mve_in,
               whole, p_out, mv_out, pe_out, mve_out)
    links.finish()


def final_kernel(number, *refs):
    shared, dense, refs = refs[:14], refs[14:20], refs[20:]
    deltas, others, refs = refs[:2], refs[2:4], refs[4:]
    (block_out, grad_out, mean_out, flat_out, turned_out, expert_out), refs = refs[:6], refs[6:]
    back_scratch, (grads, sems), refs = refs[:5], refs[5:7], refs[7:]
    scratch, boxes, refs = refs[:11], refs[11:15], refs[15:]
    expert_scratch, (sends, recvs) = refs[:4], refs[4:]
    place = Place()
    partners = ring_partners(place) + [place.in_group(k, step) for k in (1, 2, 3) for step in range(4)]
    hail(partners)
    copies, links = Copies(sems), Links(sends, recvs)
    experts = ExpertMean(links, place, copies, deltas, others, *expert_scratch)

    def begin():
        await_hails(partners)
        experts.start()

    reduction = Reduction(links, place, grads, scratch)
    extra = back_body(1, shared, back_scratch, copies, block_out, grad_out, grads, begin, reduction.start)
    final_part(
        number, place, links, reduction, extra, *dense, mean_out, flat_out, turned_out, *boxes
    )
    for k in range(2):
        expert_out[k] = experts.mean(k)
    links.finish()


def finish_kernel(*refs):
    given, refs = refs[:16], refs[16:]
    olds, refs = refs[:4], refs[4:]
    (block, grad, new_qkv, new_proj, new_mom_qkv, new_mom_proj, new_gains, new_router, new_mom_gains, new_mom_router,
     *news), (old_buf, new_buf, sems, *held) = refs[:14], refs[14:]
    copies = Copies(sems)
    rows = [copies.start(src, dst) for src, dst in zip(given, held)]
    loads = [copies.start(src, old_buf.at[n]) for n, src in enumerate(olds)]
    for copy in rows:
        copy.wait()
    (block0, block1, grad0, grad1, mean, flat_e, turned_e, experts,
     w_qkv, w_proj, mom_qkv, mom_proj, gains, router, mom_gains, mom_router) = held
    stores = []
    for k in range(2):
        for copy in loads[2 * k : 2 * k + 2]:
            copy.wait()
        new_buf[2 * k], new_buf[2 * k + 1] = outer(old_buf[2 * k], old_buf[2 * k + 1], experts[k])
        stores += [copies.start(new_buf.at[n], news[n]) for n in (2 * k, 2 * k + 1)]
    for n, (one, all_rows) in enumerate(((block0, block), (block1, block), (grad0, grad), (grad1, grad))):
        all_rows[n % 2] = one[...]
    new_gains[...], new_mom_gains[...] = outer(gains[...], mom_gains[...], flat_e[17:19])
    new_router[...], new_mom_router[...] = outer(router[...], mom_router[...], turned_e[:, :17])
    for c in range(3):
        lanes = slice(768 * c, 768 * c + 768)
        new_qkv[:, lanes], new_mom_qkv[:, lanes] = outer(w_qkv[:, lanes], mom_qkv[:, lanes], mean[c])
    new_proj[...], new_mom_proj[...] = outer(w_proj[...], mom_proj[...], mean[3])
    for copy in stores:
        copy.wait()


def finish_call(small, olds):
    part = (192, 1536)
    outs = [((2, *ROW), BF16), ((2, *ROW), F32), ((24, 2304), F32), ((24, 768), F32), ((24, 2304), F32), ((24, 768), F32),
            ((2, 24), F32), ((24, 17), F32), ((2, 24), F32), ((24, 17), F32)]
    return pl.pallas_call(
        finish_kernel,
        out_shape=tuple(jax.ShapeDtypeStruct(*out) for out in outs + [(part, F32)] * 4),
        in_specs=[pl.BlockSpec(memory_space=ANY)] * (len(small) + 4),
        out_specs=tuple([pl.BlockSpec(memory_space=VMEM)] * 10 + [pl.BlockSpec(memory_space=ANY)] * 4),
        scratch_shapes=[VMEM((4, *part), F32), VMEM((4, *part), F32), pltpu.SemaphoreType.DMA((24,))]
        + [VMEM(array.shape, array.dtype) for array in small],
        compiler_params=pltpu.CompilerParams(vmem_limit_bytes=60 << 20),
    )(*small, *olds)


def back_args(small, whole, kept, ret, frozen):
    args = [(VMEM, a) for a in small] + [(ANY, whole)]
    args += [(ANY if at in FETCHED else VMEM, a) for at, a in enumerate(kept)]
    return args + [(VMEM, ret), (VMEM, frozen)]


def renew_call(number, shared, *args):
    return call(
        functools.partial(renew_kernel, number),
        [(VMEM, ROW, BF16), (VMEM, ROW, F32), (VMEM, WHOLE, BF16), (VMEM, BLOCK, F32), (VMEM, (2, *BLOCK), F32),
         (VMEM, (24, 768), F32), (VMEM, (2, 24, 768), F32)],
        BACK_SCRATCH + REDUCE_SCRATCH + semaphores(REDUCE_COPIES + GATHER_COPIES), 2,
        back_args(*shared) + [(VMEM, a) for a in args],
    )


def final_call(number, shared, dense, deltas):
    box = VMEM((4, 24, 768), F32)
    part = (192, 1536)
    boxes = [box, box, VMEM((24, 768), F32), VMEM((4, 48, 384), BF16)]
    return call(
        functools.partial(final_kernel, number),
        [(VMEM, ROW, BF16), (VMEM, ROW, F32), (VMEM, (4, 24, 768), F32), (VMEM, (24, 24), F32), (VMEM, (24, 24), F32),
         (VMEM, (2, *part), F32)],
        BACK_SCRATCH + REDUCE_SCRATCH + boxes
        + [VMEM((2, 2, *part), BF16), VMEM((2, 2, *part), BF16), VMEM((2, *part), BF16), VMEM((2, *part), BF16)]
        + semaphores(REDUCE_COPIES + 3 + 3 + 4 + 2),
        3,
        back_args(*shared) + [(VMEM, a) for a in dense] + [(ANY, a) for a in deltas],
    )


def body(
    tokens,
    out_grad,
    expert_ids,
    replay,
    frozen_in,
    frozen_out,
    gains,
    w_qkv,
    w_proj,
    router,
    exp_in,
    exp_out,
    mom_gains,
    mom_qkv,
    mom_proj,
    mom_router,
    mom_in,
    mom_out,
    state_gains,
    state_qkv,
    state_proj,
    state_router,
    state_in,
    state_out,
):
    gap = jnp.zeros((24, 5), F32)
    packed = jnp.concatenate(
        [router, gains.T, gap, state_router[0, 0], state_gains[0, 0].T, gap, state_router[0, 1], state_gains[0, 1].T,
         jnp.zeros((24, 61), F32)], axis=1,
    )
    ids = jnp.concatenate([jnp.swapaxes(expert_ids, 1, 2), replay[:, None], jnp.zeros((2, 5, 128), jnp.int32)], axis=1)
    turn = lambda array: jnp.swapaxes(array[0], 0, 1)
    back = lambda array: jnp.swapaxes(array, 0, 1)[None]
    whole, p_start, mv, pe_start, mve, both_low = entry_call(
        w_qkv, w_proj, state_qkv[0], state_proj[0], packed, exp_in[0], turn(exp_out)
    )
    frozen_both = (frozen_in[0], frozen_out[0])
    small = (tokens, out_grad, ids, pe_start)
    made = trade_call(
        True, STEP, 4, small, whole, both_low, *frozen_both, state_in[0, :, 0], state_out[0, :, 0]
    )
    shared = (small, whole, made[:7], made[7], made[8])
    block0, grad0, whole, p_now, mv, pe_now, mve = renew_call(STEP, shared, p_start, mv, pe_start, mve)
    small = (tokens, out_grad, ids, pe_now)
    made = trade_call(False, STEP + 1, 5, small, whole, both_low, made[13], *made[9:11], *frozen_both, *made[11:13])
    shared = (small, whole, made[:7], made[7], made[8])
    dense = (p_now, mv, pe_now, mve, p_start, pe_start)
    block1, grad1, *means = final_call(STEP + 1, shared, dense, made[9:13])
    (block, grad, new_qkv, new_proj, new_mom_qkv, new_mom_proj, new_gains, new_router, new_mom_gains, new_mom_router,
     new_in, new_mom_in, new_out, new_mom_out) = finish_call(
        (block0, block1, grad0, grad1, *means, w_qkv, w_proj, mom_qkv, mom_proj, gains, router, mom_gains, mom_router),
        (exp_in[0], mom_in[0], turn(exp_out), turn(mom_out)),
    )
    return (
        block, grad, new_gains, new_qkv, new_proj, new_router, new_in[None], back(new_out),
        new_mom_gains, new_mom_qkv, new_mom_proj, new_mom_router, new_mom_in[None], back(new_mom_out),
    )


def solution(mesh):
    return jax.shard_map(
        body,
        mesh=mesh,
        in_specs=(
            P(None, ("group", "dp", "expert"), None),
            P(None, ("group", "dp", "expert"), None),
            P(None, ("group", "dp", "expert"), None),
            P(None, ("group", "dp", "expert")),
            P(),
            P(),
            P(None, ("dp", "expert")),
            P(("dp", "expert"), None),
            P(("dp", "expert"), None),
            P(("dp", "expert"), None),
            P("expert", "group", "dp"),
            P("expert", "dp", "group"),
            P(None, ("dp", "expert")),
            P(("dp", "expert"), None),
            P(("dp", "expert"), None),
            P(("dp", "expert"), None),
            P("expert", "group", "dp"),
            P("expert", "dp", "group"),
            P("group", None, None, ("dp", "expert")),
            P("group", None, ("dp", "expert"), None),
            P("group", None, ("dp", "expert"), None),
            P("group", None, ("dp", "expert"), None),
            P("group", None, "expert", None, "dp"),
            P("group", None, "expert", "dp", None),
        ),
        out_specs=(
            P(None, ("group", "dp", "expert"), None),
            P(None, ("group", "dp", "expert"), None),
            P(None, ("dp", "expert")),
            P(("dp", "expert"), None),
            P(("dp", "expert"), None),
            P(("dp", "expert"), None),
            P("expert", "group", "dp"),
            P("expert", "dp", "group"),
            P(None, ("dp", "expert")),
            P(("dp", "expert"), None),
            P(("dp", "expert"), None),
            P(("dp", "expert"), None),
            P("expert", "group", "dp"),
            P("expert", "dp", "group"),
        ),
        check_vma=False,
    )
```

```python
import functools

import jax
import jax.numpy as jnp
from jax import lax
from jax.experimental import pallas as pl
from jax.experimental.pallas import tpu as pltpu
from jax.sharding import PartitionSpec as P

MESH = pl.DeviceIdType.MESH
VMEM = pltpu.VMEM
F32 = jnp.float32
BF16 = jnp.bfloat16


class Links:
    def __init__(self, sends, recvs):
        self.sends, self.recvs, self.used, self.begun = sends, recvs, 0, []

    def send(self, src, dst, to):
        at = self.used
        self.used += 1
        copy = pltpu.make_async_remote_copy(
            src_ref=src, dst_ref=dst, send_sem=self.sends.at[at], recv_sem=self.recvs.at[at],
            device_id=to, device_id_type=MESH,
        )
        self.begun.append(copy)
        copy.start()
        return copy

    def finish(self):
        for copy in self.begun:
            copy.wait_send()


class Place:
    def __init__(self):
        self.g, self.d = lax.axis_index("group"), lax.axis_index("dp")
        e = lax.axis_index("expert")
        self.x, self.y = lax.div(e, 4), lax.rem(e, 4)

    def along_x(self, step, over=0):
        return {"dp": lax.rem(self.d + over, 2), "expert": lax.rem(self.x + step, 4) * 4 + self.y}

    def along_y(self, step, over=0):
        return {"dp": lax.rem(self.d + over, 2), "expert": self.x * 4 + lax.rem(self.y + step, 4)}

    def other_dp(self):
        return {"dp": 1 - self.d}

    def in_group(self, step, along=0, over=0):
        return {"group": lax.rem(self.g + step, 4), **self.along_y(along, over)}

    def other_core(self):
        return {"group": self.g + 1 - 2 * lax.rem(self.g, 2)}


def hail(partners):
    barrier = pltpu.get_barrier_semaphore()
    for partner in partners:
        pl.semaphore_signal(barrier, inc=1, device_id=partner, device_id_type=MESH)


def await_hails(partners):
    pl.semaphore_wait(pltpu.get_barrier_semaphore(), len(partners))


PEERS = ((0, 1), (1, 0), (3, 0), (1, 1), (3, 1), (2, 0), (2, 1))


def ring_partners(place):
    return (
        [place.along_x(*peer) for peer in PEERS]
        + [place.along_y(step) for step in (1, 2, 3)]
        + [place.along_y(step, 1) for step in (1, 2, 3)]
    )


class Gather:
    def __init__(self, links, whole, h, p1, p2, near1, near2, at, share=None):
        self.links, self.whole, self.h, self.at = links, whole, h, at
        self.p1, self.p2, self.near1, self.near2, self.share = p1, p2, near1, near2, share
        self.steps, self.shared, self.round, self.passed = (0, 1, 3, 2), [], [], []

    def push(self, n, k2, to):
        c, x = self.at(lax.rem(self.p1 + 4 - self.steps[n], 4), lax.rem(k2, 4))
        ref = self.whole.at[c, x, self.h]
        return self.links.send(ref, ref, to)

    def give(self, n, k2):
        if self.share is not None:
            self.shared.append(self.push(n, k2, self.share))

    def start(self):
        self.direct = [self.push(0, self.p2, self.near1(step)) for step in self.steps[1:]]
        self.ring(0)

    def ring(self, n):
        if n:
            self.direct[n - 1].wait_recv()
        self.round.append([self.push(n, self.p2, self.near2(step)) for step in (1, 3)])
        self.give(n, self.p2)

    def forward(self, n):
        right, left = self.round[n]
        right.wait_recv()
        if n % 2 == 0:
            self.passed.append(self.push(n, self.p2 + 3, self.near2(1)))
        self.give(n, self.p2 + 3)
        left.wait_recv()
        if n % 2 == 1:
            self.passed.append(self.push(n, self.p2 + 1, self.near2(3)))
        self.give(n, self.p2 + 1)

    def end(self):
        for n, copy in enumerate(self.passed):
            copy.wait_recv()
            self.give(n, self.p2 + 2)
        for copy in self.shared:
            copy.wait_recv()


def run_gather(parts):
    for n in range(1, 6):
        for part in parts:
            if n < 4:
                part.ring(n)
            if n >= 2:
                part.forward(n - 2)
    for part in parts:
        part.end()


def gather_parts(links, place, whole):
    by_x = lambda kx, ky: (ky, kx)
    by_y = lambda ky, kx: (ky, kx)
    first = Gather(links, whole, 0, place.x, place.y, place.along_x, place.along_y, by_x)
    second = Gather(links, whole, 1, place.y, place.x, place.along_y, place.along_x, by_y)
    return first, second


class RingSum:
    def __init__(self, links, near1, near2, p1, p2, term, far, near, mid, box):
        self.links, self.near1, self.near2, self.p1, self.p2 = links, near1, near2, p1, p2
        self.term, self.far, self.near, self.mid, self.box = term, far, near, mid, box
        self.steps = (2, 1, 3, 0)
        self.far_copies, self.direct, self.summed, self.over = [], [], [], []

    def get(self, k, i):
        return self.term(lax.rem(self.p1 + k, 4), lax.rem(self.p2 + self.steps[i], 4))

    def send_far(self, i):
        self.far_copies.append(self.links.send(self.get(2, i), self.far.at[i], self.near1((1, 3)[i % 2])))

    def send_direct(self, i):
        step = (3, 1)[i % 2]
        self.direct.append(self.links.send(self.get(step, i), self.near.at[1, i], self.near1(step)))

    def middle(self, i):
        step = (1, 3)[i % 2]
        self.far_copies[i].wait_recv()
        self.far[i] = (self.far[i].astype(F32) + self.get(step, i)[...].astype(F32)).astype(BF16)
        self.summed.append(self.links.send(self.far.at[i], self.near.at[0, i], self.near1(step)))

    def finish(self, i):
        self.direct[i].wait_recv()
        self.summed[i].wait_recv()
        self.mid[i] = (
            self.get(0, i)[...].astype(F32) + self.near[0, i].astype(F32) + self.near[1, i].astype(F32)
        ).astype(BF16)
        step = self.steps[i]
        if step:
            self.over.append(self.links.send(self.mid.at[i], self.box.at[self.p2], self.near2(step)))
        else:
            self.box[self.p2] = self.mid[i]

    def total(self):
        for copy in self.over:
            copy.wait_recv()
        value = self.box[0].astype(F32)
        for k in range(1, 4):
            value = value + self.box[k].astype(F32)
        return value


def folded(rows):
    return jnp.concatenate([rows[:, :384], rows[:, 384:]], axis=0).astype(BF16)


def unfolded(rows):
    return jnp.concatenate([rows[:24], rows[24:]], axis=1)


def add_over(links, own, box, position, size, reach):
    box[position] = folded(own)
    copies = [links.send(box.at[position], box.at[position], reach(step)) for step in range(1, size)]

    def finish():
        for copy in copies:
            copy.wait_recv()
        total = box[0].astype(F32)
        for k in range(1, size):
            total = total + box[k].astype(F32)
        return unfolded(total)

    return finish


PIECES = (4, 48, 768)
HALF_SCRATCH = [VMEM(PIECES, BF16), VMEM((2, *PIECES), BF16), VMEM(PIECES, BF16), VMEM(PIECES, BF16)]
REDUCE_SCRATCH = HALF_SCRATCH * 2 + [VMEM((4, 48, 384), BF16), VMEM((4, 48, 384), BF16), VMEM((2, 48, 384), BF16)]
REDUCE_COPIES = 2 * 15 + 7
GATHER_COPIES = 2 * 15


class Reduction:
    def __init__(self, links, place, grads, scratch):
        self.links, self.place, self.boxes = links, place, scratch[8:]
        self.parts = (
            RingSum(
                links, place.along_y, place.along_x, place.y, place.x, lambda k, j: grads.at[k, j, 0], *scratch[:4]
            ),
            RingSum(
                links, place.along_x, place.along_y, place.x, place.y, lambda k, j: grads.at[j, k, 1], *scratch[4:8]
            ),
        )

    def start(self):
        for i in range(4):
            for part in self.parts:
                part.send_far(i)
        for part in self.parts:
            part.send_direct(0)

    def finish(self, extra):
        links, place, parts = self.links, self.place, self.parts
        box_x, box_y, box_z = self.boxes
        extra_x = add_over(links, extra, box_x, place.x, 4, place.along_x)
        for i in range(4):
            for part in parts:
                if i:
                    part.send_direct(i)
                part.middle(i)
            if i == 1:
                extra_y = add_over(links, extra_x(), box_y, place.y, 4, place.along_y)
            if i == 3:
                extra_z = add_over(links, extra_y(), box_z, place.d, 2, lambda step: place.other_dp())
        for i in range(4):
            for part in parts:
                part.finish(i)
        return [part.total() for part in parts], extra_z()


EPS_NORM = 1e-06
BETA_ONE = 0.9
BETA_TWO = 0.95
ADAM_EPS = 1e-08
DECAY = 0.1
OUTER_RATE = 0.7
OUTER_MOMENTUM = 0.9
REPLAY_WEIGHT = 0.25
RATES = (0.6, 0.04, 0.3, 0.03, 0.04, 0.02)
HEADS = 12
LEN = 128
STEPS = 2
STEP = 10


PIECE = 32


class ExpertGather:
    def __init__(self, links, place, own, both):
        self.links, self.place, self.own, self.both = links, place, own, both
        self.far, self.near = [], []

    def rows(self, group, n=None):
        if n is None:
            return self.both.at[pl.ds(pl.multiple_of(group * 192, 192), 192)]
        return self.both.at[pl.ds(pl.multiple_of(group * 192 + n * PIECE, PIECE), PIECE)]

    def send(self, n):
        part = self.own.at[pl.ds(n * PIECE, PIECE)]
        self.far.append(self.links.send(part, self.rows(self.place.g, n), self.place.in_group(2)))

    def share(self):
        self.near.append(self.links.send(self.own, self.rows(self.place.g), self.place.other_core()))

    def pass_on(self, n):
        self.far[n].wait_recv()
        ref = self.rows(lax.rem(self.place.g + 2, 4), n)
        self.near.append(self.links.send(ref, ref, self.place.other_core()))

    def end(self):
        for copy in self.near:
            copy.wait_recv()


def halves(rows):
    return jnp.concatenate([rows[:, :384], rows[:, 384:]], axis=0)


def deal(links, place, src, box):
    box[place.d, place.y] = src[place.y, place.d]
    return [
        links.send(
            src.at[lax.rem(place.y + step, 4), lax.rem(place.d + over, 2)], box.at[place.d, place.y],
            place.along_y(step, over),
        )
        for step, over in PEERS
    ]


def assembled(place, box):
    upper, lower = box[:, :, :24], box[:, :, 24:]
    columns = jnp.concatenate([upper[0], upper[1]], axis=-1)
    rows = jnp.concatenate([upper, lower], axis=-1)
    rows = jnp.where(place.d == 0, rows[0], rows[1])
    return jnp.where(place.y == 3, rows, columns).reshape(2, 48, 768)


def dealt(wide, square, c, dp):
    if c < 3:
        return jnp.concatenate([wide[:, 768 * c + 384 * dp : 768 * c + 384 * dp + 384]] * 2, axis=0)
    return halves(square)


def entry_part(place, links, tokens, w_qkv, w_proj, e_in, in_hbm, out_hbm, whole, p_out, pe_out, mve_out, x_pair, both,
               p_in, own, loaded, e_out, p_box, local_sems, partners):
    loads = [
        pltpu.make_async_copy(
            src.at[pl.ds(128 * part, size)], loaded.at[k, part, pl.ds(0, size)], local_sems.at[2 * k + part]
        )
        for k, src in enumerate((in_hbm, out_hbm))
        for part, size in ((0, 128), (1, 64))
    ]
    for copy in loads:
        copy.start()
    for c in range(4):
        for dp in range(2):
            p_in[c, dp] = dealt(w_qkv, w_proj[...], c, dp).astype(BF16)
    await_hails(partners)
    x, y, d = place.x, place.y, place.d
    h = lax.rem(place.g, 2)
    masters = deal(links, place, p_in, p_box)
    e_out[d, x, y] = e_in[...]
    mine = e_out.at[d, x, y]
    extra_z = links.send(mine, mine, place.other_dp())
    pair = links.send(tokens.at[0], x_pair, place.other_dp())
    for k in range(2):
        for part, size in ((0, 128), (1, 64)):
            loads[2 * k + part].wait()
            own[128 * part : 128 * part + size, 1536 * k : 1536 * k + 1536] = loaded[k, part, :size].astype(BF16)
    experts = ExpertGather(links, place, own, both)
    mine_there = pltpu.make_async_copy(own, experts.rows(place.g), local_sems.at[4])
    mine_there.start()
    for n in range(192 // PIECE):
        experts.send(n)
    for copy in masters:
        copy.wait_recv()
    master = assembled(place, p_box[...].astype(F32))
    p_out[...] = master

    @pl.when(h == 0)
    def _():
        whole[y, x, 0] = master[0].astype(BF16)

    @pl.when(h == 1)
    def _():
        whole[y, x, 1] = master[1].astype(BF16)

    def mix(a, b):
        return a * (1 - h) + b * h

    def near1(step, over=0):
        one, two = place.along_x(step, over), place.along_y(step, over)
        return {"dp": one["dp"], "expert": mix(one["expert"], two["expert"])}

    def near2(step):
        one, two = place.along_y(step), place.along_x(step)
        return {"dp": one["dp"], "expert": mix(one["expert"], two["expert"])}

    def at(k1, k2):
        return mix(k2, k1), mix(k1, k2)

    part = Gather(links, whole, h, mix(x, y), mix(y, x), near1, near2, at, place.other_core())
    part.start()
    extra_z.wait_recv()
    mine = e_out.at[:, x, y]
    extra_x = [links.send(mine, mine, place.along_x(k)) for k in (1, 2, 3)]
    for n in (1, 2, 3):
        part.ring(n)
        part.forward(n - 1)
    for copy in extra_x:
        copy.wait_recv()
    mine = e_out.at[:, :, y]
    extra_y = [links.send(mine, mine, place.along_y(k)) for k in (1, 2, 3)]
    part.forward(3)
    part.end()
    experts.share()
    for copy in extra_y:
        copy.wait_recv()
    turned = e_out[...].reshape(768, 128).T
    pe_out[...] = turned[:24]
    mve_out[0] = turned[24:48]
    mve_out[1] = turned[48:72]
    pair.wait_recv()

    def end():
        experts.end()
        mine_there.wait()

    return experts, end


def adam_values(master, first, second, grad, rate, number):
    first = BETA_ONE * first + (1.0 - BETA_ONE) * grad
    second = BETA_TWO * second + (1.0 - BETA_TWO) * grad * grad
    level = second * (1.0 / (1.0 - BETA_TWO**number))
    below = level * lax.rsqrt(jnp.maximum(level, 1e-30)) + ADAM_EPS
    guess = pl.reciprocal(below, approx=True)
    update = first * ((1.0 / (1.0 - BETA_ONE**number)) * rate) * (guess * (2.0 - below * guess))
    return master - (update + (rate * DECAY) * master), first, second


def block_rate(place):
    return jnp.where(place.y == 3, RATES[2], RATES[1]).astype(F32)


def extra_rates():
    row = lax.broadcasted_iota(jnp.int32, (24, 768), 0)
    return jnp.where(row < 17, RATES[3], RATES[0]).astype(F32)


def renew_part(number, place, links, reduction, extra, moments, mv_box, p_in, pe_in, mve_in,
               whole, p_out, mv_out, pe_out, mve_out):
    sums, total = reduction.finish(extra)
    parts = gather_parts(links, place, whole)
    for copy in moments:
        copy.wait_recv()
    moment = mv_box[...].astype(F32)
    old = [assembled(place, moment[:, :, 48 * k : 48 * k + 48]) for k in range(2)]
    for h, part in enumerate(parts):
        fresh, first, second = adam_values(p_in[h], old[0][h], old[1][h], sums[h], block_rate(place), number)
        whole[place.y, place.x, h] = fresh.astype(BF16)
        part.start()
        p_out[h] = fresh
        mv_out[0, h] = first
        mv_out[1, h] = second
    pe_out[...], mve_out[0], mve_out[1] = adam_values(pe_in[...], mve_in[0], mve_in[1], total, extra_rates(), number)
    run_gather(parts)


def outer(begin, moment, mean):
    renewed = OUTER_MOMENTUM * moment + mean
    return begin - OUTER_RATE * (mean + OUTER_MOMENTUM * renewed), renewed


def own_features(place, rows, turned):
    at = 24 * (16 * place.d + 4 * place.x + place.y)
    pick = (lax.broadcasted_iota(jnp.int32, (768, 24), 0) == at + lax.broadcasted_iota(jnp.int32, (768, 24), 1)).astype(BF16)
    total = 0.0
    for _ in range(3):
        part = rows.astype(BF16)
        total = total + (
            lax.dot_general(pick, part, (((0,), (1,)), ((), ())), preferred_element_type=F32) if turned
            else lax.dot_general(part, pick, (((1,), (0,)), ((), ())), preferred_element_type=F32)
        )
        rows = rows - part.astype(F32)
    return total


class ExpertMean:
    def __init__(self, links, place, copies, deltas, others, own, other, sent, far):
        self.links, self.place, self.own, self.other, self.sent, self.far = links, place, own, other, sent, far
        self.high = lax.div(place.g, 2)
        self.loads = [copies.start(delta.at[:, lax.rem(place.g, 2)], own.at[k]) for k, delta in enumerate(deltas)]
        self.loads += [copies.start(array, other.at[k]) for k, array in enumerate(others)]

    def start(self):
        for copy in self.loads:
            copy.wait()
        self.copies = []
        for k in range(2):
            self.sent[k] = (
                self.own[k, 1 - self.high].astype(F32) + self.other[k, 1 - self.high].astype(F32)
            ).astype(BF16)
            self.copies.append(self.links.send(self.sent.at[k], self.far.at[k], self.place.in_group(2)))

    def mean(self, k):
        self.copies[k].wait_recv()
        mine = self.own[k, self.high].astype(F32) + self.other[k, self.high].astype(F32)
        return (mine + self.far[k].astype(F32)) * 0.25


def final_part(number, place, links, reduction, extra, p_in, mv_in, pe_in, mve_in, p_start, pe_start,
               mean_out, flat_out, turned_out, turned, delta, quarters, mean, boxes):
    g, y = place.g, place.y
    sums, total = reduction.finish(extra)
    for h in range(2):
        fresh, _, _ = adam_values(p_in[h], mv_in[0, h], mv_in[1, h], sums[h], block_rate(place), number)
        rows = (p_start[h] - fresh).reshape(2, 24, 768)
        for k in range(2):
            delta[2 * h + k] = folded(rows[k])
    summed = [
        links.send(delta.at[lax.rem(g + k, 4)], quarters.at[g], place.in_group(k)) for k in (1, 2, 3)
    ]
    fresh_e, _, _ = adam_values(pe_in[...], mve_in[0], mve_in[1], total, extra_rates(), number)
    sum_e = add_over(links, pe_start[...] - fresh_e, boxes, g, 4, place.in_group)
    quarters[g] = delta[g]
    for copy in summed:
        copy.wait_recv()
    mean[...] = (
        (quarters[0].astype(F32) + quarters[1].astype(F32) + quarters[2].astype(F32) + quarters[3].astype(F32)) * 0.25
    ).astype(BF16)
    d, at = place.d, links.used
    links.used += 8

    def spread(k, over):
        return pltpu.make_async_remote_copy(
            src_ref=mean, dst_ref=turned.at[d, y], send_sem=links.sends.at[at + 2 * k + over],
            recv_sem=links.recvs.at[at + 2 * y + d],
            device_id={"group": lax.rem(g + k, 4), "dp": lax.rem(d + over, 2), "expert": place.x * 4 + g},
            device_id_type=MESH,
        )

    def arrival(dp, c):
        return pltpu.make_async_remote_copy(
            src_ref=mean, dst_ref=turned.at[dp, c], send_sem=links.sends.at[at], recv_sem=links.recvs.at[at + 2 * c + dp],
            device_id=place.other_core(), device_id_type=MESH,
        )

    others = [(k, over) for k in range(4) for over in range(2) if k or over]
    for k, over in others:
        spread(k, over).start()

    @pl.when(y != g)
    def _():
        spread(0, 0).start()

    @pl.when(y == g)
    def _():
        turned[d, y] = mean[...]

    mean_e = sum_e() * 0.25
    flat_out[...] = own_features(place, mean_e, False)
    turned_out[...] = own_features(place, mean_e, True)
    for dp in range(2):
        for c in range(4):
            @pl.when(jnp.logical_or(y != g, jnp.logical_or(c != y, dp != d)))
            def _(c=c, dp=dp):
                arrival(dp, c).wait_recv()

    for k, over in others:
        spread(k, over).wait_send()

    @pl.when(y != g)
    def _():
        spread(0, 0).wait_send()

    landed = turned[...].astype(F32)
    upper, lower = landed[:, :, :24], landed[:, :, 24:]
    for c in range(3):
        mine = jnp.where(d == 0, upper[:, c], lower[:, c])
        mean_out[c] = jnp.concatenate([mine[0], mine[1]], axis=-1)
    rows = jnp.concatenate([upper[:, 3], lower[:, 3]], axis=-1)
    mean_out[3] = jnp.where(d == 0, rows[0], rows[1])


def semaphores(count):
    return [pltpu.SemaphoreType.DMA((count,)), pltpu.SemaphoreType.DMA((count,))]


ANY = pl.ANY
WHOLE = (4, 4, 2, 48, 768)
BLOCK = (2, 48, 768)
ROW = (128, 768)


def call(kernel, outs, scratch, collective_id, args, limit=60 << 20):
    return pl.pallas_call(
        kernel,
        out_shape=tuple(jax.ShapeDtypeStruct(shape, kind) for _, shape, kind in outs),
        in_specs=[pl.BlockSpec(memory_space=space) for space, _ in args],
        out_specs=tuple(pl.BlockSpec(memory_space=space) for space, _, _ in outs),
        scratch_shapes=scratch,
        compiler_params=pltpu.CompilerParams(
            collective_id=collective_id, has_side_effects=True, vmem_limit_bytes=limit
        ),
    )(*(array for _, array in args))

CAP = 24
TOK = 128
DIMS = {"nn": (((1,), (0,)), ((), ())), "nt": (((1,), (1,)), ((), ())), "tn": (((0,), (0,)), ((), ()))}


def mm(a, b, form="nn"):
    return lax.dot_general(a, b, DIMS[form], preferred_element_type=F32)


def split_low(values):
    high = values.astype(BF16)
    return high, (values - high.astype(F32)).astype(BF16)


def row_scale(values):
    return lax.rsqrt(jnp.mean(values * values, axis=-1, keepdims=True) + EPS_NORM)


def iota(shape, dim):
    return lax.broadcasted_iota(jnp.int32, shape, dim)


def routing(ids):
    names = [(iota((24, TOK), 0) == ids[k : k + 1]).astype(F32) for k in range(2)]
    either = names[0] + names[1]
    earlier = (iota((TOK, TOK), 0) < iota((TOK, TOK), 1)).astype(BF16)
    slot = mm(either.astype(BF16), earlier).astype(jnp.int32)
    taken = jnp.where(iota((17, CAP, TOK), 1) == slot[:17][:, None, :], 1.0, 0.0)
    return names, taken * either[:17][:, None, :]


def pair_stack(part):
    lane = iota(part.shape, 1)
    zero = jnp.zeros_like(part)
    return jnp.concatenate([jnp.where(lane < 64, part, zero), jnp.where(lane < 64, zero, part)], axis=0)


def side_by_side(stacked):
    return jnp.concatenate([stacked[:TOK], stacked[TOK:]], axis=1)


def flat(whole, c):
    return whole[c].reshape(384, 768)


def cotangent(og_ref, ids_ref):
    factor = jnp.where(ids_ref[2:3] > 0, REPLAY_WEIGHT, 1.0)
    spread = jnp.where(iota((TOK, TOK), 0) == iota((TOK, TOK), 1), factor, 0.0).astype(BF16)
    return mm(spread, og_ref[...])


def across(rows, weight):
    return mm(rows[:, :384], weight[:, :384]) + mm(rows[:, 384:], weight[:, 384:])


def front_part(x_ref, pair_ref, og_ref, ids_ref, pe_ref, whole,
               send, frozen, qkv_out, probs_out, mixed_out, middle_out, a1_out, a2_out, weights_out, swap):
    gain = pe_ref[16:24].astype(BF16).astype(F32)
    row, col = iota((2 * TOK, TOK), 0), iota((2 * TOK, TOK), 1)
    causal = lax.rem(row, TOK) >= col
    x = x_ref[...].astype(F32)
    finish = None
    for t, values in ((1, pair_ref[...].astype(F32)), (0, x)):
        a1 = (values * row_scale(values) * gain[1:2]).astype(BF16)
        a1_out[t] = a1
        for c in range(3):
            qkv_out[t, c] = across(a1, flat(whole, c)).astype(BF16)
        for pair in range(3):
            lanes = slice(128 * pair, 128 * pair + 128)
            scores = mm(pair_stack(qkv_out[t, 0, :, lanes]), qkv_out[t, 1, :, lanes], "nt") * 0.125
            scores = jnp.where(causal, scores, -1e30)
            expo = jnp.exp(scores - jnp.max(scores, axis=-1, keepdims=True))
            probs = expo / jnp.sum(expo, axis=-1, keepdims=True)
            probs_out[t, pair] = probs
            mixed_out[t, :, lanes] = mm(
                side_by_side(probs.astype(BF16)), pair_stack(qkv_out[t, 2, :, lanes])
            ).astype(BF16)
        branch = mm(mixed_out[t], flat(whole, 3))
        if t:
            finish = swap(branch.astype(BF16))
    middle = x + branch + finish()
    middle_out[...] = middle
    a2 = (middle * row_scale(middle) * gain[2:3]).astype(BF16)
    a2_out[...] = a2
    logits = mm(pe_ref[...].astype(BF16), a2, "nt")
    names, taken = routing(ids_ref[...])
    picked = [jnp.sum(name * logits, axis=0, keepdims=True) for name in names]
    top = jnp.maximum(picked[0], picked[1])
    expo = [jnp.exp(z - top) for z in picked]
    whole_sum = expo[0] + expo[1]
    weights = [e / whole_sum for e in expo]
    weights_out[...] = jnp.concatenate(weights + [jnp.zeros((6, TOK), F32)], axis=0)
    by_expert = names[0] * weights[0] + names[1] * weights[1]
    row_weight = jnp.sum(taken * by_expert[:17][:, None, :], axis=-1, keepdims=True)
    cot = cotangent(og_ref, ids_ref).astype(BF16)
    low = taken.astype(BF16).reshape(17 * CAP, TOK)
    rows = mm(low, a2).reshape(17, CAP, 768)
    grads = mm(low, cot).reshape(17, CAP, 768) * row_weight
    both = jnp.concatenate([rows, grads], axis=1).astype(BF16)
    frozen[...] = both[0]
    send[...] = both[1:]


def back_part(x_ref, og_ref, ids_ref, pe_ref, whole, qkv, probs_ref, mixed, middle_ref, a1, a2,
              weights_ref, ret, frozen, block_out, grad_out, grads, arrived, ready, swap, late):
    gain = pe_ref[16:24].astype(BF16).astype(F32)
    low_rows = pe_ref[...].astype(BF16)
    cot = cotangent(og_ref, ids_ref)
    names, taken = routing(ids_ref[...])
    weights = [weights_ref[k : k + 1] for k in range(2)]
    by_expert = names[0] * weights[0] + names[1] * weights[1]
    row_weight = jnp.sum(taken * by_expert[:17][:, None, :], axis=-1, keepdims=True)
    low = taken.astype(BF16).reshape(17 * CAP, TOK)
    both = ret[...].astype(F32)
    both = jnp.concatenate([frozen[...][None], both], axis=0)
    results, back = both[:, :CAP], both[:, CAP:].reshape(17 * CAP, 768)
    middle = middle_ref[...]
    cot_rows = mm(low, cot.astype(BF16)).reshape(17, CAP, 768)
    grad_row = jnp.sum(cot_rows * results, axis=-1, keepdims=True)
    by_name = jnp.concatenate([jnp.sum(taken * grad_row, axis=1), jnp.zeros((7, TOK), F32)], axis=0)
    grad_w = [jnp.sum(name * by_name, axis=0, keepdims=True) for name in names]
    mean = weights[0] * grad_w[0] + weights[1] * grad_w[1]
    grad_logits = sum(names[k] * (weights[k] * (grad_w[k] - mean)) for k in range(2))
    logit_parts = split_low(grad_logits)
    da2 = sum(mm(part, low_rows, "tn") for part in logit_parts)
    da2 = da2 + sum(mm(low, part, "tn") for part in split_low(back))
    scale = row_scale(middle)
    normed = middle * scale
    dg2 = jnp.sum(normed * da2, axis=0, keepdims=True)
    into = da2 * gain[2:3]
    dmiddle = cot + scale * (into - normed * jnp.mean(into * normed, axis=-1, keepdims=True))
    branch = dmiddle.astype(BF16)
    arrived()
    finish = swap(0, branch)
    branches = [branch]
    dqkv = [[], [], []]
    for t in range(2):
        if t:
            branches.append(finish())
        dmixed = mm(branches[t], flat(whole, 3), "nt").astype(BF16)
        parts = [[], [], []]
        for pair in range(3):
            lanes = slice(128 * pair, 128 * pair + 128)
            probs = probs_ref[t, pair]
            dms = pair_stack(dmixed[:, lanes])
            parts[2].append(mm(probs.astype(BF16), dms, "tn").astype(BF16))
            dpb = mm(dms, qkv[t, 2, :, lanes], "nt")
            ds = (probs * (dpb - jnp.sum(probs * dpb, axis=-1, keepdims=True))).astype(BF16)
            parts[0].append((mm(side_by_side(ds), pair_stack(qkv[t, 1, :, lanes])) * 0.125).astype(BF16))
            parts[1].append((mm(ds, pair_stack(qkv[t, 0, :, lanes]), "tn") * 0.125).astype(BF16))
        for c in range(3):
            dqkv[c].append(jnp.concatenate(parts[c], axis=1))
    a1_both = a1[...].reshape(2 * TOK, 768)
    for c in range(3):
        both = jnp.concatenate(dqkv[c], axis=0)
        grads[c] = jnp.concatenate(
            [mm(a1_both[:, :384], both, "tn"), mm(a1_both[:, 384:], both, "tn")], axis=1
        ).astype(BF16).reshape(4, 2, 48, 768)
    grads[3] = mm(
        mixed[...].reshape(2 * TOK, 384), jnp.concatenate(branches, axis=0), "tn"
    ).astype(BF16).reshape(4, 2, 48, 768)
    ready()

    def into_a1(t):
        halves_of = [
            sum(mm(dqkv[c][t], flat(whole, c)[:, side], "nt") for c in range(3))
            for side in (slice(0, 384), slice(384, 768))
        ]
        return jnp.concatenate(halves_of, axis=1)

    finish = swap(1, into_a1(1).astype(BF16))
    late()
    da1 = into_a1(0)
    grad_router = sum(mm(part, a2[...]) for part in logit_parts)
    block_out[...] = (
        middle + sum(mm(low, part, "tn") for part in split_low((results * row_weight).reshape(17 * CAP, 768)))
    ).astype(BF16)
    da1 = da1 + finish().astype(F32)
    x = x_ref[...].astype(F32)
    scale = row_scale(x)
    normed = x * scale
    dg1 = jnp.sum(normed * da1, axis=0, keepdims=True)
    into = da1 * gain[1:2]
    grad_out[...] = dmiddle + scale * (into - normed * jnp.mean(into * normed, axis=-1, keepdims=True))
    return jnp.concatenate([grad_router[:17], dg1, dg2, jnp.zeros((5, 768), F32)], axis=0)


SQRT_HALF = 0.7071067811865476
DENSITY = 0.3989422804014327


def expert_rows(rows, grad, first, second):
    u = mm(rows, first)
    chance = 0.5 + 0.5 * lax.erf(u * SQRT_HALF)
    h = (u * chance).astype(BF16)
    value = mm(h, second)
    slope = chance + u * (jnp.exp(u * u * -0.5) * DENSITY)
    du = (slope * mm(grad, second, "nt")).astype(BF16)
    return value, mm(du, first, "nt"), h, du


class Copies:
    def __init__(self, sems):
        self.sems, self.used = sems, 0

    def start(self, src, dst):
        copy = pltpu.make_async_copy(src, dst, self.sems.at[self.used])
        self.used += 1
        copy.start()
        return copy


def grow_experts(first_step, number, copies, rows, grad, h, du, w1, w2, mv1, mv2, starts, news, bufs, between):
    (mv1_buf, mv2_buf, d1_buf, d2_buf, w1_out, w2_out, mv1_out, mv2_out, d1_out, d2_out) = bufs
    tiles = [(0, t) for t in range(6)] + [(1, t) for t in range(6)]

    def cut(which, t):
        size = (128, 256)[which]
        return pl.ds(size * t, size), slice(None)

    def parts_of(t):
        begin, end = 128 * t, 128 * t + 128
        cuts = sorted({begin, end} | {192 * q for q in range(5) if begin < 192 * q < end})
        return [(low // 192, low % 192, high - low, low - begin) for low, high in zip(cuts, cuts[1:])]

    def load(n):
        which, t = tiles[n]
        slot = n % 2
        mv, buf = ((mv1, mv1_buf), (mv2, mv2_buf))[which]
        size = (128, 256)[which]
        begun = [copies.start(mv.at[:, pl.ds(size * t, size)], buf.at[slot])]
        if not first_step:
            begun.append(copies.start(starts[which].at[cut(which, t)], (d1_buf, d2_buf)[which].at[slot]))
        return begun

    loads = {0: load(0)}
    stores = {}
    for n, (which, t) in enumerate(tiles):
        slot = n % 2
        if n + 1 < len(tiles):
            loads[n + 1] = load(n + 1)
        for copy in loads[n]:
            copy.wait()
        for copy in stores.pop(n - 2, ()):
            copy.wait()
        if which == 0:
            value = mm(rows[:, 128 * t : 128 * t + 128], du[...], "tn")
            begin = w1[128 * t : 128 * t + 128].astype(F32)
            moments = mv1_buf
        else:
            value = mm(h[:, 256 * t : 256 * t + 256], grad[...], "tn")
            begin = w2[256 * t : 256 * t + 256].astype(F32)
            moments = mv2_buf
        fresh, first, second = adam_values(
            begin, moments[slot, 0].astype(F32), moments[slot, 1].astype(F32), value, RATES[4 + which], number
        )
        here = cut(which, t)
        if first_step:
            low, mv_low = (w1_out, w2_out)[which], (mv1_out, mv2_out)[which]
            low[slot] = fresh.astype(BF16)
            mv_low[slot, 0] = first.astype(BF16)
            mv_low[slot, 1] = second.astype(BF16)
            size = (128, 256)[which]
            stores[n] = [
                copies.start(low.at[slot], news[which].at[here]),
                copies.start(mv_low.at[slot], news[2 + which].at[:, pl.ds(size * t, size)]),
            ]
        else:
            change = (d1_buf, d2_buf)[which][slot].astype(F32) - fresh
            if which == 0:
                d1_out[slot] = change.astype(BF16)
                stores[n] = [
                    copies.start(d1_out.at[slot, pl.ds(inside, size)], news[0].at[q // 2, q % 2, pl.ds(low, size)])
                    for q, low, size, inside in parts_of(t)
                ]
            else:
                d2_out[slot] = change.astype(BF16).T.reshape(2, 2, 192, 256)
                stores[n] = [copies.start(d2_out.at[slot], news[1].at[:, :, :, pl.ds(256 * t, 256)])]
        between(n, stores)
    return [copy for group in (len(tiles) - 2, len(tiles) - 1) for copy in stores.get(group, ())]


KEPT = [((2, 3, 128, 384), BF16), ((2, 3, 256, 128), F32), ((2, 128, 384), BF16), (ROW, F32), ((2, *ROW), BF16), (ROW, BF16),
        ((8, 128), F32)]


def trade_kernel(first_step, number, *refs):
    if first_step:
        (x, og, ids, w_qkv, w_proj, e_in, in_hbm, out_hbm), refs = refs[:8], refs[8:]
    else:
        (x, og, ids, pe, pair, whole_hbm, both_hbm, w2_start, w1_hbm, w2_hbm), refs = refs[:10], refs[10:]
        starts = (both_hbm.at[:, :1536], w2_start)
    tokens = x
    step = 0 if first_step else 1
    x, og, ids = x.at[step], og.at[step], ids.at[step]
    (fin_hbm, fout_hbm, mv1, mv2), refs = refs[:4], refs[4:]
    kept_out, refs = refs[:7], refs[7:]
    ret, frozen_out, refs = refs[0], refs[1], refs[2:]
    news, others, refs = refs[:4], refs[2:4], refs[4:]
    if first_step:
        (w2_start, whole_out, p_out, pe, mve_out, both_hbm), refs = refs[:6], refs[6:]
        starts = ()
    kept, refs = refs[:7], refs[7:]
    (whole, w1, w2, fin, fout, send, frozen_in, recv, ans, zret, home, rows_all, grad_all, h_all, du_all, local_sems,
     in_send, in_recv, z_send, z_recv, zb_send, zb_recv, home_send, home_recv,
     core_send, core_recv, swap_send, swap_recv, swapped), refs = refs[:29], refs[29:]
    w2_turned = du_all
    bufs, refs = refs[:10], refs[10:]
    copies = Copies(local_sems)
    loads = [] if first_step else [copies.start(whole_hbm, whole)]
    loads += [copies.start(fin_hbm, fin), copies.start(fout_hbm, fout)]
    if not first_step:
        loads += [copies.start(w1_hbm, w1), copies.start(w2_hbm, w2)]
    d, e = lax.axis_index("dp"), lax.axis_index("expert")
    partner = {"dp": 1 - d}
    g = lax.axis_index("group")
    core = lax.rem(g, 2)
    other_core = {"group": g + 1 - 2 * core}

    def ahead(k):
        return lax.rem(e + k, 16)

    def behind(k):
        return lax.rem(e + 16 - k, 16)

    barrier = pltpu.get_barrier_semaphore()

    @pl.loop(1, 16)
    def _(k):
        pl.semaphore_signal(barrier, inc=1, device_id={"expert": ahead(k)}, device_id_type=MESH)

    if first_step:
        pair, p_in, own, e_out, p_box, entry_sems, entry_sends, entry_recvs = refs
        place, links = Place(), Links(entry_sends, entry_recvs)
        more = [place.along_x(step, 1) for step in range(4)] + [place.along_y(step, 1) for step in (1, 2, 3)]
        more += [place.other_core(), place.in_group(2)]
        hail(more)
        experts, experts_end = entry_part(
            place, links, tokens, w_qkv, w_proj, e_in, in_hbm, out_hbm, whole, p_out, pe, mve_out, pair, both_hbm,
            p_in, own, bufs[0], e_out, p_box, entry_sems, more + [None] * 15,
        )
        whole_kept = copies.start(whole, whole_out)
    else:
        pl.semaphore_signal(barrier, inc=1, device_id=partner, device_id_type=MESH)
        pl.semaphore_signal(barrier, inc=1, device_id=other_core, device_id_type=MESH)
        loads.pop(0).wait()

    def swap(branch):
        if not first_step:
            pl.semaphore_wait(barrier, 17)
        swapped[0] = branch
        copy = remote(swapped.at[0], swapped.at[1], swap_send, swap_recv, 0, partner)
        copy.start()

        def finish():
            copy.wait()
            return swapped[1].astype(F32)

        return finish

    def remote(src, dst, sends, recvs, k, to):
        return pltpu.make_async_remote_copy(
            src_ref=src, dst_ref=dst, send_sem=sends.at[k], recv_sem=recvs.at[k], device_id=to, device_id_type=MESH
        )

    front_part(x, pair, og, ids, pe, whole, send, frozen_in, *kept, swap)

    def to_expert(k):
        return remote(send.at[ahead(k)], recv.at[0, e], in_send, in_recv, k, {"expert": ahead(k)})

    def to_partner(k):
        return remote(recv.at[0, behind(k)], recv.at[1, behind(k)], z_send, z_recv, k, partner)

    def from_partner(k):
        return remote(ans.at[1, behind(k)], zret.at[behind(k)], zb_send, zb_recv, k, partner)

    def to_home(k):
        return remote(home.at[behind(k)], ret.at[e], home_send, home_recv, k, {"expert": behind(k)})

    @pl.loop(1, 16)
    def _(k):
        to_expert(k).start()

    recv[0, e] = send[e]
    to_partner(0).start()
    keeps = [copies.start(src, dst) for src, dst in zip(kept, kept_out)]

    def pass_on(k):
        to_expert(k).wait_recv()
        to_partner(k).start()

    pl.loop(1, 6)(pass_on)
    if first_step:
        for n in range(192 // PIECE):
            experts.pass_on(n)
    for copy in loads[:2]:
        copy.wait()
    both = frozen_in[...].astype(F32)
    value, back, _, _ = expert_rows(both[:CAP].astype(BF16), both[CAP:].astype(BF16), fin[...], fout[...])
    frozen_out[...] = jnp.concatenate([value, back], axis=0)
    pl.loop(6, 16)(pass_on)
    if first_step:
        experts_end()
        loads += [copies.start(both_hbm.at[:, :1536], w1), copies.start(both_hbm.at[:, 1536:], w2_turned)]
    for copy in loads[2:]:
        copy.wait()
    if first_step:
        for t in range(6):
            w2[256 * t : 256 * t + 256] = w2_turned[:, 256 * t : 256 * t + 256].T
        keeps += [copies.start(w2, w2_start), whole_kept]

    @pl.loop(0, 4)
    def _(j):
        other = lax.rem(lax.div(j + 1, 2) + 1, 2)
        half = lax.div(j, 2)

        @pl.when(other == 1)
        def _():
            @pl.loop(0, 8)
            def _(i):
                to_partner(half * 8 + i).wait_recv()

        blocks = [recv[other, behind(half * 8 + i)].astype(F32) for i in range(8)]
        rows = jnp.concatenate([b[:CAP] for b in blocks], axis=0).astype(BF16)
        grad = jnp.concatenate([b[CAP:] for b in blocks], axis=0).astype(BF16)
        value, back, h, du = expert_rows(rows, grad, w1[...], w2[...])
        at = pl.ds(pl.multiple_of(j * 192, 192), 192)
        rows_all[at] = rows
        grad_all[at] = grad
        h_all[at] = h
        du_all[at] = du
        for i in range(8):
            part = slice(i * CAP, (i + 1) * CAP)
            ans[other, behind(half * 8 + i)] = jnp.concatenate([value[part], back[part]], axis=0).astype(BF16)

        @pl.when(other == 1)
        def _():
            @pl.loop(0, 8)
            def _(i):
                from_partner(half * 8 + i).start()

    def serve(k):
        from_partner(k).wait_recv()
        slot = behind(k)
        total = (ans[0, slot].astype(F32) + zret[slot].astype(F32)).astype(BF16)
        if k == 0:
            ret[e] = total
        else:
            home[slot] = total
            to_home(k).start()

    def to_core(which):
        return remote(news[which].at[:, 1 - core], others[which], core_send, core_recv, which, other_core)

    def between(n, stores):
        for k in range(SERVED[n], SERVED[n + 1]):
            serve(k)
        if not first_step and n in (7, 11):
            for tile in ((4, 5) if n == 7 else (10, 11)):
                for copy in stores.pop(tile, ()):
                    copy.wait()
            to_core(0 if n == 7 else 1).start()

    for k in range(SERVED[0]):
        serve(k)
    left = grow_experts(
        first_step, number, copies, rows_all, grad_all, h_all, du_all, w1, w2, mv1, mv2, starts, news, bufs, between
    )

    @pl.loop(1, 16)
    def _(k):
        to_home(k).wait_recv()
        to_home(k).wait_send()
        to_expert(k).wait_send()

    @pl.loop(0, 16)
    def _(k):
        to_partner(k).wait_send()
        from_partner(k).wait_send()

    if not first_step:
        for which in range(2):
            to_core(which).wait_recv()
            to_core(which).wait_send()
    for copy in left + keeps:
        copy.wait()
    if first_step:
        links.finish()


SERVED = (3, 4, 6, 7, 9, 10, 12, 13, 15, 16, 16, 16, 16)


def trade_call(first_step, number, collective_id, small, *large):
    wide = (768, 1536)
    moment_kind = F32 if first_step else BF16
    tall, quarters = (1536, 768), (2, 2, 192, 1536)
    news = (
        [(ANY, wide, BF16), (ANY, tall, BF16), (ANY, (2, 768, 1536), BF16), (ANY, (2, 1536, 768), BF16), (ANY, tall, BF16),
         (ANY, WHOLE, BF16), (VMEM, BLOCK, F32), (VMEM, (24, 768), F32), (VMEM, (2, 24, 768), F32), (ANY, (768, 3072), BF16)]
        if first_step else [(ANY, quarters, BF16)] * 2 + [(ANY, (2, 192, 1536), BF16)] * 2
    )
    outs = [(ANY, *k) for k in KEPT] + [(VMEM, (16, 48, 768), BF16), (VMEM, (48, 768), F32)] + news
    t1, t2, c1, c2 = (2, 2, 128, 1536), (2, 2, 256, 768), (2, 128, 1536), (2, 256, 768)
    none = (8, 128)
    first = first_step
    bufs = [
        VMEM(t1, moment_kind), VMEM(t2, moment_kind),
        VMEM(none if first else c1, BF16), VMEM(none if first else c2, BF16),
        VMEM(c1 if first else none, BF16), VMEM(c2 if first else none, BF16),
        VMEM(t1 if first else none, BF16), VMEM(t2 if first else none, BF16),
        VMEM(none if first else c1, BF16), VMEM(none if first else (2, 2, 2, 192, 256), BF16),
    ]
    plane = (16, 48, 768)
    scratch = [VMEM(*k) for k in KEPT] + [
        VMEM(WHOLE, BF16), VMEM(wide, BF16), VMEM(tall, BF16), VMEM((768, 3072), BF16), VMEM((3072, 768), BF16),
        VMEM(plane, BF16), VMEM((48, 768), BF16), VMEM((2, *plane), BF16), VMEM((2, *plane), BF16),
        VMEM(plane, BF16), VMEM(plane, BF16),
        VMEM((768, 768), BF16), VMEM((768, 768), BF16), VMEM(wide, BF16), VMEM(wide, BF16),
        pltpu.SemaphoreType.DMA((72,)),
    ] + semaphores(16) * 4 + semaphores(2) + semaphores(1) + [VMEM((2, *ROW), BF16)] + bufs
    if first_step:
        scratch += [
            VMEM(ROW, BF16), VMEM((4, 2, 48, 384), BF16), VMEM((192, 3072), BF16),
            VMEM((2, 4, 4, 24, 128), F32), VMEM((2, 4, 48, 384), BF16), pltpu.SemaphoreType.DMA((5,)),
        ] + semaphores(7 + 1 + 1 + 15 + 16 + 6 + 2 * (192 // PIECE) + 1)
    args = [(VMEM, a) for a in small] + [(ANY, a) for a in large]
    return call(functools.partial(trade_kernel, first_step, number), outs, scratch, collective_id, args, 62 << 20)


FETCHED = (0, 1, 2, 4)


def back_body(step, refs, scratch, copies, links, place, swapped, block_out, grad_out, grads, begin, ready, late):
    (x, og, ids, pe), whole_hbm, kept, ret, frozen = refs[:4], refs[4], list(refs[5:12]), refs[12], refs[13]
    whole, buffers = scratch[0], scratch[1:5]
    loads = [copies.start(whole_hbm, whole)]
    for at, buffer in zip(FETCHED, buffers):
        loads.append(copies.start(kept[at], buffer))
        kept[at] = buffer

    def arrived():
        begin()
        for copy in loads:
            copy.wait()

    def swap(n, rows):
        swapped[n, 0] = rows
        copy = links.send(swapped.at[n, 0], swapped.at[n, 1], place.other_dp())

        def finish():
            copy.wait_recv()
            return swapped[n, 1]

        return finish

    return back_part(
        x.at[step], og.at[step], ids.at[step], pe, whole, *kept, ret, frozen, block_out, grad_out, grads, arrived, ready, swap, late
    )


BACK_SCRATCH = [VMEM(WHOLE, BF16)] + [VMEM(*KEPT[at]) for at in FETCHED] + [VMEM(WHOLE, BF16), pltpu.SemaphoreType.DMA((16,)), VMEM((2, 2, *ROW), BF16)]


def renew_kernel(number, *refs):
    shared, (p_in, s_qkv, s_proj, pe_in, mve_in), refs = refs[:14], refs[14:19], refs[19:]
    (block_out, grad_out, whole, p_out, mv_out, pe_out, mve_out, x_pair), refs = refs[:8], refs[8:]
    back_scratch, (grads, sems, swapped), refs = refs[:5], refs[5:8], refs[8:]
    scratch, (mv_msg, mv_box, sends, recvs) = refs[:11], refs[11:]
    place = Place()
    partners = ring_partners(place)
    hail(partners)
    for c in range(4):
        for dp in range(2):
            mv_msg[c, dp] = jnp.concatenate(
                [dealt(s_qkv[k], s_proj[k], c, dp) for k in range(2)], axis=0
            ).astype(BF16)
    links = Links(sends, recvs)
    reduction = Reduction(links, place, grads, scratch)
    pair, moments = [], []

    def late():
        moments.extend(deal(links, place, mv_msg, mv_box))
        pair.append(links.send(shared[0].at[1], x_pair, place.other_dp()))

    extra = back_body(
        0, shared, back_scratch, Copies(sems), links, place, swapped, block_out, grad_out, grads,
        lambda: await_hails(partners), reduction.start, late,
    )
    renew_part(number, place, links, reduction, extra, moments, mv_box, p_in, pe_in, mve_in,
               whole, p_out, mv_out, pe_out, mve_out)
    pair[0].wait_recv()
    links.finish()


def final_kernel(number, *refs):
    shared, dense, refs = refs[:14], refs[14:20], refs[20:]
    deltas, others, refs = refs[:2], refs[2:4], refs[4:]
    (block_out, grad_out, mean_out, flat_out, turned_out, expert_out), refs = refs[:6], refs[6:]
    back_scratch, (grads, sems, swapped), refs = refs[:5], refs[5:8], refs[8:]
    scratch, boxes, refs = refs[:11], refs[11:16], refs[16:]
    expert_scratch, (sends, recvs) = refs[:4], refs[4:]
    place = Place()
    partners = ring_partners(place) + [
        place.in_group(k, step, over) for k in (1, 2, 3) for step in range(4) for over in range(2)
    ]
    hail(partners)
    copies, links = Copies(sems), Links(sends, recvs)
    experts = ExpertMean(links, place, copies, deltas, others, *expert_scratch)

    reduction = Reduction(links, place, grads, scratch)
    extra = back_body(
        1, shared, back_scratch, copies, links, place, swapped, block_out, grad_out, grads,
        lambda: await_hails(partners), reduction.start, experts.start,
    )
    final_part(
        number, place, links, reduction, extra, *dense, mean_out, flat_out, turned_out, *boxes
    )
    for k in range(2):
        expert_out[k] = experts.mean(k)
    links.finish()


def finish_kernel(*refs):
    given, refs = refs[:16], refs[16:]
    olds, refs = refs[:4], refs[4:]
    (block, grad, new_qkv, new_proj, new_mom_qkv, new_mom_proj, new_gains, new_router, new_mom_gains, new_mom_router,
     *news), (old_buf, new_buf, sems, *held) = refs[:14], refs[14:]
    copies = Copies(sems)
    rows = [copies.start(src, dst) for src, dst in zip(given, held)]
    loads = [copies.start(src, old_buf.at[n]) for n, src in enumerate(olds)]
    for copy in rows:
        copy.wait()
    (block0, block1, grad0, grad1, mean, flat_e, turned_e, experts,
     w_qkv, w_proj, mom_qkv, mom_proj, gains, router, mom_gains, mom_router) = held
    stores = []
    for k in range(2):
        for copy in loads[2 * k : 2 * k + 2]:
            copy.wait()
        new_buf[2 * k], new_buf[2 * k + 1] = outer(old_buf[2 * k], old_buf[2 * k + 1], experts[k])
        stores += [copies.start(new_buf.at[n], news[n]) for n in (2 * k, 2 * k + 1)]
    for n, (one, all_rows) in enumerate(((block0, block), (block1, block), (grad0, grad), (grad1, grad))):
        all_rows[n % 2] = one[...]
    new_gains[...], new_mom_gains[...] = outer(gains[...], mom_gains[...], flat_e[17:19])
    new_router[...], new_mom_router[...] = outer(router[...], mom_router[...], turned_e[:, :17])
    for c in range(3):
        lanes = slice(768 * c, 768 * c + 768)
        new_qkv[:, lanes], new_mom_qkv[:, lanes] = outer(w_qkv[:, lanes], mom_qkv[:, lanes], mean[c])
    new_proj[...], new_mom_proj[...] = outer(w_proj[...], mom_proj[...], mean[3])
    for copy in stores:
        copy.wait()


def finish_call(small, olds):
    part = (192, 1536)
    outs = [((2, *ROW), BF16), ((2, *ROW), F32), ((24, 2304), F32), ((24, 768), F32), ((24, 2304), F32), ((24, 768), F32),
            ((2, 24), F32), ((24, 17), F32), ((2, 24), F32), ((24, 17), F32)]
    return pl.pallas_call(
        finish_kernel,
        out_shape=tuple(jax.ShapeDtypeStruct(*out) for out in outs + [(part, F32)] * 4),
        in_specs=[pl.BlockSpec(memory_space=ANY)] * (len(small) + 4),
        out_specs=tuple([pl.BlockSpec(memory_space=VMEM)] * 10 + [pl.BlockSpec(memory_space=ANY)] * 4),
        scratch_shapes=[VMEM((4, *part), F32), VMEM((4, *part), F32), pltpu.SemaphoreType.DMA((24,))]
        + [VMEM(array.shape, array.dtype) for array in small],
        compiler_params=pltpu.CompilerParams(vmem_limit_bytes=60 << 20),
    )(*small, *olds)


def back_args(small, whole, kept, ret, frozen):
    args = [(VMEM, a) for a in small] + [(ANY, whole)]
    args += [(ANY if at in FETCHED else VMEM, a) for at, a in enumerate(kept)]
    return args + [(VMEM, ret), (VMEM, frozen)]


def renew_call(number, shared, *args):
    return call(
        functools.partial(renew_kernel, number),
        [(VMEM, ROW, BF16), (VMEM, ROW, F32), (VMEM, WHOLE, BF16), (VMEM, BLOCK, F32), (VMEM, (2, *BLOCK), F32),
         (VMEM, (24, 768), F32), (VMEM, (2, 24, 768), F32), (VMEM, ROW, BF16)],
        BACK_SCRATCH + REDUCE_SCRATCH + [VMEM((4, 2, 96, 384), BF16), VMEM((2, 4, 96, 384), BF16)]
        + semaphores(REDUCE_COPIES + GATHER_COPIES + 3 + 7), 2,
        back_args(*shared) + [(VMEM, a) for a in args],
    )


def final_call(number, shared, dense, deltas):
    part = (192, 1536)
    half = (48, 384)
    boxes = [VMEM((2, 4, *half), BF16), VMEM((4, *half), BF16), VMEM((4, *half), BF16), VMEM(half, BF16), VMEM((4, *half), BF16)]
    return call(
        functools.partial(final_kernel, number),
        [(VMEM, ROW, BF16), (VMEM, ROW, F32), (VMEM, (4, 24, 768), F32), (VMEM, (24, 24), F32), (VMEM, (24, 24), F32),
         (VMEM, (2, *part), F32)],
        BACK_SCRATCH + REDUCE_SCRATCH + boxes
        + [VMEM((2, 2, *part), BF16), VMEM((2, 2, *part), BF16), VMEM((2, *part), BF16), VMEM((2, *part), BF16)]
        + semaphores(REDUCE_COPIES + 3 + 3 + 8 + 2 + 2),
        3,
        back_args(*shared) + [(VMEM, a) for a in dense] + [(ANY, a) for a in deltas],
    )


def body(
    tokens,
    out_grad,
    expert_ids,
    replay,
    frozen_in,
    frozen_out,
    gains,
    w_qkv,
    w_proj,
    router,
    exp_in,
    exp_out,
    mom_gains,
    mom_qkv,
    mom_proj,
    mom_router,
    mom_in,
    mom_out,
    state_gains,
    state_qkv,
    state_proj,
    state_router,
    state_in,
    state_out,
):
    gap = jnp.zeros((24, 5), F32)
    packed = jnp.concatenate(
        [router, gains.T, gap, state_router[0, 0], state_gains[0, 0].T, gap, state_router[0, 1], state_gains[0, 1].T,
         jnp.zeros((24, 61), F32)], axis=1,
    )
    ids = jnp.concatenate([jnp.swapaxes(expert_ids, 1, 2), replay[:, None], jnp.zeros((2, 5, 128), jnp.int32)], axis=1)
    turn = lambda array: jnp.swapaxes(array[0], 0, 1)
    back = lambda array: jnp.swapaxes(array, 0, 1)[None]
    frozen_both = (frozen_in[0], frozen_out[0])
    made = trade_call(
        True, STEP, 4, (tokens, out_grad, ids, w_qkv, w_proj, packed), exp_in[0], turn(exp_out), *frozen_both,
        state_in[0, :, 0], state_out[0, :, 0],
    )
    w2_start, whole, p_start, pe_start, mve, both_low = made[13:]
    shared = ((tokens, out_grad, ids, pe_start), whole, made[:7], made[7], made[8])
    block0, grad0, whole, p_now, mv, pe_now, mve, x_pair = renew_call(
        STEP, shared, p_start, state_qkv[0], state_proj[0], pe_start, mve
    )
    small = (tokens, out_grad, ids, pe_now)
    made = trade_call(False, STEP + 1, 5, (*small, x_pair), whole, both_low, w2_start, *made[9:11], *frozen_both, *made[11:13])
    shared = (small, whole, made[:7], made[7], made[8])
    dense = (p_now, mv, pe_now, mve, p_start, pe_start)
    block1, grad1, *means = final_call(STEP + 1, shared, dense, made[9:13])
    (block, grad, new_qkv, new_proj, new_mom_qkv, new_mom_proj, new_gains, new_router, new_mom_gains, new_mom_router,
     new_in, new_mom_in, new_out, new_mom_out) = finish_call(
        (block0, block1, grad0, grad1, *means, w_qkv, w_proj, mom_qkv, mom_proj, gains, router, mom_gains, mom_router),
        (exp_in[0], mom_in[0], turn(exp_out), turn(mom_out)),
    )
    return (
        block, grad, new_gains, new_qkv, new_proj, new_router, new_in[None], back(new_out),
        new_mom_gains, new_mom_qkv, new_mom_proj, new_mom_router, new_mom_in[None], back(new_mom_out),
    )


def solution(mesh):
    return jax.shard_map(
        body,
        mesh=mesh,
        in_specs=(
            P(None, ("group", "dp", "expert"), None),
            P(None, ("group", "dp", "expert"), None),
            P(None, ("group", "dp", "expert"), None),
            P(None, ("group", "dp", "expert")),
            P(),
            P(),
            P(None, ("dp", "expert")),
            P(("dp", "expert"), None),
            P(("dp", "expert"), None),
            P(("dp", "expert"), None),
            P("expert", "group", "dp"),
            P("expert", "dp", "group"),
            P(None, ("dp", "expert")),
            P(("dp", "expert"), None),
            P(("dp", "expert"), None),
            P(("dp", "expert"), None),
            P("expert", "group", "dp"),
            P("expert", "dp", "group"),
            P("group", None, None, ("dp", "expert")),
            P("group", None, ("dp", "expert"), None),
            P("group", None, ("dp", "expert"), None),
            P("group", None, ("dp", "expert"), None),
            P("group", None, "expert", None, "dp"),
            P("group", None, "expert", "dp", None),
        ),
        out_specs=(
            P(None, ("group", "dp", "expert"), None),
            P(None, ("group", "dp", "expert"), None),
            P(None, ("dp", "expert")),
            P(("dp", "expert"), None),
            P(("dp", "expert"), None),
            P(("dp", "expert"), None),
            P("expert", "group", "dp"),
            P("expert", "dp", "group"),
            P(None, ("dp", "expert")),
            P(("dp", "expert"), None),
            P(("dp", "expert"), None),
            P(("dp", "expert"), None),
            P("expert", "group", "dp"),
            P("expert", "dp", "group"),
        ),
        check_vma=False,
    )
```

```python
import functools

import jax
import jax.numpy as jnp
from jax import lax
from jax.experimental import pallas as pl
from jax.experimental.pallas import tpu as pltpu
from jax.sharding import PartitionSpec as P

MESH = pl.DeviceIdType.MESH
VMEM = pltpu.VMEM
F32 = jnp.float32
BF16 = jnp.bfloat16


DIMS = {"nn": (((1,), (0,)), ((), ())), "nt": (((1,), (1,)), ((), ())), "tn": (((0,), (0,)), ((), ()))}


class Links:
    def __init__(self, sends, recvs):
        self.sends, self.recvs, self.used, self.begun = sends, recvs, 0, []

    def send(self, src, dst, to):
        at = self.used
        self.used += 1
        copy = pltpu.make_async_remote_copy(
            src_ref=src, dst_ref=dst, send_sem=self.sends.at[at], recv_sem=self.recvs.at[at],
            device_id=to, device_id_type=MESH,
        )
        self.begun.append(copy)
        copy.start()
        return copy

    def finish(self):
        for copy in self.begun:
            copy.wait_send()


class Place:
    def __init__(self):
        self.g, self.d = lax.axis_index("group"), lax.axis_index("dp")
        e = lax.axis_index("expert")
        self.x, self.y = lax.div(e, 4), lax.rem(e, 4)

    def along_x(self, step, over=0):
        return {"dp": lax.rem(self.d + over, 2), "expert": lax.rem(self.x + step, 4) * 4 + self.y}

    def along_y(self, step, over=0):
        return {"dp": lax.rem(self.d + over, 2), "expert": self.x * 4 + lax.rem(self.y + step, 4)}

    def other_dp(self):
        return {"dp": 1 - self.d}

    def in_group(self, step, along=0, over=0):
        return {"group": lax.rem(self.g + step, 4), **self.along_y(along, over)}

    def other_core(self):
        return {"group": self.g + 1 - 2 * lax.rem(self.g, 2)}


def hail(partners):
    barrier = pltpu.get_barrier_semaphore()
    for partner in partners:
        pl.semaphore_signal(barrier, inc=1, device_id=partner, device_id_type=MESH)


def await_hails(partners):
    pl.semaphore_wait(pltpu.get_barrier_semaphore(), len(partners))


PEERS = ((0, 1), (1, 0), (3, 0), (1, 1), (3, 1), (2, 0), (2, 1))


def ring_partners(place):
    return (
        [place.along_x(*peer) for peer in PEERS]
        + [place.along_y(step) for step in (1, 2, 3)]
        + [place.along_y(step, 1) for step in (1, 2, 3)]
    )


class Gather:
    def __init__(self, links, whole, h, p1, p2, near1, near2, at, share=None):
        self.links, self.whole, self.h, self.at = links, whole, h, at
        self.p1, self.p2, self.near1, self.near2, self.share = p1, p2, near1, near2, share
        self.steps, self.shared, self.round, self.passed = (0, 1, 3, 2), [], [], []

    def push(self, n, k2, to):
        c, x = self.at(lax.rem(self.p1 + 4 - self.steps[n], 4), lax.rem(k2, 4))
        ref = self.whole.at[c, x, self.h]
        return self.links.send(ref, ref, to)

    def give(self, n, k2):
        if self.share is not None:
            self.shared.append(self.push(n, k2, self.share))

    def start(self):
        self.direct = [self.push(0, self.p2, self.near1(step)) for step in self.steps[1:]]
        self.ring(0)

    def ring(self, n):
        if n:
            self.direct[n - 1].wait_recv()
        self.round.append([self.push(n, self.p2, self.near2(step)) for step in (1, 3)])
        self.give(n, self.p2)

    def forward(self, n):
        right, left = self.round[n]
        right.wait_recv()
        if n % 2 == 0:
            self.passed.append(self.push(n, self.p2 + 3, self.near2(1)))
        self.give(n, self.p2 + 3)
        left.wait_recv()
        if n % 2 == 1:
            self.passed.append(self.push(n, self.p2 + 1, self.near2(3)))
        self.give(n, self.p2 + 1)

    def end(self):
        for n, copy in enumerate(self.passed):
            copy.wait_recv()
            self.give(n, self.p2 + 2)
        for copy in self.shared:
            copy.wait_recv()


def run_gather(parts):
    for n in range(1, 6):
        for part in parts:
            if n < 4:
                part.ring(n)
            if n >= 2:
                part.forward(n - 2)
    for part in parts:
        part.end()


def gather_parts(links, place, whole):
    by_x = lambda kx, ky: (ky, kx)
    by_y = lambda ky, kx: (ky, kx)
    first = Gather(links, whole, 0, place.x, place.y, place.along_x, place.along_y, by_x)
    second = Gather(links, whole, 1, place.y, place.x, place.along_y, place.along_x, by_y)
    return first, second


class RingSum:
    def __init__(self, links, near1, near2, p1, p2, term, far, near, mid, box):
        self.links, self.near1, self.near2, self.p1, self.p2 = links, near1, near2, p1, p2
        self.term, self.far, self.near, self.mid, self.box = term, far, near, mid, box
        self.steps = (2, 1, 3, 0)
        self.far_copies, self.direct, self.summed, self.over = [], [], [], []

    def get(self, k, i):
        return self.term(lax.rem(self.p1 + k, 4), lax.rem(self.p2 + self.steps[i], 4))

    def send_far(self, i):
        self.far_copies.append(self.links.send(self.get(2, i), self.far.at[i], self.near1((1, 3)[i % 2])))

    def send_direct(self, i):
        step = (3, 1)[i % 2]
        self.direct.append(self.links.send(self.get(step, i), self.near.at[1, i], self.near1(step)))

    def middle(self, i):
        step = (1, 3)[i % 2]
        self.far_copies[i].wait_recv()
        self.far[i] = (self.far[i].astype(F32) + self.get(step, i)[...].astype(F32)).astype(BF16)
        self.summed.append(self.links.send(self.far.at[i], self.near.at[0, i], self.near1(step)))

    def finish(self, i):
        self.direct[i].wait_recv()
        self.summed[i].wait_recv()
        self.mid[i] = (
            self.get(0, i)[...].astype(F32) + self.near[0, i].astype(F32) + self.near[1, i].astype(F32)
        ).astype(BF16)
        step = self.steps[i]
        if step:
            self.over.append(self.links.send(self.mid.at[i], self.box.at[self.p2], self.near2(step)))
        else:
            self.box[self.p2] = self.mid[i]

    def total(self):
        for copy in self.over:
            copy.wait_recv()
        value = self.box[0].astype(F32)
        for k in range(1, 4):
            value = value + self.box[k].astype(F32)
        return value


def folded(rows):
    return jnp.concatenate([rows[:, :384], rows[:, 384:]], axis=0).astype(BF16)


def unfolded(rows):
    return jnp.concatenate([rows[:24], rows[24:]], axis=1)


def add_over(links, own, box, position, size, reach):
    box[position] = folded(own)
    copies = [links.send(box.at[position], box.at[position], reach(step)) for step in range(1, size)]

    def finish():
        for copy in copies:
            copy.wait_recv()
        total = box[0].astype(F32)
        for k in range(1, size):
            total = total + box[k].astype(F32)
        return unfolded(total)

    return finish


PIECES = (4, 48, 768)
HALF_SCRATCH = [VMEM(PIECES, BF16), VMEM((2, *PIECES), BF16), VMEM(PIECES, BF16), VMEM(PIECES, BF16)]
REDUCE_SCRATCH = HALF_SCRATCH * 2 + [VMEM((4, 48, 384), BF16), VMEM((4, 48, 384), BF16), VMEM((2, 48, 384), BF16)]
REDUCE_COPIES = 2 * 15 + 7
GATHER_COPIES = 2 * 15


class Reduction:
    def __init__(self, links, place, grads, scratch):
        self.links, self.place, self.boxes = links, place, scratch[8:]
        self.parts = (
            RingSum(
                links, place.along_y, place.along_x, place.y, place.x, lambda k, j: grads.at[k, j, 0], *scratch[:4]
            ),
            RingSum(
                links, place.along_x, place.along_y, place.x, place.y, lambda k, j: grads.at[j, k, 1], *scratch[4:8]
            ),
        )

    def start(self):
        for i in range(4):
            for part in self.parts:
                part.send_far(i)
        for part in self.parts:
            part.send_direct(0)

    def finish(self, extra, between=None):
        links, place, parts = self.links, self.place, self.parts
        box_x, box_y, box_z = self.boxes
        extra_x = add_over(links, extra, box_x, place.x, 4, place.along_x)
        for i in range(4):
            for part in parts:
                if i:
                    part.send_direct(i)
                part.middle(i)
            if i == 1:
                extra_y = add_over(links, extra_x(), box_y, place.y, 4, place.along_y)
            if i == 3:
                extra_z = add_over(links, extra_y(), box_z, place.d, 2, lambda step: place.other_dp())
        if between is not None:
            between()
        for i in range(4):
            for part in parts:
                part.finish(i)
        return [part.total() for part in parts], extra_z()


EPS_NORM = 1e-06
BETA_ONE = 0.9
BETA_TWO = 0.95
ADAM_EPS = 1e-08
DECAY = 0.1
OUTER_RATE = 0.7
OUTER_MOMENTUM = 0.9
REPLAY_WEIGHT = 0.25
RATES = (0.6, 0.04, 0.3, 0.03, 0.04, 0.02)
HEADS = 12
LEN = 128
STEPS = 2
STEP = 10


PIECE = 32
FIRST_PIECES = 4


class ExpertGather:
    def __init__(self, links, place, own, both):
        self.links, self.place, self.own, self.both = links, place, own, both
        self.far, self.near = [], []

    def rows(self, group, n=None):
        if n is None:
            return self.both.at[pl.ds(pl.multiple_of(group * 192, 192), 192)]
        return self.both.at[pl.ds(pl.multiple_of(group * 192 + n * PIECE, PIECE), PIECE)]

    def send(self, n):
        part = self.own.at[pl.ds(n * PIECE, PIECE)]
        self.far.append(self.links.send(part, self.rows(self.place.g, n), self.place.in_group(2)))

    def share(self):
        self.near.append(self.links.send(self.own, self.rows(self.place.g), self.place.other_core()))

    def pass_on(self, n):
        self.far[n].wait_recv()
        ref = self.rows(lax.rem(self.place.g + 2, 4), n)
        self.near.append(self.links.send(ref, ref, self.place.other_core()))

    def end(self):
        for copy in self.near:
            copy.wait_recv()


def halves(rows):
    return jnp.concatenate([rows[:, :384], rows[:, 384:]], axis=0)


def deal(links, place, src, box):
    box[place.d, place.y] = src[place.y, place.d]
    return [
        links.send(
            src.at[lax.rem(place.y + step, 4), lax.rem(place.d + over, 2)], box.at[place.d, place.y],
            place.along_y(step, over),
        )
        for step, over in PEERS
    ]


def assembled(place, box):
    upper, lower = box[:, :, :24], box[:, :, 24:]
    columns = jnp.concatenate([upper[0], upper[1]], axis=-1)
    rows = jnp.concatenate([upper, lower], axis=-1)
    rows = jnp.where(place.d == 0, rows[0], rows[1])
    return jnp.where(place.y == 3, rows, columns).reshape(2, 48, 768)


def dealt(wide, square, c, dp):
    if c < 3:
        return jnp.concatenate([wide[:, 768 * c + 384 * dp : 768 * c + 384 * dp + 384]] * 2, axis=0)
    return halves(square)


def placed(values, lane, form):
    count = values.shape[1 if form == "nn" else 0]
    pick = lax.broadcasted_iota(jnp.int32, (count, 128), 0) + lane == lax.broadcasted_iota(jnp.int32, (count, 128), 1)
    return lax.dot_general(
        values, pick.astype(F32), DIMS[form], precision=lax.Precision.HIGHEST, preferred_element_type=F32
    )


def entry_part(place, links, tokens, w_qkv, w_proj, e_in, in_hbm, out_hbm, whole, p_out, pe_out, mve_out, x_pair, both,
               p_in, own, loaded, e_out, p_box, local_sems, partners):
    loads = [
        pltpu.make_async_copy(
            src.at[pl.ds(128 * part, size)], loaded.at[k, part, pl.ds(0, size)], local_sems.at[2 * k + part]
        )
        for k, src in enumerate((in_hbm, out_hbm))
        for part, size in ((0, 128), (1, 64))
    ]
    for copy in loads:
        copy.start()
    for c in range(4):
        for dp in range(2):
            p_in[c, dp] = dealt(w_qkv, w_proj[...], c, dp).astype(BF16)
    await_hails(partners)
    x, y, d = place.x, place.y, place.d
    h = lax.rem(place.g, 2)
    masters = deal(links, place, p_in, p_box)
    router, gains, s_router, s_gains = e_in
    e_out[d, x, y] = (
        placed(router[...], 0, "nn") + placed(gains[...], 17, "tn")
        + placed(s_router[0], 24, "nn") + placed(s_gains[0], 41, "tn")
        + placed(s_router[1], 48, "nn") + placed(s_gains[1], 65, "tn")
    )
    mine = e_out.at[d, x, y]
    extra_z = links.send(mine, mine, place.other_dp())
    pair = links.send(tokens.at[0], x_pair, place.other_dp())
    for k in range(2):
        for part, size in ((0, 128), (1, 64)):
            loads[2 * k + part].wait()
            own[128 * part : 128 * part + size, 1536 * k : 1536 * k + 1536] = loaded[k, part, :size].astype(BF16)
    experts = ExpertGather(links, place, own, both)
    mine_there = pltpu.make_async_copy(own, experts.rows(place.g), local_sems.at[4])
    mine_there.start()
    for n in range(FIRST_PIECES):
        experts.send(n)
    for copy in masters:
        copy.wait_recv()
    master = assembled(place, p_box[...].astype(F32))
    p_out[...] = master

    @pl.when(h == 0)
    def _():
        whole[y, x, 0] = master[0].astype(BF16)

    @pl.when(h == 1)
    def _():
        whole[y, x, 1] = master[1].astype(BF16)

    def mix(a, b):
        return a * (1 - h) + b * h

    def near1(step, over=0):
        one, two = place.along_x(step, over), place.along_y(step, over)
        return {"dp": one["dp"], "expert": mix(one["expert"], two["expert"])}

    def near2(step):
        one, two = place.along_y(step), place.along_x(step)
        return {"dp": one["dp"], "expert": mix(one["expert"], two["expert"])}

    def at(k1, k2):
        return mix(k2, k1), mix(k1, k2)

    part = Gather(links, whole, h, mix(x, y), mix(y, x), near1, near2, at, place.other_core())
    part.start()
    extra_z.wait_recv()
    mine = e_out.at[:, x, y]
    extra_x = [links.send(mine, mine, place.along_x(k)) for k in (1, 2, 3)]
    for n in (1, 2, 3):
        part.ring(n)
        part.forward(n - 1)
    for copy in extra_x:
        copy.wait_recv()
    mine = e_out.at[:, :, y]
    extra_y = [links.send(mine, mine, place.along_y(k)) for k in (1, 2, 3)]
    part.forward(3)
    part.end()
    experts.share()
    for copy in extra_y:
        copy.wait_recv()
    turned = e_out[...].reshape(768, 128).T
    pe_out[...] = turned[:24]
    mve_out[0] = turned[24:48]
    mve_out[1] = turned[48:72]
    pair.wait_recv()

    def end():
        experts.end()
        mine_there.wait()

    return experts, end


def adam_values(master, first, second, grad, rate, number):
    first = BETA_ONE * first + (1.0 - BETA_ONE) * grad
    second = BETA_TWO * second + (1.0 - BETA_TWO) * grad * grad
    level = second * (1.0 / (1.0 - BETA_TWO**number))
    below = level * lax.rsqrt(jnp.maximum(level, 1e-30)) + ADAM_EPS
    guess = pl.reciprocal(below, approx=True)
    update = first * ((1.0 / (1.0 - BETA_ONE**number)) * rate) * (guess * (2.0 - below * guess))
    return master - (update + (rate * DECAY) * master), first, second


def block_rate(place):
    return jnp.where(place.y == 3, RATES[2], RATES[1]).astype(F32)


def extra_rates():
    row = lax.broadcasted_iota(jnp.int32, (24, 768), 0)
    return jnp.where(row < 17, RATES[3], RATES[0]).astype(F32)


def renew_part(number, place, links, reduction, extra, moments, mv_box, p_in, pe_in, mve_in,
               whole, p_out, mv_out, pe_out, mve_out):
    sums, total = reduction.finish(extra)
    parts = gather_parts(links, place, whole)
    for copy in moments:
        copy.wait_recv()
    moment = mv_box[...].astype(F32)
    old = [assembled(place, moment[:, :, 48 * k : 48 * k + 48]) for k in range(2)]
    for h, part in enumerate(parts):
        fresh, first, second = adam_values(p_in[h], old[0][h], old[1][h], sums[h], block_rate(place), number)
        whole[place.y, place.x, h] = fresh.astype(BF16)
        part.start()
        p_out[h] = fresh
        mv_out[0, h] = first
        mv_out[1, h] = second
    pe_out[...], mve_out[0], mve_out[1] = adam_values(pe_in[...], mve_in[0], mve_in[1], total, extra_rates(), number)
    run_gather(parts)


def outer(begin, moment, mean):
    renewed = OUTER_MOMENTUM * moment + mean
    return begin - OUTER_RATE * (mean + OUTER_MOMENTUM * renewed), renewed


def own_features(place, rows, turned):
    at = 24 * (16 * place.d + 4 * place.x + place.y)
    pick = (lax.broadcasted_iota(jnp.int32, (768, 24), 0) == at + lax.broadcasted_iota(jnp.int32, (768, 24), 1)).astype(BF16)
    total = 0.0
    for _ in range(3):
        part = rows.astype(BF16)
        total = total + (
            lax.dot_general(pick, part, (((0,), (1,)), ((), ())), preferred_element_type=F32) if turned
            else lax.dot_general(part, pick, (((1,), (0,)), ((), ())), preferred_element_type=F32)
        )
        rows = rows - part.astype(F32)
    return total


class ExpertMean:
    def __init__(self, links, place, copies, deltas, others, own, other, sent, far):
        self.links, self.place, self.own, self.other, self.sent, self.far = links, place, own, other, sent, far
        self.high = lax.div(place.g, 2)
        self.loads = [copies.start(delta.at[:, lax.rem(place.g, 2)], own.at[k]) for k, delta in enumerate(deltas)]
        self.loads += [copies.start(array, other.at[k]) for k, array in enumerate(others)]

    def start(self):
        for copy in self.loads:
            copy.wait()
        self.copies = []
        self.push()
        self.push()

    def push(self):
        k, rows = len(self.copies) // 2, pl.ds(len(self.copies) % 2 * 96, 96)
        self.sent[k, rows] = (
            self.own[k, 1 - self.high, rows].astype(F32) + self.other[k, 1 - self.high, rows].astype(F32)
        ).astype(BF16)
        self.copies.append(self.links.send(self.sent.at[k, rows], self.far.at[k, rows], self.place.in_group(2)))

    def mean(self, k):
        for copy in self.copies[2 * k : 2 * k + 2]:
            copy.wait_recv()
        mine = self.own[k, self.high].astype(F32) + self.other[k, self.high].astype(F32)
        return (mine + self.far[k].astype(F32)) * 0.25


def final_part(number, place, links, reduction, extra, experts, p_in, mv_in, pe_in, mve_in, p_start, pe_start,
               mean_out, flat_out, turned_out, turned, delta, quarters, mean, boxes):
    g, y = place.g, place.y
    sums, total = reduction.finish(extra, experts.push)
    for h in range(2):
        fresh, _, _ = adam_values(p_in[h], mv_in[0, h], mv_in[1, h], sums[h], block_rate(place), number)
        rows = (p_start[h] - fresh).reshape(2, 24, 768)
        for k in range(2):
            delta[2 * h + k] = folded(rows[k])
    summed = [
        links.send(delta.at[lax.rem(g + k, 4)], quarters.at[g], place.in_group(k)) for k in (1, 2, 3)
    ]
    fresh_e, _, _ = adam_values(pe_in[...], mve_in[0], mve_in[1], total, extra_rates(), number)
    sum_e = add_over(links, pe_start[...] - fresh_e, boxes, g, 4, place.in_group)
    experts.push()
    quarters[g] = delta[g]
    for copy in summed:
        copy.wait_recv()
    mean[...] = (
        (quarters[0].astype(F32) + quarters[1].astype(F32) + quarters[2].astype(F32) + quarters[3].astype(F32)) * 0.25
    ).astype(BF16)
    d, at = place.d, links.used
    links.used += 8

    def spread(k, over):
        return pltpu.make_async_remote_copy(
            src_ref=mean, dst_ref=turned.at[d, y], send_sem=links.sends.at[at + 2 * k + over],
            recv_sem=links.recvs.at[at + 2 * y + d],
            device_id={"group": lax.rem(g + k, 4), "dp": lax.rem(d + over, 2), "expert": place.x * 4 + g},
            device_id_type=MESH,
        )

    def arrival(dp, c):
        return pltpu.make_async_remote_copy(
            src_ref=mean, dst_ref=turned.at[dp, c], send_sem=links.sends.at[at], recv_sem=links.recvs.at[at + 2 * c + dp],
            device_id=place.other_core(), device_id_type=MESH,
        )

    others = [(k, over) for k in range(4) for over in range(2) if k or over]
    for k, over in others:
        spread(k, over).start()

    @pl.when(y != g)
    def _():
        spread(0, 0).start()

    @pl.when(y == g)
    def _():
        turned[d, y] = mean[...]

    mean_e = sum_e() * 0.25
    flat_out[...] = own_features(place, mean_e, False)
    turned_out[...] = own_features(place, mean_e, True)
    for dp in range(2):
        for c in range(4):
            @pl.when(jnp.logical_or(y != g, jnp.logical_or(c != y, dp != d)))
            def _(c=c, dp=dp):
                arrival(dp, c).wait_recv()

    for k, over in others:
        spread(k, over).wait_send()

    @pl.when(y != g)
    def _():
        spread(0, 0).wait_send()

    landed = turned[...].astype(F32)
    upper, lower = landed[:, :, :24], landed[:, :, 24:]
    for c in range(3):
        mine = jnp.where(d == 0, upper[:, c], lower[:, c])
        mean_out[c] = jnp.concatenate([mine[0], mine[1]], axis=-1)
    rows = jnp.concatenate([upper[:, 3], lower[:, 3]], axis=-1)
    mean_out[3] = jnp.where(d == 0, rows[0], rows[1])


def semaphores(count):
    return [pltpu.SemaphoreType.DMA((count,)), pltpu.SemaphoreType.DMA((count,))]


ANY = pl.ANY
WHOLE = (4, 4, 2, 48, 768)
BLOCK = (2, 48, 768)
ROW = (128, 768)


def call(kernel, outs, scratch, collective_id, args, limit=60 << 20):
    return pl.pallas_call(
        kernel,
        out_shape=tuple(jax.ShapeDtypeStruct(shape, kind) for _, shape, kind in outs),
        in_specs=[pl.BlockSpec(memory_space=space) for space, _ in args],
        out_specs=tuple(pl.BlockSpec(memory_space=space) for space, _, _ in outs),
        scratch_shapes=scratch,
        compiler_params=pltpu.CompilerParams(
            collective_id=collective_id, has_side_effects=True, vmem_limit_bytes=limit
        ),
    )(*(array for _, array in args))

CAP = 24
TOK = 128


def mm(a, b, form="nn"):
    return lax.dot_general(a, b, DIMS[form], preferred_element_type=F32)


def split_low(values):
    high = values.astype(BF16)
    return high, (values - high.astype(F32)).astype(BF16)


def row_scale(values):
    return lax.rsqrt(jnp.mean(values * values, axis=-1, keepdims=True) + EPS_NORM)


def iota(shape, dim):
    return lax.broadcasted_iota(jnp.int32, shape, dim)


def routing(ids):
    names = [(iota((24, TOK), 0) == ids[k : k + 1]).astype(F32) for k in range(2)]
    either = names[0] + names[1]
    earlier = (iota((TOK, TOK), 0) < iota((TOK, TOK), 1)).astype(BF16)
    slot = mm(either.astype(BF16), earlier).astype(jnp.int32)
    taken = jnp.where(iota((17, CAP, TOK), 1) == slot[:17][:, None, :], 1.0, 0.0)
    return names, taken * either[:17][:, None, :]


def pair_stack(part):
    lane = iota(part.shape, 1)
    zero = jnp.zeros_like(part)
    return jnp.concatenate([jnp.where(lane < 64, part, zero), jnp.where(lane < 64, zero, part)], axis=0)


def side_by_side(stacked):
    return jnp.concatenate([stacked[:TOK], stacked[TOK:]], axis=1)


def flat(whole, c):
    return whole[c].reshape(384, 768)


def cotangent(og_ref, ids_ref):
    factor = jnp.where(ids_ref[1][...] > 0, REPLAY_WEIGHT, 1.0)
    spread = jnp.where(iota((TOK, TOK), 0) == iota((TOK, TOK), 1), factor, 0.0).astype(BF16)
    return mm(spread, og_ref[...])


def across(rows, weight):
    return mm(rows[:, :384], weight[:, :384]) + mm(rows[:, 384:], weight[:, 384:])


def front_part(x_ref, pair_ref, og_ref, ids_ref, pe_ref, whole,
               send, frozen, qkv_out, probs_out, mixed_out, middle_out, a1_out, a2_out, weights_out, swap):
    gain = pe_ref[16:24].astype(BF16).astype(F32)
    row, col = iota((2 * TOK, TOK), 0), iota((2 * TOK, TOK), 1)
    causal = lax.rem(row, TOK) >= col
    x = x_ref[...].astype(F32)
    finish = None
    for t, values in ((1, pair_ref[...].astype(F32)), (0, x)):
        a1 = (values * row_scale(values) * gain[1:2]).astype(BF16)
        a1_out[t] = a1
        for c in range(3):
            qkv_out[t, c] = across(a1, flat(whole, c)).astype(BF16)
        for pair in range(3):
            lanes = slice(128 * pair, 128 * pair + 128)
            scores = mm(pair_stack(qkv_out[t, 0, :, lanes]), qkv_out[t, 1, :, lanes], "nt") * 0.125
            scores = jnp.where(causal, scores, -1e30)
            expo = jnp.exp(scores - jnp.max(scores, axis=-1, keepdims=True))
            probs = expo / jnp.sum(expo, axis=-1, keepdims=True)
            probs_out[t, pair] = probs
            mixed_out[t, :, lanes] = mm(
                side_by_side(probs.astype(BF16)), pair_stack(qkv_out[t, 2, :, lanes])
            ).astype(BF16)
        branch = mm(mixed_out[t], flat(whole, 3))
        if t:
            finish = swap(branch.astype(BF16))
    middle = x + branch + finish()
    middle_out[...] = middle
    a2 = (middle * row_scale(middle) * gain[2:3]).astype(BF16)
    a2_out[...] = a2
    logits = mm(pe_ref[...].astype(BF16), a2, "nt")
    names, taken = routing(ids_ref[0][...])
    picked = [jnp.sum(name * logits, axis=0, keepdims=True) for name in names]
    top = jnp.maximum(picked[0], picked[1])
    expo = [jnp.exp(z - top) for z in picked]
    whole_sum = expo[0] + expo[1]
    weights = [e / whole_sum for e in expo]
    weights_out[...] = jnp.concatenate(weights + [jnp.zeros((6, TOK), F32)], axis=0)
    by_expert = names[0] * weights[0] + names[1] * weights[1]
    row_weight = jnp.sum(taken * by_expert[:17][:, None, :], axis=-1, keepdims=True)
    cot = cotangent(og_ref, ids_ref).astype(BF16)
    low = taken.astype(BF16).reshape(17 * CAP, TOK)
    rows = mm(low, a2).reshape(17, CAP, 768)
    grads = mm(low, cot).reshape(17, CAP, 768) * row_weight
    both = jnp.concatenate([rows, grads], axis=1).astype(BF16)
    frozen[...] = both[0]
    send[...] = both[1:]


def back_part(x_ref, og_ref, ids_ref, pe_ref, whole, qkv, probs_ref, mixed, middle_ref, a1, a2,
              weights_ref, ret, frozen, block_out, grad_out, grads, arrived, ready, swap, early, late):
    gain = pe_ref[16:24].astype(BF16).astype(F32)
    low_rows = pe_ref[...].astype(BF16)
    cot = cotangent(og_ref, ids_ref)
    names, taken = routing(ids_ref[0][...])
    weights = [weights_ref[k : k + 1] for k in range(2)]
    by_expert = names[0] * weights[0] + names[1] * weights[1]
    row_weight = jnp.sum(taken * by_expert[:17][:, None, :], axis=-1, keepdims=True)
    low = taken.astype(BF16).reshape(17 * CAP, TOK)
    both = ret[...].astype(F32)
    both = jnp.concatenate([frozen[...][None], both], axis=0)
    results, back = both[:, :CAP], both[:, CAP:].reshape(17 * CAP, 768)
    middle = middle_ref[...]
    cot_rows = mm(low, cot.astype(BF16)).reshape(17, CAP, 768)
    grad_row = jnp.sum(cot_rows * results, axis=-1, keepdims=True)
    by_name = jnp.concatenate([jnp.sum(taken * grad_row, axis=1), jnp.zeros((7, TOK), F32)], axis=0)
    grad_w = [jnp.sum(name * by_name, axis=0, keepdims=True) for name in names]
    mean = weights[0] * grad_w[0] + weights[1] * grad_w[1]
    grad_logits = sum(names[k] * (weights[k] * (grad_w[k] - mean)) for k in range(2))
    logit_parts = split_low(grad_logits)
    da2 = sum(mm(part, low_rows, "tn") for part in logit_parts)
    da2 = da2 + sum(mm(low, part, "tn") for part in split_low(back))
    scale = row_scale(middle)
    normed = middle * scale
    dg2 = jnp.sum(normed * da2, axis=0, keepdims=True)
    into = da2 * gain[2:3]
    dmiddle = cot + scale * (into - normed * jnp.mean(into * normed, axis=-1, keepdims=True))
    branch = dmiddle.astype(BF16)
    arrived()
    finish = swap(0, branch)
    early()
    branches = [branch]
    dqkv = [[], [], []]
    for t in range(2):
        if t:
            branches.append(finish())
        dmixed = mm(branches[t], flat(whole, 3), "nt").astype(BF16)
        parts = [[], [], []]
        for pair in range(3):
            lanes = slice(128 * pair, 128 * pair + 128)
            probs = probs_ref[t, pair]
            dms = pair_stack(dmixed[:, lanes])
            parts[2].append(mm(probs.astype(BF16), dms, "tn").astype(BF16))
            dpb = mm(dms, qkv[t, 2, :, lanes], "nt")
            ds = (probs * (dpb - jnp.sum(probs * dpb, axis=-1, keepdims=True))).astype(BF16)
            parts[0].append((mm(side_by_side(ds), pair_stack(qkv[t, 1, :, lanes])) * 0.125).astype(BF16))
            parts[1].append((mm(ds, pair_stack(qkv[t, 0, :, lanes]), "tn") * 0.125).astype(BF16))
        for c in range(3):
            dqkv[c].append(jnp.concatenate(parts[c], axis=1))
    a1_both = a1[...].reshape(2 * TOK, 768)
    for c in range(3):
        both = jnp.concatenate(dqkv[c], axis=0)
        grads[c] = jnp.concatenate(
            [mm(a1_both[:, :384], both, "tn"), mm(a1_both[:, 384:], both, "tn")], axis=1
        ).astype(BF16).reshape(4, 2, 48, 768)
    grads[3] = mm(
        mixed[...].reshape(2 * TOK, 384), jnp.concatenate(branches, axis=0), "tn"
    ).astype(BF16).reshape(4, 2, 48, 768)
    ready()

    def into_a1(t):
        halves_of = [
            sum(mm(dqkv[c][t], flat(whole, c)[:, side], "nt") for c in range(3))
            for side in (slice(0, 384), slice(384, 768))
        ]
        return jnp.concatenate(halves_of, axis=1)

    finish = swap(1, into_a1(1).astype(BF16))
    late()
    da1 = into_a1(0)
    grad_router = sum(mm(part, a2[...]) for part in logit_parts)
    block_out[...] = (
        middle + sum(mm(low, part, "tn") for part in split_low((results * row_weight).reshape(17 * CAP, 768)))
    ).astype(BF16)
    da1 = da1 + finish().astype(F32)
    x = x_ref[...].astype(F32)
    scale = row_scale(x)
    normed = x * scale
    dg1 = jnp.sum(normed * da1, axis=0, keepdims=True)
    into = da1 * gain[1:2]
    grad_out[...] = dmiddle + scale * (into - normed * jnp.mean(into * normed, axis=-1, keepdims=True))
    return jnp.concatenate([grad_router[:17], dg1, dg2, jnp.zeros((5, 768), F32)], axis=0)


SQRT_HALF = 0.7071067811865476
DENSITY = 0.3989422804014327


def expert_rows(rows, grad, first, second):
    u = mm(rows, first)
    chance = 0.5 + 0.5 * lax.erf(u * SQRT_HALF)
    h = (u * chance).astype(BF16)
    value = mm(h, second)
    slope = chance + u * (jnp.exp(u * u * -0.5) * DENSITY)
    du = (slope * mm(grad, second, "nt")).astype(BF16)
    return value, mm(du, first, "nt"), h, du


class Copies:
    def __init__(self, sems):
        self.sems, self.used = sems, 0

    def start(self, src, dst):
        copy = pltpu.make_async_copy(src, dst, self.sems.at[self.used])
        self.used += 1
        copy.start()
        return copy


def grow_experts(first_step, number, copies, rows, grad, h, du, w1, w2, mv1, mv2, starts, news, bufs, between):
    (mv1_buf, mv2_buf, d1_buf, d2_buf, w1_out, w2_out, mv1_out, mv2_out, d1_out, d2_out) = bufs
    tiles = [(0, t) for t in range(6)] + [(1, t) for t in range(6)]

    def cut(which, t):
        size = (128, 256)[which]
        return pl.ds(size * t, size), slice(None)

    def parts_of(t):
        begin, end = 128 * t, 128 * t + 128
        cuts = sorted({begin, end} | {192 * q for q in range(5) if begin < 192 * q < end})
        return [(low // 192, low % 192, high - low, low - begin) for low, high in zip(cuts, cuts[1:])]

    def load(n):
        which, t = tiles[n]
        slot = n % 2
        mv, buf = ((mv1, mv1_buf), (mv2, mv2_buf))[which]
        size = (128, 256)[which]
        begun = [copies.start(mv.at[:, pl.ds(size * t, size)], buf.at[slot])]
        if not first_step:
            begun.append(copies.start(starts[which].at[cut(which, t)], (d1_buf, d2_buf)[which].at[slot]))
        return begun

    loads = {0: load(0)}
    stores = {}
    for n, (which, t) in enumerate(tiles):
        slot = n % 2
        if n + 1 < len(tiles):
            loads[n + 1] = load(n + 1)
        for copy in loads[n]:
            copy.wait()
        for copy in stores.pop(n - 2, ()):
            copy.wait()
        if which == 0:
            value = mm(rows[:, 128 * t : 128 * t + 128], du[...], "tn")
            begin = w1[128 * t : 128 * t + 128].astype(F32)
            moments = mv1_buf
        else:
            value = mm(h[:, 256 * t : 256 * t + 256], grad[...], "tn")
            begin = w2[256 * t : 256 * t + 256].astype(F32)
            moments = mv2_buf
        fresh, first, second = adam_values(
            begin, moments[slot, 0].astype(F32), moments[slot, 1].astype(F32), value, RATES[4 + which], number
        )
        here = cut(which, t)
        if first_step:
            low, mv_low = (w1_out, w2_out)[which], (mv1_out, mv2_out)[which]
            low[slot] = fresh.astype(BF16)
            mv_low[slot, 0] = first.astype(BF16)
            mv_low[slot, 1] = second.astype(BF16)
            size = (128, 256)[which]
            stores[n] = [
                copies.start(low.at[slot], news[which].at[here]),
                copies.start(mv_low.at[slot], news[2 + which].at[:, pl.ds(size * t, size)]),
            ]
        else:
            change = (d1_buf, d2_buf)[which][slot].astype(F32) - fresh
            if which == 0:
                d1_out[slot] = change.astype(BF16)
                stores[n] = [
                    copies.start(d1_out.at[slot, pl.ds(inside, size)], news[0].at[q // 2, q % 2, pl.ds(low, size)])
                    for q, low, size, inside in parts_of(t)
                ]
            else:
                d2_out[slot] = change.astype(BF16).T.reshape(2, 2, 192, 256)
                stores[n] = [copies.start(d2_out.at[slot], news[1].at[:, :, :, pl.ds(256 * t, 256)])]
        between(n, stores)
    return [copy for group in (len(tiles) - 2, len(tiles) - 1) for copy in stores.get(group, ())]


KEPT = [((2, 3, 128, 384), BF16), ((2, 3, 256, 128), F32), ((2, 128, 384), BF16), (ROW, F32), ((2, *ROW), BF16), (ROW, BF16),
        ((8, 128), F32)]


def trade_kernel(first_step, number, *refs):
    if first_step:
        (x, og, ids, replay, w_qkv, w_proj, *e_in), (in_hbm, out_hbm), refs = refs[:10], refs[10:12], refs[12:]
    else:
        (x, og, ids, replay, pe, pair, whole_hbm, both_hbm, w2_start, w1_hbm, w2_hbm), refs = refs[:11], refs[11:]
        starts = (both_hbm.at[:, :1536], w2_start)
    tokens = x
    step = 0 if first_step else 1
    x, og, ids = x.at[step], og.at[step], (ids.at[step], replay.at[pl.ds(step, 1)])
    (fin_hbm, fout_hbm, mv1, mv2), refs = refs[:4], refs[4:]
    kept_out, refs = refs[:7], refs[7:]
    ret, frozen_out, refs = refs[0], refs[1], refs[2:]
    news, others, refs = refs[:4], refs[2:4], refs[4:]
    if first_step:
        (w2_start, whole_out, p_out, pe, mve_out, both_hbm), refs = refs[:6], refs[6:]
        starts = ()
    kept, refs = refs[:7], refs[7:]
    (whole, w1, w2, fin, fout, send, frozen_in, recv, ans, zret, home, rows_all, grad_all, h_all, du_all, local_sems,
     in_send, in_recv, z_send, z_recv, zb_send, zb_recv, home_send, home_recv,
     core_send, core_recv, swap_send, swap_recv, swapped), refs = refs[:29], refs[29:]
    w2_turned = du_all
    bufs, refs = refs[:10], refs[10:]
    copies = Copies(local_sems)
    loads = [] if first_step else [copies.start(whole_hbm, whole)]
    loads += [copies.start(fin_hbm, fin), copies.start(fout_hbm, fout)]
    if not first_step:
        loads += [copies.start(w1_hbm, w1), copies.start(w2_hbm, w2)]
    d, e = lax.axis_index("dp"), lax.axis_index("expert")
    partner = {"dp": 1 - d}
    g = lax.axis_index("group")
    core = lax.rem(g, 2)
    other_core = {"group": g + 1 - 2 * core}

    def ahead(k):
        return lax.rem(e + k, 16)

    def behind(k):
        return lax.rem(e + 16 - k, 16)

    barrier = pltpu.get_barrier_semaphore()

    @pl.loop(1, 16)
    def _(k):
        pl.semaphore_signal(barrier, inc=1, device_id={"expert": ahead(k)}, device_id_type=MESH)

    if first_step:
        pair, p_in, own, e_out, p_box, entry_sems, entry_sends, entry_recvs = refs
        place, links = Place(), Links(entry_sends, entry_recvs)
        more = [place.along_x(step, 1) for step in range(4)] + [place.along_y(step, 1) for step in (1, 2, 3)]
        more += [place.other_core(), place.in_group(2)]
        hail(more)
        experts, experts_end = entry_part(
            place, links, tokens, w_qkv, w_proj, e_in, in_hbm, out_hbm, whole, p_out, pe, mve_out, pair, both_hbm,
            p_in, own, bufs[0], e_out, p_box, entry_sems, more + [None] * 15,
        )
        whole_kept = copies.start(whole, whole_out)
    else:
        pl.semaphore_signal(barrier, inc=1, device_id=partner, device_id_type=MESH)
        pl.semaphore_signal(barrier, inc=1, device_id=other_core, device_id_type=MESH)
        loads.pop(0).wait()

    def swap(branch):
        if not first_step:
            pl.semaphore_wait(barrier, 17)
        swapped[0] = branch
        copy = remote(swapped.at[0], swapped.at[1], swap_send, swap_recv, 0, partner)
        copy.start()
        if first_step:
            for n in range(FIRST_PIECES, 192 // PIECE):
                experts.send(n)

        def finish():
            copy.wait()
            return swapped[1].astype(F32)

        return finish

    def remote(src, dst, sends, recvs, k, to):
        return pltpu.make_async_remote_copy(
            src_ref=src, dst_ref=dst, send_sem=sends.at[k], recv_sem=recvs.at[k], device_id=to, device_id_type=MESH
        )

    front_part(x, pair, og, ids, pe, whole, send, frozen_in, *kept, swap)

    def to_expert(k):
        return remote(send.at[ahead(k)], recv.at[0, e], in_send, in_recv, k, {"expert": ahead(k)})

    def to_partner(k):
        return remote(recv.at[0, behind(k)], recv.at[1, behind(k)], z_send, z_recv, k, partner)

    def from_partner(k):
        return remote(ans.at[1, behind(k)], zret.at[behind(k)], zb_send, zb_recv, k, partner)

    def to_home(k):
        return remote(home.at[behind(k)], ret.at[e], home_send, home_recv, k, {"expert": behind(k)})

    @pl.loop(1, 16)
    def _(k):
        to_expert(k).start()

    recv[0, e] = send[e]
    to_partner(0).start()
    keeps = [copies.start(src, dst) for src, dst in zip(kept, kept_out)]

    def pass_on(k):
        to_expert(k).wait_recv()
        to_partner(k).start()

    pl.loop(1, 6)(pass_on)
    if first_step:
        for n in range(192 // PIECE):
            experts.pass_on(n)
    for copy in loads[:2]:
        copy.wait()
    both = frozen_in[...].astype(F32)
    value, back, _, _ = expert_rows(both[:CAP].astype(BF16), both[CAP:].astype(BF16), fin[...], fout[...])
    frozen_out[...] = jnp.concatenate([value, back], axis=0)
    pl.loop(6, 16)(pass_on)
    if first_step:
        experts_end()
        loads += [copies.start(both_hbm.at[:, :1536], w1), copies.start(both_hbm.at[:, 1536:], w2_turned)]
    for copy in loads[2:]:
        copy.wait()
    if first_step:
        for t in range(6):
            w2[256 * t : 256 * t + 256] = w2_turned[:, 256 * t : 256 * t + 256].T
        keeps += [copies.start(w2, w2_start), whole_kept]

    @pl.loop(0, 4)
    def _(j):
        other = lax.rem(lax.div(j + 1, 2) + 1, 2)
        half = lax.div(j, 2)

        @pl.when(other == 1)
        def _():
            @pl.loop(0, 8)
            def _(i):
                to_partner(half * 8 + i).wait_recv()

        blocks = [recv[other, behind(half * 8 + i)].astype(F32) for i in range(8)]
        rows = jnp.concatenate([b[:CAP] for b in blocks], axis=0).astype(BF16)
        grad = jnp.concatenate([b[CAP:] for b in blocks], axis=0).astype(BF16)
        value, back, h, du = expert_rows(rows, grad, w1[...], w2[...])
        at = pl.ds(pl.multiple_of(j * 192, 192), 192)
        rows_all[at] = rows
        grad_all[at] = grad
        h_all[at] = h
        du_all[at] = du
        for i in range(8):
            part = slice(i * CAP, (i + 1) * CAP)
            ans[other, behind(half * 8 + i)] = jnp.concatenate([value[part], back[part]], axis=0).astype(BF16)

        @pl.when(other == 1)
        def _():
            @pl.loop(0, 8)
            def _(i):
                from_partner(half * 8 + i).start()

    def serve(k):
        from_partner(k).wait_recv()
        slot = behind(k)
        total = (ans[0, slot].astype(F32) + zret[slot].astype(F32)).astype(BF16)
        if k == 0:
            ret[e] = total
        else:
            home[slot] = total
            to_home(k).start()

    def to_core(which):
        return remote(news[which].at[:, 1 - core], others[which], core_send, core_recv, which, other_core)

    def between(n, stores):
        for k in range(SERVED[n], SERVED[n + 1]):
            serve(k)
        if not first_step and n in (7, 11):
            for tile in ((4, 5) if n == 7 else (10, 11)):
                for copy in stores.pop(tile, ()):
                    copy.wait()
            to_core(0 if n == 7 else 1).start()

    for k in range(SERVED[0]):
        serve(k)
    left = grow_experts(
        first_step, number, copies, rows_all, grad_all, h_all, du_all, w1, w2, mv1, mv2, starts, news, bufs, between
    )

    @pl.loop(1, 16)
    def _(k):
        to_home(k).wait_recv()
        to_home(k).wait_send()
        to_expert(k).wait_send()

    @pl.loop(0, 16)
    def _(k):
        to_partner(k).wait_send()
        from_partner(k).wait_send()

    if not first_step:
        for which in range(2):
            to_core(which).wait_recv()
            to_core(which).wait_send()
    for copy in left + keeps:
        copy.wait()
    if first_step:
        links.finish()


SERVED = (3, 4, 6, 7, 9, 10, 12, 13, 15, 16, 16, 16, 16)


def trade_call(first_step, number, collective_id, small, *large):
    wide = (768, 1536)
    moment_kind = F32 if first_step else BF16
    tall, quarters = (1536, 768), (2, 2, 192, 1536)
    news = (
        [(ANY, wide, BF16), (ANY, tall, BF16), (ANY, (2, 768, 1536), BF16), (ANY, (2, 1536, 768), BF16), (ANY, tall, BF16),
         (ANY, WHOLE, BF16), (VMEM, BLOCK, F32), (VMEM, (24, 768), F32), (VMEM, (2, 24, 768), F32), (ANY, (768, 3072), BF16)]
        if first_step else [(ANY, quarters, BF16)] * 2 + [(ANY, (2, 192, 1536), BF16)] * 2
    )
    outs = [(ANY, *k) for k in KEPT] + [(VMEM, (16, 48, 768), BF16), (VMEM, (48, 768), F32)] + news
    t1, t2, c1, c2 = (2, 2, 128, 1536), (2, 2, 256, 768), (2, 128, 1536), (2, 256, 768)
    none = (8, 128)
    first = first_step
    bufs = [
        VMEM(t1, moment_kind), VMEM(t2, moment_kind),
        VMEM(none if first else c1, BF16), VMEM(none if first else c2, BF16),
        VMEM(c1 if first else none, BF16), VMEM(c2 if first else none, BF16),
        VMEM(t1 if first else none, BF16), VMEM(t2 if first else none, BF16),
        VMEM(none if first else c1, BF16), VMEM(none if first else (2, 2, 2, 192, 256), BF16),
    ]
    plane = (16, 48, 768)
    scratch = [VMEM(*k) for k in KEPT] + [
        VMEM(WHOLE, BF16), VMEM(wide, BF16), VMEM(tall, BF16), VMEM((768, 3072), BF16), VMEM((3072, 768), BF16),
        VMEM(plane, BF16), VMEM((48, 768), BF16), VMEM((2, *plane), BF16), VMEM((2, *plane), BF16),
        VMEM(plane, BF16), VMEM(plane, BF16),
        VMEM((768, 768), BF16), VMEM((768, 768), BF16), VMEM(wide, BF16), VMEM(wide, BF16),
        pltpu.SemaphoreType.DMA((72,)),
    ] + semaphores(16) * 4 + semaphores(2) + semaphores(1) + [VMEM((2, *ROW), BF16)] + bufs
    if first_step:
        scratch += [
            VMEM(ROW, BF16), VMEM((4, 2, 48, 384), BF16), VMEM((192, 3072), BF16),
            VMEM((2, 4, 4, 24, 128), F32), VMEM((2, 4, 48, 384), BF16), pltpu.SemaphoreType.DMA((5,)),
        ] + semaphores(7 + 1 + 1 + 15 + 16 + 6 + 2 * (192 // PIECE) + 1)
    args = [(VMEM, a) for a in small] + [(ANY, a) for a in large]
    return call(functools.partial(trade_kernel, first_step, number), outs, scratch, collective_id, args, 62 << 20)


FETCHED = (0, 1, 2, 4)


def back_body(step, refs, scratch, copies, links, place, swapped, block_out, grad_out, grads, begin, ready, early, late):
    (x, og, ids, replay, pe), whole_hbm, kept, ret, frozen = refs[:5], refs[5], list(refs[6:13]), refs[13], refs[14]
    ids = (ids.at[step], replay.at[pl.ds(step, 1)])
    whole, buffers = scratch[0], scratch[1:5]
    loads = [copies.start(whole_hbm, whole)]
    for at, buffer in zip(FETCHED, buffers):
        loads.append(copies.start(kept[at], buffer))
        kept[at] = buffer

    def arrived():
        begin()
        for copy in loads:
            copy.wait()

    def swap(n, rows):
        swapped[n, 0] = rows
        copy = links.send(swapped.at[n, 0], swapped.at[n, 1], place.other_dp())

        def finish():
            copy.wait_recv()
            return swapped[n, 1]

        return finish

    return back_part(
        x.at[step], og.at[step], ids, pe, whole, *kept, ret, frozen, block_out, grad_out, grads, arrived, ready, swap, early, late
    )


BACK_SCRATCH = [VMEM(WHOLE, BF16)] + [VMEM(*KEPT[at]) for at in FETCHED] + [VMEM(WHOLE, BF16), pltpu.SemaphoreType.DMA((16,)), VMEM((2, 2, *ROW), BF16)]


def renew_kernel(number, *refs):
    shared, (p_in, s_qkv, s_proj, pe_in, mve_in), refs = refs[:15], refs[15:20], refs[20:]
    (block_out, grad_out, whole, p_out, mv_out, pe_out, mve_out, x_pair), refs = refs[:8], refs[8:]
    back_scratch, (grads, sems, swapped), refs = refs[:5], refs[5:8], refs[8:]
    scratch, (mv_msg, mv_box, sends, recvs) = refs[:11], refs[11:]
    place = Place()
    partners = ring_partners(place)
    hail(partners)
    for c in range(4):
        for dp in range(2):
            mv_msg[c, dp] = jnp.concatenate(
                [dealt(s_qkv[k], s_proj[k], c, dp) for k in range(2)], axis=0
            ).astype(BF16)
    links = Links(sends, recvs)
    reduction = Reduction(links, place, grads, scratch)
    pair, moments = [], []

    def late():
        moments.extend(deal(links, place, mv_msg, mv_box))
        pair.append(links.send(shared[0].at[1], x_pair, place.other_dp()))

    extra = back_body(
        0, shared, back_scratch, Copies(sems), links, place, swapped, block_out, grad_out, grads,
        lambda: await_hails(partners), reduction.start, lambda: None, late,
    )
    renew_part(number, place, links, reduction, extra, moments, mv_box, p_in, pe_in, mve_in,
               whole, p_out, mv_out, pe_out, mve_out)
    pair[0].wait_recv()
    links.finish()


def final_kernel(number, *refs):
    shared, dense, refs = refs[:15], refs[15:21], refs[21:]
    deltas, others, refs = refs[:2], refs[2:4], refs[4:]
    (block_out, grad_out, mean_out, flat_out, turned_out, expert_out), refs = refs[:6], refs[6:]
    back_scratch, (grads, sems, swapped), refs = refs[:5], refs[5:8], refs[8:]
    scratch, boxes, refs = refs[:11], refs[11:16], refs[16:]
    expert_scratch, (sends, recvs) = refs[:4], refs[4:]
    place = Place()
    partners = ring_partners(place) + [
        place.in_group(k, step, over) for k in (1, 2, 3) for step in range(4) for over in range(2)
    ]
    hail(partners)
    copies, links = Copies(sems), Links(sends, recvs)
    experts = ExpertMean(links, place, copies, deltas, others, *expert_scratch)

    reduction = Reduction(links, place, grads, scratch)
    extra = back_body(
        1, shared, back_scratch, copies, links, place, swapped, block_out, grad_out, grads,
        lambda: await_hails(partners), reduction.start, experts.start, lambda: None,
    )
    final_part(
        number, place, links, reduction, extra, experts, *dense, mean_out, flat_out, turned_out, *boxes
    )
    for k in range(2):
        expert_out[k] = experts.mean(k)
    links.finish()


def finish_kernel(*refs):
    given, refs = refs[:16], refs[16:]
    olds, refs = refs[:4], refs[4:]
    (block, grad, new_qkv, new_proj, new_mom_qkv, new_mom_proj, new_gains, new_router, new_mom_gains, new_mom_router,
     *news), (old_buf, new_buf, sems, *held) = refs[:14], refs[14:]
    copies = Copies(sems)
    rows = [copies.start(src, dst) for src, dst in zip(given, held)]
    loads = [copies.start(src, old_buf.at[n]) for n, src in enumerate(olds)]
    for copy in rows:
        copy.wait()
    (block0, block1, grad0, grad1, mean, flat_e, turned_e, experts,
     w_qkv, w_proj, mom_qkv, mom_proj, gains, router, mom_gains, mom_router) = held
    stores = []
    for k in range(2):
        for copy in loads[2 * k : 2 * k + 2]:
            copy.wait()
        new_buf[2 * k], new_buf[2 * k + 1] = outer(old_buf[2 * k], old_buf[2 * k + 1], experts[k])
        stores += [copies.start(new_buf.at[n], news[n]) for n in (2 * k, 2 * k + 1)]
    for n, (one, all_rows) in enumerate(((block0, block), (block1, block), (grad0, grad), (grad1, grad))):
        all_rows[n % 2] = one[...]
    new_gains[...], new_mom_gains[...] = outer(gains[...], mom_gains[...], flat_e[17:19])
    new_router[...], new_mom_router[...] = outer(router[...], mom_router[...], turned_e[:, :17])
    for c in range(3):
        lanes = slice(768 * c, 768 * c + 768)
        new_qkv[:, lanes], new_mom_qkv[:, lanes] = outer(w_qkv[:, lanes], mom_qkv[:, lanes], mean[c])
    new_proj[...], new_mom_proj[...] = outer(w_proj[...], mom_proj[...], mean[3])
    for copy in stores:
        copy.wait()


def finish_call(small, olds):
    part = (192, 1536)
    outs = [((2, *ROW), BF16), ((2, *ROW), F32), ((24, 2304), F32), ((24, 768), F32), ((24, 2304), F32), ((24, 768), F32),
            ((2, 24), F32), ((24, 17), F32), ((2, 24), F32), ((24, 17), F32)]
    return pl.pallas_call(
        finish_kernel,
        out_shape=tuple(jax.ShapeDtypeStruct(*out) for out in outs + [(part, F32)] * 4),
        in_specs=[pl.BlockSpec(memory_space=ANY)] * (len(small) + 4),
        out_specs=tuple([pl.BlockSpec(memory_space=VMEM)] * 10 + [pl.BlockSpec(memory_space=ANY)] * 4),
        scratch_shapes=[VMEM((4, *part), F32), VMEM((4, *part), F32), pltpu.SemaphoreType.DMA((24,))]
        + [VMEM(array.shape, array.dtype) for array in small],
        compiler_params=pltpu.CompilerParams(vmem_limit_bytes=60 << 20),
    )(*small, *olds)


def back_args(small, whole, kept, ret, frozen):
    args = [(VMEM, a) for a in small] + [(ANY, whole)]
    args += [(ANY if at in FETCHED else VMEM, a) for at, a in enumerate(kept)]
    return args + [(VMEM, ret), (VMEM, frozen)]


def renew_call(number, shared, *args):
    return call(
        functools.partial(renew_kernel, number),
        [(VMEM, ROW, BF16), (VMEM, ROW, F32), (VMEM, WHOLE, BF16), (VMEM, BLOCK, F32), (VMEM, (2, *BLOCK), F32),
         (VMEM, (24, 768), F32), (VMEM, (2, 24, 768), F32), (VMEM, ROW, BF16)],
        BACK_SCRATCH + REDUCE_SCRATCH + [VMEM((4, 2, 96, 384), BF16), VMEM((2, 4, 96, 384), BF16)]
        + semaphores(REDUCE_COPIES + GATHER_COPIES + 3 + 7), 2,
        back_args(*shared) + [(VMEM, a) for a in args],
    )


def final_call(number, shared, dense, deltas):
    part = (192, 1536)
    half = (48, 384)
    boxes = [VMEM((2, 4, *half), BF16), VMEM((4, *half), BF16), VMEM((4, *half), BF16), VMEM(half, BF16), VMEM((4, *half), BF16)]
    return call(
        functools.partial(final_kernel, number),
        [(VMEM, ROW, BF16), (VMEM, ROW, F32), (VMEM, (4, 24, 768), F32), (VMEM, (24, 24), F32), (VMEM, (24, 24), F32),
         (VMEM, (2, *part), F32)],
        BACK_SCRATCH + REDUCE_SCRATCH + boxes
        + [VMEM((2, 2, *part), BF16), VMEM((2, 2, *part), BF16), VMEM((2, *part), BF16), VMEM((2, *part), BF16)]
        + semaphores(REDUCE_COPIES + 3 + 3 + 8 + 4 + 2),
        3,
        back_args(*shared) + [(VMEM, a) for a in dense] + [(ANY, a) for a in deltas],
    )


def body(
    tokens,
    out_grad,
    expert_ids,
    replay,
    frozen_in,
    frozen_out,
    gains,
    w_qkv,
    w_proj,
    router,
    exp_in,
    exp_out,
    mom_gains,
    mom_qkv,
    mom_proj,
    mom_router,
    mom_in,
    mom_out,
    state_gains,
    state_qkv,
    state_proj,
    state_router,
    state_in,
    state_out,
):
    ids = jnp.swapaxes(expert_ids, 1, 2)
    turn = lambda array: jnp.swapaxes(array[0], 0, 1)
    back = lambda array: jnp.swapaxes(array, 0, 1)[None]
    frozen_both = (frozen_in[0], frozen_out[0])
    made = trade_call(
        True, STEP, 4, (tokens, out_grad, ids, replay, w_qkv, w_proj, router, gains, state_router[0], state_gains[0]), exp_in[0], turn(exp_out), *frozen_both,
        state_in[0, :, 0], state_out[0, :, 0],
    )
    w2_start, whole, p_start, pe_start, mve, both_low = made[13:]
    shared = ((tokens, out_grad, ids, replay, pe_start), whole, made[:7], made[7], made[8])
    block0, grad0, whole, p_now, mv, pe_now, mve, x_pair = renew_call(
        STEP, shared, p_start, state_qkv[0], state_proj[0], pe_start, mve
    )
    small = (tokens, out_grad, ids, replay, pe_now)
    made = trade_call(False, STEP + 1, 5, (*small, x_pair), whole, both_low, w2_start, *made[9:11], *frozen_both, *made[11:13])
    shared = (small, whole, made[:7], made[7], made[8])
    dense = (p_now, mv, pe_now, mve, p_start, pe_start)
    block1, grad1, *means = final_call(STEP + 1, shared, dense, made[9:13])
    (block, grad, new_qkv, new_proj, new_mom_qkv, new_mom_proj, new_gains, new_router, new_mom_gains, new_mom_router,
     new_in, new_mom_in, new_out, new_mom_out) = finish_call(
        (block0, block1, grad0, grad1, *means, w_qkv, w_proj, mom_qkv, mom_proj, gains, router, mom_gains, mom_router),
        (exp_in[0], mom_in[0], turn(exp_out), turn(mom_out)),
    )
    return (
        block, grad, new_gains, new_qkv, new_proj, new_router, new_in[None], back(new_out),
        new_mom_gains, new_mom_qkv, new_mom_proj, new_mom_router, new_mom_in[None], back(new_mom_out),
    )


def solution(mesh):
    return jax.shard_map(
        body,
        mesh=mesh,
        in_specs=(
            P(None, ("group", "dp", "expert"), None),
            P(None, ("group", "dp", "expert"), None),
            P(None, ("group", "dp", "expert"), None),
            P(None, ("group", "dp", "expert")),
            P(),
            P(),
            P(None, ("dp", "expert")),
            P(("dp", "expert"), None),
            P(("dp", "expert"), None),
            P(("dp", "expert"), None),
            P("expert", "group", "dp"),
            P("expert", "dp", "group"),
            P(None, ("dp", "expert")),
            P(("dp", "expert"), None),
            P(("dp", "expert"), None),
            P(("dp", "expert"), None),
            P("expert", "group", "dp"),
            P("expert", "dp", "group"),
            P("group", None, None, ("dp", "expert")),
            P("group", None, ("dp", "expert"), None),
            P("group", None, ("dp", "expert"), None),
            P("group", None, ("dp", "expert"), None),
            P("group", None, "expert", None, "dp"),
            P("group", None, "expert", "dp", None),
        ),
        out_specs=(
            P(None, ("group", "dp", "expert"), None),
            P(None, ("group", "dp", "expert"), None),
            P(None, ("dp", "expert")),
            P(("dp", "expert"), None),
            P(("dp", "expert"), None),
            P(("dp", "expert"), None),
            P("expert", "group", "dp"),
            P("expert", "dp", "group"),
            P(None, ("dp", "expert")),
            P(("dp", "expert"), None),
            P(("dp", "expert"), None),
            P(("dp", "expert"), None),
            P("expert", "group", "dp"),
            P("expert", "dp", "group"),
        ),
        check_vma=False,
    )
```

```python
import functools

import jax
import jax.numpy as jnp
from jax import lax
from jax.experimental import pallas as pl
from jax.experimental.pallas import tpu as pltpu
from jax.sharding import PartitionSpec as P

MESH = pl.DeviceIdType.MESH
VMEM = pltpu.VMEM
F32 = jnp.float32
BF16 = jnp.bfloat16


DIMS = {"nn": (((1,), (0,)), ((), ())), "nt": (((1,), (1,)), ((), ())), "tn": (((0,), (0,)), ((), ()))}


class Links:
    def __init__(self, sends, recvs):
        self.sends, self.recvs, self.used, self.begun = sends, recvs, 0, []

    def send(self, src, dst, to):
        at = self.used
        self.used += 1
        copy = pltpu.make_async_remote_copy(
            src_ref=src, dst_ref=dst, send_sem=self.sends.at[at], recv_sem=self.recvs.at[at],
            device_id=to, device_id_type=MESH,
        )
        self.begun.append(copy)
        copy.start()
        return copy

    def finish(self):
        for copy in self.begun:
            copy.wait_send()


class Place:
    def __init__(self):
        self.g, self.d = lax.axis_index("group"), lax.axis_index("dp")
        e = lax.axis_index("expert")
        self.x, self.y = lax.div(e, 4), lax.rem(e, 4)

    def along_x(self, step, over=0):
        return {"dp": lax.rem(self.d + over, 2), "expert": lax.rem(self.x + step, 4) * 4 + self.y}

    def along_y(self, step, over=0):
        return {"dp": lax.rem(self.d + over, 2), "expert": self.x * 4 + lax.rem(self.y + step, 4)}

    def other_dp(self):
        return {"dp": 1 - self.d}

    def in_group(self, step, along=0, over=0):
        return {"group": lax.rem(self.g + step, 4), **self.along_y(along, over)}

    def other_core(self):
        return {"group": self.g + 1 - 2 * lax.rem(self.g, 2)}


def hail(partners):
    barrier = pltpu.get_barrier_semaphore()
    for partner in partners:
        pl.semaphore_signal(barrier, inc=1, device_id=partner, device_id_type=MESH)


def await_hails(partners):
    pl.semaphore_wait(pltpu.get_barrier_semaphore(), len(partners))


PEERS = ((0, 1), (1, 0), (3, 0), (1, 1), (3, 1), (2, 0), (2, 1))


def ring_partners(place):
    return (
        [place.along_x(*peer) for peer in PEERS]
        + [place.along_y(step) for step in (1, 2, 3)]
        + [place.along_y(step, 1) for step in (1, 2, 3)]
    )


class Gather:
    def __init__(self, links, whole, h, p1, p2, near1, near2, at, share=None):
        self.links, self.whole, self.h, self.at = links, whole, h, at
        self.p1, self.p2, self.near1, self.near2, self.share = p1, p2, near1, near2, share
        self.steps, self.shared, self.round, self.passed = (0, 1, 3, 2), [], [], []

    def push(self, n, k2, to):
        c, x = self.at(lax.rem(self.p1 + 4 - self.steps[n], 4), lax.rem(k2, 4))
        ref = self.whole.at[c, x, self.h]
        return self.links.send(ref, ref, to)

    def give(self, n, k2):
        if self.share is not None:
            self.shared.append(self.push(n, k2, self.share))

    def start(self):
        self.direct = [self.push(0, self.p2, self.near1(step)) for step in self.steps[1:]]
        self.ring(0)

    def ring(self, n):
        if n:
            self.direct[n - 1].wait_recv()
        self.round.append([self.push(n, self.p2, self.near2(step)) for step in (1, 3)])
        self.give(n, self.p2)

    def forward(self, n):
        right, left = self.round[n]
        right.wait_recv()
        if n % 2 == 0:
            self.passed.append(self.push(n, self.p2 + 3, self.near2(1)))
        self.give(n, self.p2 + 3)
        left.wait_recv()
        if n % 2 == 1:
            self.passed.append(self.push(n, self.p2 + 1, self.near2(3)))
        self.give(n, self.p2 + 1)

    def end(self):
        for n, copy in enumerate(self.passed):
            copy.wait_recv()
            self.give(n, self.p2 + 2)
        for copy in self.shared:
            copy.wait_recv()


def run_gather(parts):
    for n in range(1, 6):
        for part in parts:
            if n < 4:
                part.ring(n)
            if n >= 2:
                part.forward(n - 2)
    for part in parts:
        part.end()


def gather_parts(links, place, whole):
    by_x = lambda kx, ky: (ky, kx)
    by_y = lambda ky, kx: (ky, kx)
    first = Gather(links, whole, 0, place.x, place.y, place.along_x, place.along_y, by_x)
    second = Gather(links, whole, 1, place.y, place.x, place.along_y, place.along_x, by_y)
    return first, second


class RingSum:
    def __init__(self, links, near1, near2, p1, p2, term, far, near, mid, box):
        self.links, self.near1, self.near2, self.p1, self.p2 = links, near1, near2, p1, p2
        self.term, self.far, self.near, self.mid, self.box = term, far, near, mid, box
        self.steps = (2, 1, 3, 0)
        self.far_copies, self.direct, self.summed, self.over = [], [], [], []

    def get(self, k, i):
        return self.term(lax.rem(self.p1 + k, 4), lax.rem(self.p2 + self.steps[i], 4))

    def send_far(self, i):
        self.far_copies.append(self.links.send(self.get(2, i), self.far.at[i], self.near1((1, 3)[i % 2])))

    def send_direct(self, i):
        step = (3, 1)[i % 2]
        self.direct.append(self.links.send(self.get(step, i), self.near.at[1, i], self.near1(step)))

    def middle(self, i):
        step = (1, 3)[i % 2]
        self.far_copies[i].wait_recv()
        self.far[i] = (self.far[i].astype(F32) + self.get(step, i)[...].astype(F32)).astype(BF16)
        self.summed.append(self.links.send(self.far.at[i], self.near.at[0, i], self.near1(step)))

    def finish(self, i):
        self.direct[i].wait_recv()
        self.summed[i].wait_recv()
        self.mid[i] = (
            self.get(0, i)[...].astype(F32) + self.near[0, i].astype(F32) + self.near[1, i].astype(F32)
        ).astype(BF16)
        step = self.steps[i]
        if step:
            self.over.append(self.links.send(self.mid.at[i], self.box.at[self.p2], self.near2(step)))
        else:
            self.box[self.p2] = self.mid[i]

    def total(self):
        for copy in self.over:
            copy.wait_recv()
        value = self.box[0].astype(F32)
        for k in range(1, 4):
            value = value + self.box[k].astype(F32)
        return value


def folded(rows):
    return jnp.concatenate([rows[:, :384], rows[:, 384:]], axis=0).astype(BF16)


def unfolded(rows):
    return jnp.concatenate([rows[:24], rows[24:]], axis=1)


def add_over(links, own, box, position, size, reach):
    box[position] = folded(own)
    copies = [links.send(box.at[position], box.at[position], reach(step)) for step in range(1, size)]

    def finish():
        for copy in copies:
            copy.wait_recv()
        total = box[0].astype(F32)
        for k in range(1, size):
            total = total + box[k].astype(F32)
        return unfolded(total)

    return finish


PIECES = (4, 48, 768)
HALF_SCRATCH = [VMEM(PIECES, BF16), VMEM((2, *PIECES), BF16), VMEM(PIECES, BF16), VMEM(PIECES, BF16)]
REDUCE_SCRATCH = HALF_SCRATCH * 2 + [VMEM((4, 48, 384), BF16), VMEM((4, 48, 384), BF16), VMEM((2, 48, 384), BF16)]
REDUCE_COPIES = 2 * 15 + 7
GATHER_COPIES = 2 * 15


class Reduction:
    def __init__(self, links, place, grads, scratch):
        self.links, self.place, self.boxes = links, place, scratch[8:]
        self.parts = (
            RingSum(
                links, place.along_y, place.along_x, place.y, place.x, lambda k, j: grads.at[k, j, 0], *scratch[:4]
            ),
            RingSum(
                links, place.along_x, place.along_y, place.x, place.y, lambda k, j: grads.at[j, k, 1], *scratch[4:8]
            ),
        )

    def start(self):
        for i in range(4):
            for part in self.parts:
                part.send_far(i)
        for part in self.parts:
            part.send_direct(0)

    def finish(self, extra, between=None):
        links, place, parts = self.links, self.place, self.parts
        box_x, box_y, box_z = self.boxes
        extra_x = add_over(links, extra, box_x, place.x, 4, place.along_x)
        for i in range(4):
            for part in parts:
                if i:
                    part.send_direct(i)
                part.middle(i)
            if i == 1:
                extra_y = add_over(links, extra_x(), box_y, place.y, 4, place.along_y)
            if i == 3:
                extra_z = add_over(links, extra_y(), box_z, place.d, 2, lambda step: place.other_dp())
        if between is not None:
            between()
        for i in range(4):
            for part in parts:
                part.finish(i)
        return [part.total() for part in parts], extra_z()


EPS_NORM = 1e-06
BETA_ONE = 0.9
BETA_TWO = 0.95
ADAM_EPS = 1e-08
DECAY = 0.1
OUTER_RATE = 0.7
OUTER_MOMENTUM = 0.9
REPLAY_WEIGHT = 0.25
RATES = (0.6, 0.04, 0.3, 0.03, 0.04, 0.02)
HEADS = 12
LEN = 128
STEPS = 2
STEP = 10


PIECE = 32
FIRST_PIECES = 4


class ExpertGather:
    def __init__(self, links, place, own, both):
        self.links, self.place, self.own, self.both = links, place, own, both
        self.far, self.near = [], []

    def rows(self, group, n=None):
        if n is None:
            return self.both.at[pl.ds(pl.multiple_of(group * 192, 192), 192)]
        return self.both.at[pl.ds(pl.multiple_of(group * 192 + n * PIECE, PIECE), PIECE)]

    def send(self, n):
        part = self.own.at[pl.ds(n * PIECE, PIECE)]
        self.far.append(self.links.send(part, self.rows(self.place.g, n), self.place.in_group(2)))

    def share(self):
        self.near.append(self.links.send(self.own, self.rows(self.place.g), self.place.other_core()))

    def pass_on(self, n):
        self.far[n].wait_recv()
        ref = self.rows(lax.rem(self.place.g + 2, 4), n)
        self.near.append(self.links.send(ref, ref, self.place.other_core()))

    def end(self):
        for copy in self.near:
            copy.wait_recv()


def halves(rows):
    return jnp.concatenate([rows[:, :384], rows[:, 384:]], axis=0)


def deal(links, place, src, box):
    box[place.d, place.y] = src[place.y, place.d]
    return [
        links.send(
            src.at[lax.rem(place.y + step, 4), lax.rem(place.d + over, 2)], box.at[place.d, place.y],
            place.along_y(step, over),
        )
        for step, over in PEERS
    ]


def assembled(place, box):
    upper, lower = box[:, :, :24], box[:, :, 24:]
    columns = jnp.concatenate([upper[0], upper[1]], axis=-1)
    rows = jnp.concatenate([upper, lower], axis=-1)
    rows = jnp.where(place.d == 0, rows[0], rows[1])
    return jnp.where(place.y == 3, rows, columns).reshape(2, 48, 768)


def dealt(wide, square, c, dp):
    if c < 3:
        return jnp.concatenate([wide[:, 768 * c + 384 * dp : 768 * c + 384 * dp + 384]] * 2, axis=0)
    return halves(square)


def placed(values, lane, form):
    count = values.shape[1 if form == "nn" else 0]
    pick = lax.broadcasted_iota(jnp.int32, (count, 128), 0) + lane == lax.broadcasted_iota(jnp.int32, (count, 128), 1)
    return lax.dot_general(
        values, pick.astype(F32), DIMS[form], precision=lax.Precision.HIGHEST, preferred_element_type=F32
    )


def entry_part(place, links, tokens, w_qkv, w_proj, e_in, in_hbm, out_hbm, whole, p_out, pe_out, mve_out, x_pair, both,
               p_in, own, loaded, e_out, p_box, local_sems, partners):
    loads = [
        pltpu.make_async_copy(
            src.at[pl.ds(128 * part, size)], loaded.at[k, part, pl.ds(0, size)], local_sems.at[2 * k + part]
        )
        for k, src in enumerate((in_hbm, out_hbm))
        for part, size in ((0, 128), (1, 64))
    ]
    for copy in loads:
        copy.start()
    for c in range(4):
        for dp in range(2):
            p_in[c, dp] = dealt(w_qkv, w_proj[...], c, dp).astype(BF16)
    await_hails(partners)
    x, y, d = place.x, place.y, place.d
    h = lax.rem(place.g, 2)
    masters = deal(links, place, p_in, p_box)
    router, gains, s_router, s_gains = e_in
    e_out[d, x, y] = (
        placed(router[...], 0, "nn") + placed(gains[...], 17, "tn")
        + placed(s_router[0], 24, "nn") + placed(s_gains[0], 41, "tn")
        + placed(s_router[1], 48, "nn") + placed(s_gains[1], 65, "tn")
    )
    mine = e_out.at[d, x, y]
    extra_z = links.send(mine, mine, place.other_dp())
    pair = links.send(tokens.at[0], x_pair, place.other_dp())
    for k in range(2):
        for part, size in ((0, 128), (1, 64)):
            loads[2 * k + part].wait()
            own[128 * part : 128 * part + size, 1536 * k : 1536 * k + 1536] = loaded[k, part, :size].astype(BF16)
    experts = ExpertGather(links, place, own, both)
    mine_there = pltpu.make_async_copy(own, experts.rows(place.g), local_sems.at[4])
    mine_there.start()
    for n in range(FIRST_PIECES):
        experts.send(n)
    for copy in masters:
        copy.wait_recv()
    master = assembled(place, p_box[...].astype(F32))
    p_out[...] = master

    @pl.when(h == 0)
    def _():
        whole[y, x, 0] = master[0].astype(BF16)

    @pl.when(h == 1)
    def _():
        whole[y, x, 1] = master[1].astype(BF16)

    def mix(a, b):
        return a * (1 - h) + b * h

    def near1(step, over=0):
        one, two = place.along_x(step, over), place.along_y(step, over)
        return {"dp": one["dp"], "expert": mix(one["expert"], two["expert"])}

    def near2(step):
        one, two = place.along_y(step), place.along_x(step)
        return {"dp": one["dp"], "expert": mix(one["expert"], two["expert"])}

    def at(k1, k2):
        return mix(k2, k1), mix(k1, k2)

    part = Gather(links, whole, h, mix(x, y), mix(y, x), near1, near2, at, place.other_core())
    part.start()
    extra_z.wait_recv()
    mine = e_out.at[:, x, y]
    extra_x = [links.send(mine, mine, place.along_x(k)) for k in (1, 2, 3)]
    for n in (1, 2, 3):
        part.ring(n)
        part.forward(n - 1)
    for copy in extra_x:
        copy.wait_recv()
    mine = e_out.at[:, :, y]
    extra_y = [links.send(mine, mine, place.along_y(k)) for k in (1, 2, 3)]
    part.forward(3)
    part.end()
    experts.share()
    for copy in extra_y:
        copy.wait_recv()
    turned = e_out[...].reshape(768, 128).T
    pe_out[...] = turned[:24]
    mve_out[0] = turned[24:48]
    mve_out[1] = turned[48:72]
    pair.wait_recv()

    def end():
        experts.end()
        mine_there.wait()

    return experts, end


def adam_values(master, first, second, grad, rate, number):
    first = BETA_ONE * first + (1.0 - BETA_ONE) * grad
    second = BETA_TWO * second + (1.0 - BETA_TWO) * grad * grad
    level = second * (1.0 / (1.0 - BETA_TWO**number))
    below = level * lax.rsqrt(jnp.maximum(level, 1e-30)) + ADAM_EPS
    guess = pl.reciprocal(below, approx=True)
    update = first * ((1.0 / (1.0 - BETA_ONE**number)) * rate) * (guess * (2.0 - below * guess))
    return master - (update + (rate * DECAY) * master), first, second


def block_rate(place):
    return jnp.where(place.y == 3, RATES[2], RATES[1]).astype(F32)


def extra_rates():
    row = lax.broadcasted_iota(jnp.int32, (24, 768), 0)
    return jnp.where(row < 17, RATES[3], RATES[0]).astype(F32)


def renew_part(number, place, links, reduction, extra, moments, mv_box, p_in, pe_in, mve_in,
               whole, p_out, mv_out, pe_out, mve_out):
    sums, total = reduction.finish(extra)
    parts = gather_parts(links, place, whole)
    for copy in moments:
        copy.wait_recv()
    moment = mv_box[...].astype(F32)
    old = [assembled(place, moment[:, :, 48 * k : 48 * k + 48]) for k in range(2)]
    for h, part in enumerate(parts):
        fresh, first, second = adam_values(p_in[h], old[0][h], old[1][h], sums[h], block_rate(place), number)
        whole[place.y, place.x, h] = fresh.astype(BF16)
        part.start()
        p_out[h] = fresh
        mv_out[0, h] = first
        mv_out[1, h] = second
    pe_out[...], mve_out[0], mve_out[1] = adam_values(pe_in[...], mve_in[0], mve_in[1], total, extra_rates(), number)
    run_gather(parts)


def outer(begin, moment, mean):
    renewed = OUTER_MOMENTUM * moment + mean
    return begin - OUTER_RATE * (mean + OUTER_MOMENTUM * renewed), renewed


def own_features(place, rows, turned):
    at = 24 * (16 * place.d + 4 * place.x + place.y)
    pick = (lax.broadcasted_iota(jnp.int32, (768, 24), 0) == at + lax.broadcasted_iota(jnp.int32, (768, 24), 1)).astype(BF16)
    total = 0.0
    for _ in range(3):
        part = rows.astype(BF16)
        total = total + (
            lax.dot_general(pick, part, (((0,), (1,)), ((), ())), preferred_element_type=F32) if turned
            else lax.dot_general(part, pick, (((1,), (0,)), ((), ())), preferred_element_type=F32)
        )
        rows = rows - part.astype(F32)
    return total


class ExpertMean:
    def __init__(self, links, place, copies, deltas, others, own, other, sent, far):
        self.links, self.place, self.own, self.other, self.sent, self.far = links, place, own, other, sent, far
        self.high = lax.div(place.g, 2)
        self.loads = [copies.start(delta.at[:, lax.rem(place.g, 2)], own.at[k]) for k, delta in enumerate(deltas)]
        self.loads += [copies.start(array, other.at[k]) for k, array in enumerate(others)]

    def start(self):
        for copy in self.loads:
            copy.wait()
        self.copies = []
        self.push()
        self.push()

    def push(self):
        k, rows = len(self.copies) // 2, pl.ds(len(self.copies) % 2 * 96, 96)
        self.sent[k, rows] = (
            self.own[k, 1 - self.high, rows].astype(F32) + self.other[k, 1 - self.high, rows].astype(F32)
        ).astype(BF16)
        self.copies.append(self.links.send(self.sent.at[k, rows], self.far.at[k, rows], self.place.in_group(2)))

    def mean(self, k):
        for copy in self.copies[2 * k : 2 * k + 2]:
            copy.wait_recv()
        mine = self.own[k, self.high].astype(F32) + self.other[k, self.high].astype(F32)
        return (mine + self.far[k].astype(F32)) * 0.25


def final_part(number, place, links, reduction, extra, experts, p_in, mv_in, pe_in, mve_in, p_start, pe_start,
               mean_out, flat_out, turned_out, turned, delta, quarters, mean, boxes):
    g, y = place.g, place.y
    sums, total = reduction.finish(extra, experts.push)
    for h in range(2):
        fresh, _, _ = adam_values(p_in[h], mv_in[0, h], mv_in[1, h], sums[h], block_rate(place), number)
        rows = (p_start[h] - fresh).reshape(2, 24, 768)
        for k in range(2):
            delta[2 * h + k] = folded(rows[k])
    summed = [
        links.send(delta.at[lax.rem(g + k, 4)], quarters.at[g], place.in_group(k)) for k in (1, 2, 3)
    ]
    fresh_e, _, _ = adam_values(pe_in[...], mve_in[0], mve_in[1], total, extra_rates(), number)
    sum_e = add_over(links, pe_start[...] - fresh_e, boxes, g, 4, place.in_group)
    experts.push()
    quarters[g] = delta[g]
    for copy in summed:
        copy.wait_recv()
    mean[...] = (
        (quarters[0].astype(F32) + quarters[1].astype(F32) + quarters[2].astype(F32) + quarters[3].astype(F32)) * 0.25
    ).astype(BF16)
    d, at = place.d, links.used
    links.used += 8

    def spread(k, over):
        return pltpu.make_async_remote_copy(
            src_ref=mean, dst_ref=turned.at[d, y], send_sem=links.sends.at[at + 2 * k + over],
            recv_sem=links.recvs.at[at + 2 * y + d],
            device_id={"group": lax.rem(g + k, 4), "dp": lax.rem(d + over, 2), "expert": place.x * 4 + g},
            device_id_type=MESH,
        )

    def arrival(dp, c):
        return pltpu.make_async_remote_copy(
            src_ref=mean, dst_ref=turned.at[dp, c], send_sem=links.sends.at[at], recv_sem=links.recvs.at[at + 2 * c + dp],
            device_id=place.other_core(), device_id_type=MESH,
        )

    others = [(k, over) for k in range(4) for over in range(2) if k or over]
    for k, over in others:
        spread(k, over).start()

    @pl.when(y != g)
    def _():
        spread(0, 0).start()

    @pl.when(y == g)
    def _():
        turned[d, y] = mean[...]

    mean_e = sum_e() * 0.25
    flat_out[...] = own_features(place, mean_e, False)
    turned_out[...] = own_features(place, mean_e, True)
    for dp in range(2):
        for c in range(4):
            @pl.when(jnp.logical_or(y != g, jnp.logical_or(c != y, dp != d)))
            def _(c=c, dp=dp):
                arrival(dp, c).wait_recv()

    for k, over in others:
        spread(k, over).wait_send()

    @pl.when(y != g)
    def _():
        spread(0, 0).wait_send()

    landed = turned[...].astype(F32)
    upper, lower = landed[:, :, :24], landed[:, :, 24:]
    for c in range(3):
        mine = jnp.where(d == 0, upper[:, c], lower[:, c])
        mean_out[c] = jnp.concatenate([mine[0], mine[1]], axis=-1)
    rows = jnp.concatenate([upper[:, 3], lower[:, 3]], axis=-1)
    mean_out[3] = jnp.where(d == 0, rows[0], rows[1])


def semaphores(count):
    return [pltpu.SemaphoreType.DMA((count,)), pltpu.SemaphoreType.DMA((count,))]


ANY = pl.ANY
WHOLE = (4, 4, 2, 48, 768)
BLOCK = (2, 48, 768)
ROW = (128, 768)


def call(kernel, outs, scratch, collective_id, args, limit=60 << 20):
    return pl.pallas_call(
        kernel,
        out_shape=tuple(jax.ShapeDtypeStruct(shape, kind) for _, shape, kind in outs),
        in_specs=[pl.BlockSpec(memory_space=space) for space, _ in args],
        out_specs=tuple(pl.BlockSpec(memory_space=space) for space, _, _ in outs),
        scratch_shapes=scratch,
        compiler_params=pltpu.CompilerParams(
            collective_id=collective_id, has_side_effects=True, vmem_limit_bytes=limit
        ),
    )(*(array for _, array in args))

CAP = 24
TOK = 128


def mm(a, b, form="nn"):
    return lax.dot_general(a, b, DIMS[form], preferred_element_type=F32)


def split_low(values):
    high = values.astype(BF16)
    return high, (values - high.astype(F32)).astype(BF16)


def row_scale(values):
    return lax.rsqrt(jnp.mean(values * values, axis=-1, keepdims=True) + EPS_NORM)


def iota(shape, dim):
    return lax.broadcasted_iota(jnp.int32, shape, dim)


def routing(ids):
    names = [(iota((24, TOK), 0) == ids[k : k + 1]).astype(F32) for k in range(2)]
    either = names[0] + names[1]
    earlier = (iota((TOK, TOK), 0) < iota((TOK, TOK), 1)).astype(BF16)
    slot = mm(either.astype(BF16), earlier).astype(jnp.int32)
    taken = jnp.where(iota((17, CAP, TOK), 1) == slot[:17][:, None, :], 1.0, 0.0)
    return names, taken * either[:17][:, None, :]


def pair_stack(part):
    lane = iota(part.shape, 1)
    zero = jnp.zeros_like(part)
    return jnp.concatenate([jnp.where(lane < 64, part, zero), jnp.where(lane < 64, zero, part)], axis=0)


def side_by_side(stacked):
    return jnp.concatenate([stacked[:TOK], stacked[TOK:]], axis=1)


def flat(whole, c):
    return whole[c].reshape(384, 768)


def cotangent(og_ref, ids_ref):
    factor = jnp.where(ids_ref[1][...] > 0, REPLAY_WEIGHT, 1.0)
    spread = jnp.where(iota((TOK, TOK), 0) == iota((TOK, TOK), 1), factor, 0.0).astype(BF16)
    return mm(spread, og_ref[...])


def across(rows, weight):
    return mm(rows[:, :384], weight[:, :384]) + mm(rows[:, 384:], weight[:, 384:])


def front_part(x_ref, pair_ref, og_ref, ids_ref, pe_ref, whole,
               send, frozen, qkv_out, probs_out, mixed_out, middle_out, a1_out, a2_out, weights_out, swap):
    gain = pe_ref[16:24].astype(BF16).astype(F32)
    row, col = iota((2 * TOK, TOK), 0), iota((2 * TOK, TOK), 1)
    causal = lax.rem(row, TOK) >= col
    x = x_ref[...].astype(F32)
    finish = None
    for t, values in ((1, pair_ref[...].astype(F32)), (0, x)):
        a1 = (values * row_scale(values) * gain[1:2]).astype(BF16)
        a1_out[t] = a1
        for c in range(3):
            qkv_out[t, c] = across(a1, flat(whole, c)).astype(BF16)
        for pair in range(3):
            lanes = slice(128 * pair, 128 * pair + 128)
            scores = mm(pair_stack(qkv_out[t, 0, :, lanes]), qkv_out[t, 1, :, lanes], "nt") * 0.125
            scores = jnp.where(causal, scores, -1e30)
            expo = jnp.exp(scores - jnp.max(scores, axis=-1, keepdims=True))
            probs = expo / jnp.sum(expo, axis=-1, keepdims=True)
            probs_out[t, pair] = probs
            mixed_out[t, :, lanes] = mm(
                side_by_side(probs.astype(BF16)), pair_stack(qkv_out[t, 2, :, lanes])
            ).astype(BF16)
        branch = mm(mixed_out[t], flat(whole, 3))
        if t:
            finish = swap(branch.astype(BF16))
    middle = x + branch + finish()
    middle_out[...] = middle
    a2 = (middle * row_scale(middle) * gain[2:3]).astype(BF16)
    a2_out[...] = a2
    logits = mm(pe_ref[...].astype(BF16), a2, "nt")
    names, taken = routing(ids_ref[0][...])
    picked = [jnp.sum(name * logits, axis=0, keepdims=True) for name in names]
    top = jnp.maximum(picked[0], picked[1])
    expo = [jnp.exp(z - top) for z in picked]
    whole_sum = expo[0] + expo[1]
    weights = [e / whole_sum for e in expo]
    weights_out[...] = jnp.concatenate(weights + [jnp.zeros((6, TOK), F32)], axis=0)
    by_expert = names[0] * weights[0] + names[1] * weights[1]
    row_weight = jnp.sum(taken * by_expert[:17][:, None, :], axis=-1, keepdims=True)
    cot = cotangent(og_ref, ids_ref).astype(BF16)
    low = taken.astype(BF16).reshape(17 * CAP, TOK)
    rows = mm(low, a2).reshape(17, CAP, 768)
    grads = mm(low, cot).reshape(17, CAP, 768) * row_weight
    both = jnp.concatenate([rows, grads], axis=1).astype(BF16)
    frozen[...] = both[0]
    send[...] = both[1:]


def back_part(x_ref, og_ref, ids_ref, pe_ref, whole, qkv, probs_ref, mixed, middle_ref, a1, a2,
              weights_ref, ret, frozen, block_out, grad_out, grads, arrived, ready, swap, early, late):
    gain = pe_ref[16:24].astype(BF16).astype(F32)
    low_rows = pe_ref[...].astype(BF16)
    cot = cotangent(og_ref, ids_ref)
    names, taken = routing(ids_ref[0][...])
    weights = [weights_ref[k : k + 1] for k in range(2)]
    by_expert = names[0] * weights[0] + names[1] * weights[1]
    row_weight = jnp.sum(taken * by_expert[:17][:, None, :], axis=-1, keepdims=True)
    low = taken.astype(BF16).reshape(17 * CAP, TOK)
    both = ret[...].astype(F32)
    both = jnp.concatenate([frozen[...][None], both], axis=0)
    results, back = both[:, :CAP], both[:, CAP:].reshape(17 * CAP, 768)
    middle = middle_ref[...]
    cot_rows = mm(low, cot.astype(BF16)).reshape(17, CAP, 768)
    grad_row = jnp.sum(cot_rows * results, axis=-1, keepdims=True)
    by_name = jnp.concatenate([jnp.sum(taken * grad_row, axis=1), jnp.zeros((7, TOK), F32)], axis=0)
    grad_w = [jnp.sum(name * by_name, axis=0, keepdims=True) for name in names]
    mean = weights[0] * grad_w[0] + weights[1] * grad_w[1]
    grad_logits = sum(names[k] * (weights[k] * (grad_w[k] - mean)) for k in range(2))
    logit_parts = split_low(grad_logits)
    da2 = sum(mm(part, low_rows, "tn") for part in logit_parts)
    da2 = da2 + sum(mm(low, part, "tn") for part in split_low(back))
    scale = row_scale(middle)
    normed = middle * scale
    dg2 = jnp.sum(normed * da2, axis=0, keepdims=True)
    into = da2 * gain[2:3]
    dmiddle = cot + scale * (into - normed * jnp.mean(into * normed, axis=-1, keepdims=True))
    branch = dmiddle.astype(BF16)
    arrived()
    finish = swap(0, branch)
    early()
    branches = [branch]
    dqkv = [[], [], []]
    for t in range(2):
        if t:
            branches.append(finish())
        dmixed = mm(branches[t], flat(whole, 3), "nt").astype(BF16)
        parts = [[], [], []]
        for pair in range(3):
            lanes = slice(128 * pair, 128 * pair + 128)
            probs = probs_ref[t, pair]
            dms = pair_stack(dmixed[:, lanes])
            parts[2].append(mm(probs.astype(BF16), dms, "tn").astype(BF16))
            dpb = mm(dms, qkv[t, 2, :, lanes], "nt")
            ds = (probs * (dpb - jnp.sum(probs * dpb, axis=-1, keepdims=True))).astype(BF16)
            parts[0].append((mm(side_by_side(ds), pair_stack(qkv[t, 1, :, lanes])) * 0.125).astype(BF16))
            parts[1].append((mm(ds, pair_stack(qkv[t, 0, :, lanes]), "tn") * 0.125).astype(BF16))
        for c in range(3):
            dqkv[c].append(jnp.concatenate(parts[c], axis=1))
    a1_both = a1[...].reshape(2 * TOK, 768)
    for c in range(3):
        both = jnp.concatenate(dqkv[c], axis=0)
        grads[c] = jnp.concatenate(
            [mm(a1_both[:, :384], both, "tn"), mm(a1_both[:, 384:], both, "tn")], axis=1
        ).astype(BF16).reshape(4, 2, 48, 768)
    grads[3] = mm(
        mixed[...].reshape(2 * TOK, 384), jnp.concatenate(branches, axis=0), "tn"
    ).astype(BF16).reshape(4, 2, 48, 768)
    ready()

    def into_a1(t):
        halves_of = [
            sum(mm(dqkv[c][t], flat(whole, c)[:, side], "nt") for c in range(3))
            for side in (slice(0, 384), slice(384, 768))
        ]
        return jnp.concatenate(halves_of, axis=1)

    finish = swap(1, into_a1(1).astype(BF16))
    late()
    da1 = into_a1(0)
    grad_router = sum(mm(part, a2[...]) for part in logit_parts)
    block_out[...] = (
        middle + sum(mm(low, part, "tn") for part in split_low((results * row_weight).reshape(17 * CAP, 768)))
    ).astype(BF16)
    da1 = da1 + finish().astype(F32)
    x = x_ref[...].astype(F32)
    scale = row_scale(x)
    normed = x * scale
    dg1 = jnp.sum(normed * da1, axis=0, keepdims=True)
    into = da1 * gain[1:2]
    grad_out[...] = dmiddle + scale * (into - normed * jnp.mean(into * normed, axis=-1, keepdims=True))
    return jnp.concatenate([grad_router[:17], dg1, dg2, jnp.zeros((5, 768), F32)], axis=0)


SQRT_HALF = 0.7071067811865476
DENSITY = 0.3989422804014327


def expert_rows(rows, grad, first, second):
    u = mm(rows, first)
    chance = 0.5 + 0.5 * lax.erf(u * SQRT_HALF)
    h = (u * chance).astype(BF16)
    value = mm(h, second)
    slope = chance + u * (jnp.exp(u * u * -0.5) * DENSITY)
    du = (slope * mm(grad, second, "nt")).astype(BF16)
    return value, mm(du, first, "nt"), h, du


class Copies:
    def __init__(self, sems):
        self.sems, self.used = sems, 0

    def start(self, src, dst):
        copy = pltpu.make_async_copy(src, dst, self.sems.at[self.used])
        self.used += 1
        copy.start()
        return copy


def grow_experts(first_step, number, copies, rows, grad, h, du, w1, w2, mv1, mv2, starts, news, bufs, between):
    (mv1_buf, mv2_buf, d1_buf, d2_buf, w1_out, w2_out, mv1_out, mv2_out, d1_out, d2_out) = bufs
    tiles = [(0, t) for t in range(6)] + [(1, t) for t in range(6)]

    def cut(which, t):
        size = (128, 256)[which]
        return pl.ds(size * t, size), slice(None)

    def parts_of(t):
        begin, end = 128 * t, 128 * t + 128
        cuts = sorted({begin, end} | {192 * q for q in range(5) if begin < 192 * q < end})
        return [(low // 192, low % 192, high - low, low - begin) for low, high in zip(cuts, cuts[1:])]

    def load(n):
        which, t = tiles[n]
        slot = n % 2
        mv, buf = ((mv1, mv1_buf), (mv2, mv2_buf))[which]
        size = (128, 256)[which]
        begun = [copies.start(mv.at[:, pl.ds(size * t, size)], buf.at[slot])]
        if not first_step:
            begun.append(copies.start(starts[which].at[cut(which, t)], (d1_buf, d2_buf)[which].at[slot]))
        return begun

    loads = {0: load(0)}
    stores = {}
    for n, (which, t) in enumerate(tiles):
        slot = n % 2
        if n + 1 < len(tiles):
            loads[n + 1] = load(n + 1)
        for copy in loads[n]:
            copy.wait()
        for copy in stores.pop(n - 2, ()):
            copy.wait()
        if which == 0:
            value = mm(rows[:, 128 * t : 128 * t + 128], du[...], "tn")
            begin = w1[128 * t : 128 * t + 128].astype(F32)
            moments = mv1_buf
        else:
            value = mm(h[:, 256 * t : 256 * t + 256], grad[...], "tn")
            begin = w2[256 * t : 256 * t + 256].astype(F32)
            moments = mv2_buf
        fresh, first, second = adam_values(
            begin, moments[slot, 0].astype(F32), moments[slot, 1].astype(F32), value, RATES[4 + which], number
        )
        here = cut(which, t)
        if first_step:
            low, mv_low = (w1_out, w2_out)[which], (mv1_out, mv2_out)[which]
            low[slot] = fresh.astype(BF16)
            mv_low[slot, 0] = first.astype(BF16)
            mv_low[slot, 1] = second.astype(BF16)
            size = (128, 256)[which]
            stores[n] = [
                copies.start(low.at[slot], news[which].at[here]),
                copies.start(mv_low.at[slot], news[2 + which].at[:, pl.ds(size * t, size)]),
            ]
        else:
            change = (d1_buf, d2_buf)[which][slot].astype(F32) - fresh
            if which == 0:
                d1_out[slot] = change.astype(BF16)
                stores[n] = [
                    copies.start(d1_out.at[slot, pl.ds(inside, size)], news[0].at[q // 2, q % 2, pl.ds(low, size)])
                    for q, low, size, inside in parts_of(t)
                ]
            else:
                d2_out[slot] = change.astype(BF16).T.reshape(2, 2, 192, 256)
                stores[n] = [copies.start(d2_out.at[slot], news[1].at[:, :, :, pl.ds(256 * t, 256)])]
        between(n, stores)
    return [copy for group in (len(tiles) - 2, len(tiles) - 1) for copy in stores.get(group, ())]


KEPT = [((2, 3, 128, 384), BF16), ((2, 3, 256, 128), F32), ((2, 128, 384), BF16), (ROW, F32), ((2, *ROW), BF16), (ROW, BF16),
        ((8, 128), F32)]


def trade_kernel(first_step, number, *refs):
    if first_step:
        (x, og, ids, replay, w_qkv, w_proj, *e_in), (in_hbm, out_hbm), refs = refs[:10], refs[10:12], refs[12:]
    else:
        (x, og, ids, replay, pe, pair, whole_hbm, both_hbm, w2_start, w1_hbm, w2_hbm), refs = refs[:11], refs[11:]
        starts = (both_hbm.at[:, :1536], w2_start)
    tokens = x
    step = 0 if first_step else 1
    x, og, ids = x.at[step], og.at[step], (ids.at[step], replay.at[pl.ds(step, 1)])
    (fin_hbm, fout_hbm, mv1, mv2), refs = refs[:4], refs[4:]
    kept_out, refs = refs[:7], refs[7:]
    ret, frozen_out, refs = refs[0], refs[1], refs[2:]
    news, others, refs = refs[:4], refs[2:4], refs[4:]
    if first_step:
        (w2_start, whole_out, p_out, pe, mve_out, both_hbm), refs = refs[:6], refs[6:]
        starts = ()
    kept, refs = refs[:7], refs[7:]
    (whole, w1, w2, fin, fout, send, frozen_in, recv, ans, zret, home, rows_all, grad_all, h_all, du_all, local_sems,
     in_send, in_recv, z_send, z_recv, zb_send, zb_recv, home_send, home_recv,
     core_send, core_recv, swap_send, swap_recv, swapped), refs = refs[:29], refs[29:]
    w2_turned = du_all
    bufs, refs = refs[:10], refs[10:]
    copies = Copies(local_sems)
    loads = [] if first_step else [copies.start(whole_hbm, whole)]
    loads += [copies.start(fin_hbm, fin), copies.start(fout_hbm, fout)]
    if not first_step:
        loads += [copies.start(w1_hbm, w1), copies.start(w2_hbm, w2)]
    d, e = lax.axis_index("dp"), lax.axis_index("expert")
    partner = {"dp": 1 - d}
    g = lax.axis_index("group")
    core = lax.rem(g, 2)
    other_core = {"group": g + 1 - 2 * core}

    def ahead(k):
        return lax.rem(e + k, 16)

    def behind(k):
        return lax.rem(e + 16 - k, 16)

    barrier = pltpu.get_barrier_semaphore()

    @pl.loop(1, 16)
    def _(k):
        pl.semaphore_signal(barrier, inc=1, device_id={"expert": ahead(k)}, device_id_type=MESH)

    if first_step:
        pair, p_in, own, e_out, p_box, entry_sems, entry_sends, entry_recvs = refs
        place, links = Place(), Links(entry_sends, entry_recvs)
        more = [place.along_x(step, 1) for step in range(4)] + [place.along_y(step, 1) for step in (1, 2, 3)]
        more += [place.other_core(), place.in_group(2)]
        hail(more)
        experts, experts_end = entry_part(
            place, links, tokens, w_qkv, w_proj, e_in, in_hbm, out_hbm, whole, p_out, pe, mve_out, pair, both_hbm,
            p_in, own, bufs[0], e_out, p_box, entry_sems, more + [None] * 15,
        )
        whole_kept = copies.start(whole, whole_out)
    else:
        pl.semaphore_signal(barrier, inc=1, device_id=partner, device_id_type=MESH)
        pl.semaphore_signal(barrier, inc=1, device_id=other_core, device_id_type=MESH)
        loads.pop(0).wait()

    def swap(branch):
        if not first_step:
            pl.semaphore_wait(barrier, 17)
        swapped[0] = branch
        copy = remote(swapped.at[0], swapped.at[1], swap_send, swap_recv, 0, partner)
        copy.start()
        if first_step:
            for n in range(FIRST_PIECES, 192 // PIECE):
                experts.send(n)

        def finish():
            copy.wait()
            return swapped[1].astype(F32)

        return finish

    def remote(src, dst, sends, recvs, k, to):
        return pltpu.make_async_remote_copy(
            src_ref=src, dst_ref=dst, send_sem=sends.at[k], recv_sem=recvs.at[k], device_id=to, device_id_type=MESH
        )

    front_part(x, pair, og, ids, pe, whole, send, frozen_in, *kept, swap)

    def to_expert(k):
        return remote(send.at[ahead(k)], recv.at[0, e], in_send, in_recv, k, {"expert": ahead(k)})

    def to_partner(k):
        return remote(recv.at[0, behind(k)], recv.at[1, behind(k)], z_send, z_recv, k, partner)

    def from_partner(k):
        return remote(ans.at[1, behind(k)], zret.at[behind(k)], zb_send, zb_recv, k, partner)

    def to_home(k):
        return remote(home.at[behind(k)], ret.at[e], home_send, home_recv, k, {"expert": behind(k)})

    @pl.loop(1, AT_ONCE + 1)
    def _(k):
        to_expert(k).start()

    recv[0, e] = send[e]
    to_partner(0).start()
    keeps = [copies.start(src, dst) for src, dst in zip(kept, kept_out)]

    def pass_on(k):
        to_expert(k).wait_recv()
        to_partner(k).start()

        @pl.when(k + AT_ONCE < 16)
        def _():
            to_expert(k + AT_ONCE).start()

    pl.loop(1, 6)(pass_on)
    if first_step:
        for n in range(192 // PIECE):
            experts.pass_on(n)
    for copy in loads[:2]:
        copy.wait()
    both = frozen_in[...].astype(F32)
    value, back, _, _ = expert_rows(both[:CAP].astype(BF16), both[CAP:].astype(BF16), fin[...], fout[...])
    frozen_out[...] = jnp.concatenate([value, back], axis=0)
    pl.loop(6, 16)(pass_on)
    if first_step:
        experts_end()
        loads += [copies.start(both_hbm.at[:, :1536], w1), copies.start(both_hbm.at[:, 1536:], w2_turned)]
    for copy in loads[2:]:
        copy.wait()
    if first_step:
        for t in range(6):
            w2[256 * t : 256 * t + 256] = w2_turned[:, 256 * t : 256 * t + 256].T
        keeps += [copies.start(w2, w2_start), whole_kept]

    @pl.loop(0, 4)
    def _(j):
        other = lax.rem(lax.div(j + 1, 2) + 1, 2)
        half = lax.div(j, 2)

        @pl.when(other == 1)
        def _():
            @pl.loop(0, 8)
            def _(i):
                to_partner(half * 8 + i).wait_recv()

        blocks = [recv[other, behind(half * 8 + i)].astype(F32) for i in range(8)]
        rows = jnp.concatenate([b[:CAP] for b in blocks], axis=0).astype(BF16)
        grad = jnp.concatenate([b[CAP:] for b in blocks], axis=0).astype(BF16)
        value, back, h, du = expert_rows(rows, grad, w1[...], w2[...])
        at = pl.ds(pl.multiple_of(j * 192, 192), 192)
        rows_all[at] = rows
        grad_all[at] = grad
        h_all[at] = h
        du_all[at] = du
        for i in range(8):
            part = slice(i * CAP, (i + 1) * CAP)
            ans[other, behind(half * 8 + i)] = jnp.concatenate([value[part], back[part]], axis=0).astype(BF16)

        @pl.when(other == 1)
        def _():
            @pl.loop(0, 8)
            def _(i):
                from_partner(half * 8 + i).start()

    def serve(k):
        from_partner(k).wait_recv()
        slot = behind(k)
        total = (ans[0, slot].astype(F32) + zret[slot].astype(F32)).astype(BF16)
        if k == 0:
            ret[e] = total
        else:
            home[slot] = total
            to_home(k).start()

    def to_core(which):
        return remote(news[which].at[:, 1 - core], others[which], core_send, core_recv, which, other_core)

    def between(n, stores):
        for k in range(SERVED[n], SERVED[n + 1]):
            serve(k)
        if not first_step and n in (7, 11):
            for tile in ((4, 5) if n == 7 else (10, 11)):
                for copy in stores.pop(tile, ()):
                    copy.wait()
            to_core(0 if n == 7 else 1).start()

    for k in range(SERVED[0]):
        serve(k)
    left = grow_experts(
        first_step, number, copies, rows_all, grad_all, h_all, du_all, w1, w2, mv1, mv2, starts, news, bufs, between
    )

    @pl.loop(1, 16)
    def _(k):
        to_home(k).wait_recv()
        to_home(k).wait_send()
        to_expert(k).wait_send()

    @pl.loop(0, 16)
    def _(k):
        to_partner(k).wait_send()
        from_partner(k).wait_send()

    if not first_step:
        for which in range(2):
            to_core(which).wait_recv()
            to_core(which).wait_send()
    for copy in left + keeps:
        copy.wait()
    if first_step:
        links.finish()


AT_ONCE = 8
SERVED = (3, 4, 6, 7, 9, 10, 12, 13, 15, 16, 16, 16, 16)


def trade_call(first_step, number, collective_id, small, *large):
    wide = (768, 1536)
    moment_kind = F32 if first_step else BF16
    tall, quarters = (1536, 768), (2, 2, 192, 1536)
    news = (
        [(ANY, wide, BF16), (ANY, tall, BF16), (ANY, (2, 768, 1536), BF16), (ANY, (2, 1536, 768), BF16), (ANY, tall, BF16),
         (ANY, WHOLE, BF16), (VMEM, BLOCK, F32), (VMEM, (24, 768), F32), (VMEM, (2, 24, 768), F32), (ANY, (768, 3072), BF16)]
        if first_step else [(ANY, quarters, BF16)] * 2 + [(ANY, (2, 192, 1536), BF16)] * 2
    )
    outs = [(ANY, *k) for k in KEPT] + [(VMEM, (16, 48, 768), BF16), (VMEM, (48, 768), F32)] + news
    t1, t2, c1, c2 = (2, 2, 128, 1536), (2, 2, 256, 768), (2, 128, 1536), (2, 256, 768)
    none = (8, 128)
    first = first_step
    bufs = [
        VMEM(t1, moment_kind), VMEM(t2, moment_kind),
        VMEM(none if first else c1, BF16), VMEM(none if first else c2, BF16),
        VMEM(c1 if first else none, BF16), VMEM(c2 if first else none, BF16),
        VMEM(t1 if first else none, BF16), VMEM(t2 if first else none, BF16),
        VMEM(none if first else c1, BF16), VMEM(none if first else (2, 2, 2, 192, 256), BF16),
    ]
    plane = (16, 48, 768)
    scratch = [VMEM(*k) for k in KEPT] + [
        VMEM(WHOLE, BF16), VMEM(wide, BF16), VMEM(tall, BF16), VMEM((768, 3072), BF16), VMEM((3072, 768), BF16),
        VMEM(plane, BF16), VMEM((48, 768), BF16), VMEM((2, *plane), BF16), VMEM((2, *plane), BF16),
        VMEM(plane, BF16), VMEM(plane, BF16),
        VMEM((768, 768), BF16), VMEM((768, 768), BF16), VMEM(wide, BF16), VMEM(wide, BF16),
        pltpu.SemaphoreType.DMA((72,)),
    ] + semaphores(16) * 4 + semaphores(2) + semaphores(1) + [VMEM((2, *ROW), BF16)] + bufs
    if first_step:
        scratch += [
            VMEM(ROW, BF16), VMEM((4, 2, 48, 384), BF16), VMEM((192, 3072), BF16),
            VMEM((2, 4, 4, 24, 128), F32), VMEM((2, 4, 48, 384), BF16), pltpu.SemaphoreType.DMA((5,)),
        ] + semaphores(7 + 1 + 1 + 15 + 16 + 6 + 2 * (192 // PIECE) + 1)
    args = [(VMEM, a) for a in small] + [(ANY, a) for a in large]
    return call(functools.partial(trade_kernel, first_step, number), outs, scratch, collective_id, args, 62 << 20)


FETCHED = (0, 1, 2, 4)


def back_body(step, refs, scratch, copies, links, place, swapped, block_out, grad_out, grads, begin, ready, early, late):
    (x, og, ids, replay, pe), whole_hbm, kept, ret, frozen = refs[:5], refs[5], list(refs[6:13]), refs[13], refs[14]
    ids = (ids.at[step], replay.at[pl.ds(step, 1)])
    whole, buffers = scratch[0], scratch[1:5]
    loads = [copies.start(whole_hbm, whole)]
    for at, buffer in zip(FETCHED, buffers):
        loads.append(copies.start(kept[at], buffer))
        kept[at] = buffer

    def arrived():
        begin()
        for copy in loads:
            copy.wait()

    def swap(n, rows):
        swapped[n, 0] = rows
        copy = links.send(swapped.at[n, 0], swapped.at[n, 1], place.other_dp())

        def finish():
            copy.wait_recv()
            return swapped[n, 1]

        return finish

    return back_part(
        x.at[step], og.at[step], ids, pe, whole, *kept, ret, frozen, block_out, grad_out, grads, arrived, ready, swap, early, late
    )


BACK_SCRATCH = [VMEM(WHOLE, BF16)] + [VMEM(*KEPT[at]) for at in FETCHED] + [VMEM(WHOLE, BF16), pltpu.SemaphoreType.DMA((16,)), VMEM((2, 2, *ROW), BF16)]


def renew_kernel(number, *refs):
    shared, (p_in, s_qkv, s_proj, pe_in, mve_in), refs = refs[:15], refs[15:20], refs[20:]
    (block_out, grad_out, whole, p_out, mv_out, pe_out, mve_out, x_pair), refs = refs[:8], refs[8:]
    back_scratch, (grads, sems, swapped), refs = refs[:5], refs[5:8], refs[8:]
    scratch, (mv_msg, mv_box, sends, recvs) = refs[:11], refs[11:]
    place = Place()
    partners = ring_partners(place)
    hail(partners)
    for c in range(4):
        for dp in range(2):
            mv_msg[c, dp] = jnp.concatenate(
                [dealt(s_qkv[k], s_proj[k], c, dp) for k in range(2)], axis=0
            ).astype(BF16)
    links = Links(sends, recvs)
    reduction = Reduction(links, place, grads, scratch)
    pair, moments = [], []

    def late():
        moments.extend(deal(links, place, mv_msg, mv_box))
        pair.append(links.send(shared[0].at[1], x_pair, place.other_dp()))

    extra = back_body(
        0, shared, back_scratch, Copies(sems), links, place, swapped, block_out, grad_out, grads,
        lambda: await_hails(partners), reduction.start, lambda: None, late,
    )
    renew_part(number, place, links, reduction, extra, moments, mv_box, p_in, pe_in, mve_in,
               whole, p_out, mv_out, pe_out, mve_out)
    pair[0].wait_recv()
    links.finish()


def final_kernel(number, *refs):
    shared, dense, refs = refs[:15], refs[15:21], refs[21:]
    deltas, others, refs = refs[:2], refs[2:4], refs[4:]
    (block_out, grad_out, mean_out, flat_out, turned_out, expert_out), refs = refs[:6], refs[6:]
    back_scratch, (grads, sems, swapped), refs = refs[:5], refs[5:8], refs[8:]
    scratch, boxes, refs = refs[:11], refs[11:16], refs[16:]
    expert_scratch, (sends, recvs) = refs[:4], refs[4:]
    place = Place()
    partners = ring_partners(place) + [
        place.in_group(k, step, over) for k in (1, 2, 3) for step in range(4) for over in range(2)
    ]
    hail(partners)
    copies, links = Copies(sems), Links(sends, recvs)
    experts = ExpertMean(links, place, copies, deltas, others, *expert_scratch)

    reduction = Reduction(links, place, grads, scratch)
    extra = back_body(
        1, shared, back_scratch, copies, links, place, swapped, block_out, grad_out, grads,
        lambda: await_hails(partners), reduction.start, experts.start, lambda: None,
    )
    final_part(
        number, place, links, reduction, extra, experts, *dense, mean_out, flat_out, turned_out, *boxes
    )
    for k in range(2):
        expert_out[k] = experts.mean(k).astype(BF16)
    links.finish()


def finish_kernel(*refs):
    given, refs = refs[:16], refs[16:]
    olds, refs = refs[:4], refs[4:]
    (block, grad, new_qkv, new_proj, new_mom_qkv, new_mom_proj, new_gains, new_router, new_mom_gains, new_mom_router,
     *news), (old_buf, new_buf, sems, *held) = refs[:14], refs[14:]
    copies = Copies(sems)
    rows = [copies.start(src, dst) for src, dst in zip(given, held)]
    loads = [copies.start(src, old_buf.at[n]) for n, src in enumerate(olds)]
    for copy in rows:
        copy.wait()
    (block0, block1, grad0, grad1, mean, flat_e, turned_e, experts,
     w_qkv, w_proj, mom_qkv, mom_proj, gains, router, mom_gains, mom_router) = held
    stores = []
    for k in range(2):
        for copy in loads[2 * k : 2 * k + 2]:
            copy.wait()
        new_buf[2 * k], new_buf[2 * k + 1] = outer(old_buf[2 * k], old_buf[2 * k + 1], experts[k].astype(F32))
        stores += [copies.start(new_buf.at[n], news[n]) for n in (2 * k, 2 * k + 1)]
    for n, (one, all_rows) in enumerate(((block0, block), (block1, block), (grad0, grad), (grad1, grad))):
        all_rows[n % 2] = one[...]
    new_gains[...], new_mom_gains[...] = outer(gains[...], mom_gains[...], flat_e[17:19])
    new_router[...], new_mom_router[...] = outer(router[...], mom_router[...], turned_e[:, :17])
    for c in range(3):
        lanes = slice(768 * c, 768 * c + 768)
        new_qkv[:, lanes], new_mom_qkv[:, lanes] = outer(w_qkv[:, lanes], mom_qkv[:, lanes], mean[c])
    new_proj[...], new_mom_proj[...] = outer(w_proj[...], mom_proj[...], mean[3])
    for copy in stores:
        copy.wait()


def finish_call(small, olds):
    part = (192, 1536)
    outs = [((2, *ROW), BF16), ((2, *ROW), F32), ((24, 2304), F32), ((24, 768), F32), ((24, 2304), F32), ((24, 768), F32),
            ((2, 24), F32), ((24, 17), F32), ((2, 24), F32), ((24, 17), F32)]
    return pl.pallas_call(
        finish_kernel,
        out_shape=tuple(jax.ShapeDtypeStruct(*out) for out in outs + [(part, F32)] * 4),
        in_specs=[pl.BlockSpec(memory_space=ANY)] * (len(small) + 4),
        out_specs=tuple([pl.BlockSpec(memory_space=VMEM)] * 10 + [pl.BlockSpec(memory_space=ANY)] * 4),
        scratch_shapes=[VMEM((4, *part), F32), VMEM((4, *part), F32), pltpu.SemaphoreType.DMA((24,))]
        + [VMEM(array.shape, array.dtype) for array in small],
        compiler_params=pltpu.CompilerParams(vmem_limit_bytes=60 << 20),
    )(*small, *olds)


def back_args(small, whole, kept, ret, frozen):
    args = [(VMEM, a) for a in small] + [(ANY, whole)]
    args += [(ANY if at in FETCHED else VMEM, a) for at, a in enumerate(kept)]
    return args + [(VMEM, ret), (VMEM, frozen)]


def renew_call(number, shared, *args):
    return call(
        functools.partial(renew_kernel, number),
        [(VMEM, ROW, BF16), (VMEM, ROW, F32), (VMEM, WHOLE, BF16), (VMEM, BLOCK, F32), (VMEM, (2, *BLOCK), F32),
         (VMEM, (24, 768), F32), (VMEM, (2, 24, 768), F32), (VMEM, ROW, BF16)],
        BACK_SCRATCH + REDUCE_SCRATCH + [VMEM((4, 2, 96, 384), BF16), VMEM((2, 4, 96, 384), BF16)]
        + semaphores(REDUCE_COPIES + GATHER_COPIES + 3 + 7), 2,
        back_args(*shared) + [(VMEM, a) for a in args],
    )


def final_call(number, shared, dense, deltas):
    part = (192, 1536)
    half = (48, 384)
    boxes = [VMEM((2, 4, *half), BF16), VMEM((4, *half), BF16), VMEM((4, *half), BF16), VMEM(half, BF16), VMEM((4, *half), BF16)]
    return call(
        functools.partial(final_kernel, number),
        [(VMEM, ROW, BF16), (VMEM, ROW, F32), (VMEM, (4, 24, 768), F32), (VMEM, (24, 24), F32), (VMEM, (24, 24), F32),
         (VMEM, (2, *part), BF16)],
        BACK_SCRATCH + REDUCE_SCRATCH + boxes
        + [VMEM((2, 2, *part), BF16), VMEM((2, 2, *part), BF16), VMEM((2, *part), BF16), VMEM((2, *part), BF16)]
        + semaphores(REDUCE_COPIES + 3 + 3 + 8 + 4 + 2),
        3,
        back_args(*shared) + [(VMEM, a) for a in dense] + [(ANY, a) for a in deltas],
    )


def body(
    tokens,
    out_grad,
    expert_ids,
    replay,
    frozen_in,
    frozen_out,
    gains,
    w_qkv,
    w_proj,
    router,
    exp_in,
    exp_out,
    mom_gains,
    mom_qkv,
    mom_proj,
    mom_router,
    mom_in,
    mom_out,
    state_gains,
    state_qkv,
    state_proj,
    state_router,
    state_in,
    state_out,
):
    ids = jnp.swapaxes(expert_ids, 1, 2)
    turn = lambda array: jnp.swapaxes(array[0], 0, 1)
    back = lambda array: jnp.swapaxes(array, 0, 1)[None]
    frozen_both = (frozen_in[0], frozen_out[0])
    made = trade_call(
        True, STEP, 4, (tokens, out_grad, ids, replay, w_qkv, w_proj, router, gains, state_router[0], state_gains[0]), exp_in[0], turn(exp_out), *frozen_both,
        state_in[0, :, 0], state_out[0, :, 0],
    )
    w2_start, whole, p_start, pe_start, mve, both_low = made[13:]
    shared = ((tokens, out_grad, ids, replay, pe_start), whole, made[:7], made[7], made[8])
    block0, grad0, whole, p_now, mv, pe_now, mve, x_pair = renew_call(
        STEP, shared, p_start, state_qkv[0], state_proj[0], pe_start, mve
    )
    small = (tokens, out_grad, ids, replay, pe_now)
    made = trade_call(False, STEP + 1, 5, (*small, x_pair), whole, both_low, w2_start, *made[9:11], *frozen_both, *made[11:13])
    shared = (small, whole, made[:7], made[7], made[8])
    dense = (p_now, mv, pe_now, mve, p_start, pe_start)
    block1, grad1, *means = final_call(STEP + 1, shared, dense, made[9:13])
    (block, grad, new_qkv, new_proj, new_mom_qkv, new_mom_proj, new_gains, new_router, new_mom_gains, new_mom_router,
     new_in, new_mom_in, new_out, new_mom_out) = finish_call(
        (block0, block1, grad0, grad1, *means, w_qkv, w_proj, mom_qkv, mom_proj, gains, router, mom_gains, mom_router),
        (exp_in[0], mom_in[0], turn(exp_out), turn(mom_out)),
    )
    return (
        block, grad, new_gains, new_qkv, new_proj, new_router, new_in[None], back(new_out),
        new_mom_gains, new_mom_qkv, new_mom_proj, new_mom_router, new_mom_in[None], back(new_mom_out),
    )


def solution(mesh):
    return jax.shard_map(
        body,
        mesh=mesh,
        in_specs=(
            P(None, ("group", "dp", "expert"), None),
            P(None, ("group", "dp", "expert"), None),
            P(None, ("group", "dp", "expert"), None),
            P(None, ("group", "dp", "expert")),
            P(),
            P(),
            P(None, ("dp", "expert")),
            P(("dp", "expert"), None),
            P(("dp", "expert"), None),
            P(("dp", "expert"), None),
            P("expert", "group", "dp"),
            P("expert", "dp", "group"),
            P(None, ("dp", "expert")),
            P(("dp", "expert"), None),
            P(("dp", "expert"), None),
            P(("dp", "expert"), None),
            P("expert", "group", "dp"),
            P("expert", "dp", "group"),
            P("group", None, None, ("dp", "expert")),
            P("group", None, ("dp", "expert"), None),
            P("group", None, ("dp", "expert"), None),
            P("group", None, ("dp", "expert"), None),
            P("group", None, "expert", None, "dp"),
            P("group", None, "expert", "dp", None),
        ),
        out_specs=(
            P(None, ("group", "dp", "expert"), None),
            P(None, ("group", "dp", "expert"), None),
            P(None, ("dp", "expert")),
            P(("dp", "expert"), None),
            P(("dp", "expert"), None),
            P(("dp", "expert"), None),
            P("expert", "group", "dp"),
            P("expert", "dp", "group"),
            P(None, ("dp", "expert")),
            P(("dp", "expert"), None),
            P(("dp", "expert"), None),
            P(("dp", "expert"), None),
            P("expert", "group", "dp"),
            P("expert", "dp", "group"),
        ),
        check_vma=False,
    )
```
